32 devices in a mesh: wide: 8 (over z, y), narrow: 4 (over x, core).
Axes of the slice: x: 2, y: 2, z: 4, core: 2. Of those that a mesh axis runs over, the one named last changes fastest.
Arguments:
- target_states: bfloat16 [8, 2048, 512], P('wide', 'narrow'), may hold values from -6 to 6
- memory: bfloat16 [8, 2048, 512], P('wide', 'narrow'), may hold values from -6 to 6
- target_lengths: int32 [8, 16], P('wide'), may hold values from 1 to 1792, as said below
- source_lengths: int32 [8, 16], P('wide'), may hold values from 1 to 1792, as said below
- self_project: bfloat16 [512, 1536], P(('wide', 'narrow')), may hold values from -0.375 to 0.375
- self_output: bfloat16 [512, 512], P(('wide', 'narrow')), may hold values from -1 to 1
- cross_project: bfloat16 [512, 512], P(('wide', 'narrow')), may hold values from -0.375 to 0.375
- memory_project: bfloat16 [512, 1024], P(('wide', 'narrow')), may hold values from -0.375 to 0.375
- cross_output: bfloat16 [512, 512], P(('wide', 'narrow')), may hold values from -1 to 1
- expand_weight: bfloat16 [512, 2048], P(('wide', 'narrow')), may hold values from -0.25 to 0.25
- contract_weight: bfloat16 [2048, 512], P(('wide', 'narrow')), may hold values from -0.125 to 0.125
- norm_gain: bfloat16 [3, 512], P(None, ('wide', 'narrow')), may hold values from 0.5 to 1.5
- norm_bias: bfloat16 [3, 512], P(None, ('wide', 'narrow')), may hold values from -3 to 3
- out_grad: float32 [8, 2048, 512], P('wide', 'narrow'), may hold values from -6 to 6
Outputs:
- output: float32 [8, 2048, 512], P('wide', 'narrow')
- states_grad: float32 [8, 2048, 512], P('wide', 'narrow')
- memory_grad: float32 [8, 2048, 512], P('wide', 'narrow')
- self_project_grad: float32 [512, 1536], P(('wide', 'narrow'))
- self_output_grad: float32 [512, 512], P(('wide', 'narrow'))
- cross_project_grad: float32 [512, 512], P(('wide', 'narrow'))
- memory_project_grad: float32 [512, 1024], P(('wide', 'narrow'))
- cross_output_grad: float32 [512, 512], P(('wide', 'narrow'))
- expand_grad: float32 [512, 2048], P(('wide', 'narrow'))
- contract_grad: float32 [2048, 512], P(('wide', 'narrow'))
- norm_gain_grad: float32 [3, 512], P(None, ('wide', 'narrow'))
- norm_bias_grad: float32 [3, 512], P(None, ('wide', 'narrow'))
The draws below stay inside these ranges and needn't reach their ends.
Inputs may be any that keep to these rules, and one draw needn't show every extreme that they name: `target_lengths`: each row's 16 sentence lengths are at least 1 and sum to less than 2048; the rest of the row is padding. `source_lengths`: each row's 16 sentence lengths are at least 1 and sum to less than 2048; the rest of the row is padding.
All inputs are finite; a program needn't handle non-finite values.
Results may differ from the reference program's by a relative error of at most 0.025.
The reference program's roundings to bfloat16 on the way count: a program that leaves them out, or rounds other values in their place, can miss the bound.
Values may be sent and summed in bfloat16 or wider, within the bound.
No kernel may reach another device: no remote copies, remote signals or barrier semaphores. Data moves between devices by JAX's collectives and lax.ppermute only.
A program may use at most 128 MiB of HBM per device.

```python
from functools import partial
import jax
import jax.numpy as jnp
from jax import lax

D = 512
HEADS = 8
HEAD_DIM = 64
FF = 2048
ROW_LEN = 2048
SRC_LEN = 2048
SEGS = 16
BATCH_ROWS = 8


def chosen_slot(key):
    return jax.random.randint(key, (BATCH_ROWS, 1), 0, SEGS)


def packed_lengths(key, chosen, row_span):
    first_key, second_key, third_key = jax.random.split(key, 3)
    shorts = jax.random.randint(first_key, (BATCH_ROWS, SEGS), 1, row_span // (8 * SEGS) + 1)
    extra = jax.random.randint(second_key, (BATCH_ROWS, 1), 0, row_span // 32 + 1)
    full_row = jax.random.randint(third_key, (1, 1), 0, BATCH_ROWS)
    row_number = lax.broadcasted_iota(jnp.int32, (BATCH_ROWS, 1), 0)
    extra = jnp.where(row_number == full_row, 0, extra)
    is_long = lax.broadcasted_iota(jnp.int32, (BATCH_ROWS, SEGS), 1) == chosen
    longest = row_span - row_span // 8 - extra
    return jnp.where(is_long, longest, shorts).astype(jnp.int32)


def draw_target_lengths(key, part):
    chosen = chosen_slot(key)
    key = jax.random.fold_in(key, 11)
    return packed_lengths(key, chosen, ROW_LEN)


def draw_source_lengths(key, part):
    chosen = chosen_slot(key)
    key = jax.random.fold_in(key, 23)
    return packed_lengths(key, chosen, SRC_LEN)


def strengthened(entries, stream_key, source, target, blocks, factor):
    def block_of(axis_at):
        return (jnp.arange(entries.shape[axis_at]) // (entries.shape[axis_at] // blocks)).reshape((-1,) + (1,) * (entries.ndim - 1 - axis_at))

    first = jax.random.permutation(stream_key, blocks)[block_of(target)]
    second = (block_of(target) + blocks // 2) % blocks
    return jnp.where((block_of(source) == first) | (block_of(source) == second), factor * entries, entries)


def block_levels(rng, shape, pieces, least, largest):
    def one(dim, parts):
        heights = jax.random.uniform(jax.random.fold_in(jax.random.fold_in(rng, 6), dim), (parts,), jnp.float32, least / len(pieces), largest / len(pieces))
        return jnp.repeat(jnp.exp(heights), shape[dim] // parts).reshape((-1,) + (1,) * (len(shape) - dim - 1))

    gain = one(*pieces[0])
    for cut in pieces[1:]:
        gain = gain * one(*cut)
    return gain


def scatter_about(own_key, extent, scale, limit, cuts=(), kind=jnp.bfloat16):
    entries = scale * jax.random.normal(own_key, extent, jnp.float32)
    if cuts:
        entries = entries * block_levels(own_key, extent, cuts, -0.22, 0.18)
    return jnp.clip(entries, -limit, limit).astype(kind)


def bell_draw_with(stream_key, shape, scale, reach, cuts, heavy, held_as=jnp.bfloat16):
    drawn = scale * jax.random.normal(stream_key, shape, jnp.float32)
    if cuts:
        drawn = drawn * block_levels(stream_key, shape, cuts, -0.22, 0.18)
    return jnp.clip(strengthened(drawn, jax.random.fold_in(stream_key, 3), *heavy), -reach, reach).astype(held_as)


def setup_inputs(seed: int = 0) -> dict:
    streams_of = jax.random.split(jax.random.key(seed), 15)
    target_states = scatter_about(streams_of[0], (BATCH_ROWS, ROW_LEN, D), 1.0, 6.0, ((0, 8), (1, 4)))
    memory = scatter_about(streams_of[1], (BATCH_ROWS, SRC_LEN, D), 1.0, 6.0, ((0, 8), (1, 4)))
    target_lengths = draw_target_lengths(jax.random.fold_in(streams_of[14], 71), 0)
    source_lengths = draw_source_lengths(jax.random.fold_in(streams_of[14], 71), 0)
    self_project = scatter_about(streams_of[4], (D, 3 * D), (D // 2) ** -0.5, 0.375, ((0, 32),))
    self_output = scatter_about(streams_of[5], (D, D), (D // 16) ** -0.5, 1.0, ((0, 32),))
    cross_project = scatter_about(streams_of[6], (D, D), (D // 2) ** -0.5, 0.375, ((0, 32),))
    memory_project = scatter_about(streams_of[7], (D, 2 * D), (D // 2) ** -0.5, 0.375, ((0, 32),))
    cross_output = scatter_about(streams_of[8], (D, D), (D // 16) ** -0.5, 1.0, ((0, 32),))
    expand_weight = scatter_about(streams_of[9], (D, FF), D ** -0.5, 0.25, ((0, 32),))
    contract_weight = scatter_about(streams_of[10], (FF, D), FF ** -0.5, 0.125, ((0, 32),))
    norm_gain = jnp.clip(1.0 + 0.1 * jax.random.normal(streams_of[11], (3, D), jnp.float32), 0.5, 1.5).astype(jnp.bfloat16)
    norm_bias = scatter_about(streams_of[12], (3, D), 0.5, 3.0, ((1, 32),))
    out_grad = bell_draw_with(streams_of[13], (BATCH_ROWS, ROW_LEN, D), 1.0, 6.0, ((0, 8), (1, 4)), (0, 2, 8, 2.0), jnp.float32)
    return dict(target_states=target_states, memory=memory, target_lengths=target_lengths, source_lengths=source_lengths, self_project=self_project, self_output=self_output, cross_project=cross_project, memory_project=memory_project, cross_output=cross_output, expand_weight=expand_weight, contract_weight=contract_weight, norm_gain=norm_gain, norm_bias=norm_bias, out_grad=out_grad)


@jax.custom_vjp
def low(v):
    return lax.optimization_barrier(v.astype(jnp.bfloat16)).astype(jnp.float32)

@jax.custom_vjp
def low_back(v):
    return v

def low_keep(v):
    return (low(v), None)

def low_pass(kept, grad):
    return (grad,)

def back_keep(v):
    return (v, None)

def back_low(kept, grad):
    return (low(grad),)
low.defvjp(low_keep, low_pass)
low_back.defvjp(back_keep, back_low)
ln_eps = 1e-05
masked_score = -1000000000.0
highest = lax.Precision.HIGHEST

def segment_numbers(lengths, row_span):
    segment_ends = jnp.cumsum(lengths, axis=-1).astype(jnp.int32)
    position = jnp.arange(row_span, dtype=jnp.int32)
    return lax.optimization_barrier(jnp.sum((position[:, None] >= segment_ends[None, :]).astype(jnp.int32), axis=1)).astype(jnp.int32)

def layer_norm(states, gain_row, offset):
    centred = states - lax.optimization_barrier(jnp.mean(states, axis=-1, keepdims=True))
    spread = lax.optimization_barrier(jnp.mean(centred * centred, axis=-1, keepdims=True))
    return centred * lax.rsqrt(spread + ln_eps) * gain_row + offset

def project(states, weight):
    return jnp.dot(states, weight, precision=highest)

def attend(queries, key_values, allowed):
    query_count = queries.shape[0]
    model_width = key_values.shape[1] // 2
    head_query = queries.reshape(query_count, HEADS, HEAD_DIM).transpose(1, 0, 2)
    head_key = key_values[:, :model_width].reshape(-1, HEADS, HEAD_DIM).transpose(1, 0, 2)
    head_value = key_values[:, model_width:].reshape(-1, HEADS, HEAD_DIM).transpose(1, 0, 2)
    raw_scores = low_back(jnp.einsum('hqd,hkd->hqk', head_query, head_key, precision=highest))
    scaled = jnp.where(allowed[None], raw_scores * HEAD_DIM ** (-0.5), masked_score)
    prob_low = low(jax.nn.softmax(scaled, axis=-1))
    mixture = jnp.einsum('hqk,hkd->hqd', prob_low, head_value, precision=highest)
    return mixture.transpose(1, 0, 2).reshape(query_count, HEADS * HEAD_DIM)

def decoder_layer(target_ids, source_ids, states, memory, self_project, self_output, cross_project, memory_project, cross_output, expand_weight, contract_weight, norm_gain, norm_bias):

    def one_row(row_items):
        row_states, row_memory, row_target, row_source = row_items
        model_width = row_states.shape[1]
        packed = low(low_back(project(row_states, self_project)))
        self_allowed = row_target[:, None] == row_target[None, :]
        self_mix = low(low_back(attend(packed[:, :model_width], packed[:, model_width:], self_allowed)))
        first_norm = layer_norm(row_states + low_back(project(self_mix, self_output)), norm_gain[0], norm_bias[0])
        cross_query = low(low_back(project(low(first_norm), cross_project)))
        memory_pairs = low(low_back(project(row_memory, memory_project)))
        cross_allowed = row_target[:, None] == row_source[None, :]
        cross_mix = low(low_back(attend(cross_query, memory_pairs, cross_allowed)))
        second_norm = layer_norm(first_norm + low_back(project(cross_mix, cross_output)), norm_gain[1], norm_bias[1])
        hidden = low_back(project(low(second_norm), expand_weight))
        active = low(jax.nn.gelu(hidden))
        return layer_norm(second_norm + low_back(project(active, contract_weight)), norm_gain[2], norm_bias[2])
    return lax.map(jax.checkpoint(one_row), (states, memory, target_ids, source_ids))

def reference(target_states, memory, target_lengths, source_lengths, self_project, self_output, cross_project, memory_project, cross_output, expand_weight, contract_weight, norm_gain, norm_bias, out_grad):
    target_ids = jax.vmap(lambda lengths: segment_numbers(lengths, ROW_LEN))(target_lengths)
    source_ids = jax.vmap(lambda lengths: segment_numbers(lengths, SRC_LEN))(source_lengths)
    float_args = [item.astype(jnp.float32) for item in (target_states, memory, self_project, self_output, cross_project, memory_project, cross_output, expand_weight, contract_weight, norm_gain, norm_bias)]
    output, pullback = jax.vjp(partial(decoder_layer, target_ids, source_ids), *float_args)
    gradients = pullback(out_grad.astype(jnp.float32))
    return (output, gradients[0], gradients[1], gradients[2], gradients[3], gradients[4], gradients[5], gradients[6], gradients[7], gradients[8], gradients[9], gradients[10])
```

```python
import jax
import jax.numpy as jnp
from jax import lax
from jax.sharding import PartitionSpec as P

HEAD_DIM = 64


ln_eps = 1e-05
masked_score = -1000000000.0


def segment_numbers(lengths, row_span):
    segment_ends = jnp.cumsum(lengths, axis=1)
    position = lax.broadcasted_iota(jnp.int32, (1, row_span, 1), 1)
    return jnp.sum((position >= segment_ends[:, None, :]).astype(jnp.int32), axis=2)


def layer_norm(states, gain_row, offset):
    centred = states - jnp.mean(states, axis=-1, keepdims=True)
    spread = jnp.mean(centred * centred, axis=-1, keepdims=True)
    return centred * lax.rsqrt(spread + ln_eps) * gain_row + offset


def split_heads(tensor):
    row_count, token_count, feature_width = tensor.shape
    return tensor.reshape(row_count, token_count, feature_width // HEAD_DIM, HEAD_DIM).transpose(
        2, 0, 1, 3
    )


def merge_heads(tensor):
    head_count, row_count, token_count, head_width = tensor.shape
    return tensor.transpose(1, 2, 0, 3).reshape(row_count, token_count, head_count * head_width)


def attend_forward(queries, key_block, value_block, allowed):
    score_scale = HEAD_DIM ** (-0.5)

    def one_head(head_items):
        query_head, key_head, value_head = head_items
        raw_scores = jnp.einsum(
            "rqd,rkd->rqk", query_head, key_head, preferred_element_type=jnp.float32
        )
        scaled = jnp.where(allowed, raw_scores * score_scale, masked_score)
        peak_score = jnp.max(scaled, axis=2, keepdims=True)
        weights = jnp.exp(scaled - peak_score)
        totals = jnp.sum(weights, axis=2, keepdims=True)
        prob_low = (weights / totals).astype(jnp.bfloat16)
        mixture = jnp.einsum(
            "rqk,rkd->rqd", prob_low, value_head, preferred_element_type=jnp.float32
        )
        return (mixture, (peak_score + jnp.log(totals))[:, :, 0])

    return lax.map(one_head, (queries, key_block, value_block))


def attend_backward(queries, key_block, value_block, allowed, log_totals, mix_grad):
    score_scale = HEAD_DIM ** (-0.5)

    def one_head(head_items):
        query_head, key_head, value_head, log_head, grad_head = head_items
        raw_scores = jnp.einsum(
            "rqd,rkd->rqk", query_head, key_head, preferred_element_type=jnp.float32
        )
        scaled = jnp.where(allowed, raw_scores * score_scale, masked_score)
        probs_full = jnp.exp(scaled - log_head[:, :, None])
        prob_grad = jnp.einsum(
            "rqd,rkd->rqk", grad_head, value_head, preferred_element_type=jnp.float32
        )
        inner_sum = jnp.sum(probs_full * prob_grad, axis=2, keepdims=True)
        score_grad = (probs_full * (prob_grad - inner_sum) * score_scale).astype(jnp.bfloat16)
        query_grad = jnp.einsum(
            "rqk,rkd->rqd", score_grad, key_head, preferred_element_type=jnp.float32
        )
        key_grad = jnp.einsum(
            "rqk,rqd->rkd", score_grad, query_head, preferred_element_type=jnp.float32
        )
        value_grad = jnp.einsum(
            "rqk,rqd->rkd",
            probs_full.astype(jnp.bfloat16),
            grad_head,
            preferred_element_type=jnp.float32,
        )
        return (query_grad, key_grad, value_grad)

    return lax.map(one_head, (queries, key_block, value_block, log_totals, mix_grad))


def axis_bits():
    wide_bits = lax.axis_size("wide").bit_length() - 1
    narrow_bits = lax.axis_size("narrow").bit_length() - 1
    return wide_bits, narrow_bits


def exchange(block, mask):
    device_count = lax.axis_size("wide") * lax.axis_size("narrow")
    pairs = [(device, device ^ mask) for device in range(device_count)]
    return lax.ppermute(block, ("wide", "narrow"), pairs)


def stages():
    wide_bits, narrow_bits = axis_bits()
    total = wide_bits + narrow_bits
    near = list(range(0, narrow_bits - 1))
    plane = [narrow_bits - 1, narrow_bits]
    far = list(range(narrow_bits + 1, total))
    groups = [tuple(far[at : at + 2]) for at in range(0, len(far), 2)][::-1]
    return groups + [tuple(plane)] + [(bit,) for bit in near]


def masks_of(bits):
    out = []
    for number in range(2 ** len(bits)):
        out.append(sum(1 << bit for at, bit in enumerate(bits) if number >> at & 1))
    return out


def device_number():
    return lax.axis_index("wide") * lax.axis_size("narrow") + lax.axis_index("narrow")


def local_number(me, bits):
    return sum(((me >> bit) & 1) << at for at, bit in enumerate(bits))


def gather_shards(shard):
    me = device_number()
    wide_bits, narrow_bits = axis_bits()
    total = wide_bits + narrow_bits
    held = shard[None]
    done = []
    for bits in stages():
        mine = local_number(me, bits)
        whole = jnp.zeros((2 ** len(bits),) + held.shape, held.dtype)
        for number, mask in enumerate(masks_of(bits)):
            block = held if number == 0 else exchange(held, mask)
            whole = lax.dynamic_update_slice_in_dim(whole, block[None], mine ^ number, 0)
        held = whole
        done = list(bits) + done
    groups = stages()
    shape = []
    order = []
    for bits in groups[::-1]:
        for bit in bits[::-1]:
            shape.append(2)
            order.append(bit)
    held = held.reshape(tuple(shape) + shard.shape)
    places = [order.index(bit) for bit in range(total - 1, -1, -1)]
    held = held.transpose(tuple(places) + (total, total + 1))
    return held.reshape((2**total,) + shard.shape)


def scatter_sums(terms):
    me = device_number()
    wide_bits, narrow_bits = axis_bits()
    total = wide_bits + narrow_bits
    groups = stages()
    order = []
    for bits in groups[::-1]:
        order += list(bits[::-1])
    tail = terms.shape[1:]
    held = terms.astype(jnp.bfloat16).reshape((2,) * total + tail)
    places = [total - 1 - bit for bit in order]
    held = held.transpose(tuple(places) + (total, total + 1))
    for bits in groups[::-1]:
        held = held.reshape((2 ** len(bits), -1) + tail)
        mine = local_number(me, bits)
        total_sum = lax.dynamic_index_in_dim(held, mine, 0, keepdims=False).astype(jnp.float32)
        for number, mask in enumerate(masks_of(bits)):
            if number:
                block = lax.dynamic_index_in_dim(held, mine ^ number, 0, keepdims=False)
                total_sum = total_sum + exchange(block, mask).astype(jnp.float32)
        held = total_sum.astype(jnp.bfloat16)
    return total_sum[0]


def fetch_weights(
    self_project,
    self_output,
    cross_project,
    memory_project,
    cross_output,
    expand_weight,
    contract_weight,
    norm_gain,
    norm_bias,
):
    rows, width = cross_output.shape
    folds = contract_weight.shape[0] // rows
    folded = contract_weight.reshape(folds, rows, width).transpose(1, 0, 2).reshape(rows, -1)
    norms = jnp.concatenate([norm_gain, norm_bias], axis=0).T
    packed = jnp.concatenate(
        [
            self_project,
            self_output,
            cross_project,
            memory_project,
            cross_output,
            expand_weight,
            folded,
            jnp.pad(norms, ((0, 0), (0, 128 - norms.shape[1]))),
        ],
        axis=1,
    )
    whole = gather_shards(packed)
    out = []
    start = 0
    for part in (self_project, self_output, cross_project, memory_project, cross_output, expand_weight):
        out.append(whole[:, :, start : start + part.shape[1]].reshape(-1, part.shape[1]))
        start += part.shape[1]
    span = folded.shape[1]
    contract = whole[:, :, start : start + span].reshape(-1, rows, folds, width)
    out.append(contract.transpose(0, 2, 1, 3).reshape(-1, width))
    start += span
    count = norm_gain.shape[0]
    out.append(whole[:, :, start : start + count].reshape(-1, count).T)
    out.append(whole[:, :, start + count : start + 2 * count].reshape(-1, count).T)
    return tuple(out)


def settle_grads(
    project_grad,
    output_grad,
    cross_grad,
    memory_proj_grad,
    cross_out_grad,
    expand_grad,
    contract_grad,
    gain_grad,
    offset_grad,
):
    device_count = lax.axis_size("wide") * lax.axis_size("narrow")
    straight = (project_grad, output_grad, cross_grad, memory_proj_grad, cross_out_grad, expand_grad)
    width = output_grad.shape[1]
    rows = output_grad.shape[0] // device_count
    folds = contract_grad.shape[0] // output_grad.shape[0]
    folded = contract_grad.reshape(device_count, folds, rows, width).transpose(0, 2, 1, 3)
    folded = folded.reshape(device_count, rows, folds * width)
    norms = jnp.concatenate([gain_grad, offset_grad], axis=0).T
    norms = jnp.pad(norms, ((0, 0), (0, 128 - norms.shape[1])))
    terms = jnp.concatenate(
        [part.reshape(device_count, rows, -1) for part in straight]
        + [folded, norms.reshape(device_count, rows, 128)],
        axis=2,
    )
    own = scatter_sums(terms)
    out = []
    start = 0
    for part in straight:
        out.append(own[:, start : start + part.shape[1]])
        start += part.shape[1]
    span = folds * width
    contract = own[:, start : start + span].reshape(rows, folds, width).transpose(1, 0, 2)
    out.append(contract.reshape(folds * rows, width))
    start += span
    count = gain_grad.shape[0]
    out.append(own[:, start : start + count].T)
    out.append(own[:, start + count : start + 2 * count].T)
    return tuple(out)


def per_device(
    target_states,
    memory,
    target_lengths,
    source_lengths,
    self_project,
    self_output,
    cross_project,
    memory_project,
    cross_output,
    expand_weight,
    contract_weight,
    norm_gain,
    norm_bias,
    out_grad,
):
    row_count, local_len, model_width = target_states.shape
    source_local = memory.shape[1]
    narrow_size = lax.axis_size("narrow")
    narrow_index = lax.axis_index("narrow")
    target_ids = segment_numbers(target_lengths, local_len * narrow_size)
    source_ids = segment_numbers(source_lengths, source_local * narrow_size)
    own_ids = lax.dynamic_slice_in_dim(target_ids, narrow_index * local_len, local_len, 1)
    self_allowed = own_ids[:, :, None] == target_ids[:, None, :]
    cross_allowed = own_ids[:, :, None] == source_ids[:, None, :]
    (
        self_whole,
        sout_whole,
        cproj_whole,
        mproj_whole,
        cout_whole,
        expand_whole,
        contract_whole,
        gain_whole,
        offset_whole,
    ) = fetch_weights(
        self_project,
        self_output,
        cross_project,
        memory_project,
        cross_output,
        expand_weight,
        contract_weight,
        norm_gain,
        norm_bias,
    )
    gain_rows = gain_whole.astype(jnp.float32)
    offset_rows = offset_whole.astype(jnp.float32)
    query_low = jnp.dot(
        target_states, self_whole[:, :model_width], preferred_element_type=jnp.float32
    ).astype(jnp.bfloat16)
    pair_low = jnp.dot(
        target_states, self_whole[:, model_width:], preferred_element_type=jnp.float32
    ).astype(jnp.bfloat16)
    pair_rows = lax.all_gather(pair_low, "narrow", axis=1, tiled=True)
    key_part = pair_rows[:, :, :model_width]
    value_part = pair_rows[:, :, model_width:]
    self_query = split_heads(query_low)
    self_key = split_heads(key_part)
    self_value = split_heads(value_part)
    self_mixture, self_logs = attend_forward(self_query, self_key, self_value, self_allowed)
    self_mix = merge_heads(self_mixture).astype(jnp.bfloat16)
    states_float = target_states.astype(jnp.float32)
    first_norm, first_pull = jax.vjp(
        layer_norm,
        states_float + jnp.dot(self_mix, sout_whole, preferred_element_type=jnp.float32),
        gain_rows[0],
        offset_rows[0],
    )
    first_low = first_norm.astype(jnp.bfloat16)
    cross_low = jnp.dot(first_low, cproj_whole, preferred_element_type=jnp.float32).astype(
        jnp.bfloat16
    )
    memory_pairs = jnp.dot(memory, mproj_whole, preferred_element_type=jnp.float32).astype(
        jnp.bfloat16
    )
    memory_rows = lax.all_gather(memory_pairs, "narrow", axis=1, tiled=True)
    mkey_part = memory_rows[:, :, :model_width]
    mvalue_part = memory_rows[:, :, model_width:]
    cross_query = split_heads(cross_low)
    cross_key = split_heads(mkey_part)
    cross_value = split_heads(mvalue_part)
    cross_mixture, cross_logs = attend_forward(cross_query, cross_key, cross_value, cross_allowed)
    cross_mix = merge_heads(cross_mixture).astype(jnp.bfloat16)
    second_norm, second_pull = jax.vjp(
        layer_norm,
        first_norm + jnp.dot(cross_mix, cout_whole, preferred_element_type=jnp.float32),
        gain_rows[1],
        offset_rows[1],
    )
    second_low = second_norm.astype(jnp.bfloat16)
    forward_hidden = jnp.dot(second_low, expand_whole, preferred_element_type=jnp.float32)
    forward_active = jax.nn.gelu(forward_hidden).astype(jnp.bfloat16)
    output, third_pull = jax.vjp(
        layer_norm,
        second_norm + jnp.dot(forward_active, contract_whole, preferred_element_type=jnp.float32),
        gain_rows[2],
        offset_rows[2],
    )
    third_grad, gain_three, offset_three = third_pull(out_grad)
    ffn_grad = third_grad.astype(jnp.bfloat16)
    hidden = jnp.dot(second_low, expand_whole, preferred_element_type=jnp.float32)
    active = jax.nn.gelu(hidden).astype(jnp.bfloat16)
    contract_grad = jnp.einsum("rnf,rnd->fd", active, ffn_grad, preferred_element_type=jnp.float32)
    active_grad = jnp.dot(ffn_grad, contract_whole.T, preferred_element_type=jnp.float32)
    hidden_grad = jax.vjp(jax.nn.gelu, hidden)[1](active_grad)[0].astype(jnp.bfloat16)
    expand_grad = jnp.einsum(
        "rnd,rnf->df", second_low, hidden_grad, preferred_element_type=jnp.float32
    )
    second_grad, gain_two, offset_two = second_pull(
        third_grad + jnp.dot(hidden_grad, expand_whole.T, preferred_element_type=jnp.float32)
    )
    cross_out_low = second_grad.astype(jnp.bfloat16)
    cross_out_grad = jnp.einsum(
        "rnc,rnd->cd", cross_mix, cross_out_low, preferred_element_type=jnp.float32
    )
    cross_mix_grad = jnp.dot(
        cross_out_low, cout_whole.T, preferred_element_type=jnp.float32
    ).astype(jnp.bfloat16)
    cross_query_grad, cross_key_grad, cross_value_grad = attend_backward(
        cross_query, cross_key, cross_value, cross_allowed, cross_logs, split_heads(cross_mix_grad)
    )
    memory_terms = jnp.concatenate(
        [merge_heads(cross_key_grad), merge_heads(cross_value_grad)], axis=2
    )
    memory_pair_grad = lax.psum_scatter(
        memory_terms.astype(jnp.bfloat16), "narrow", scatter_dimension=1, tiled=True
    )
    cross_query_low = merge_heads(cross_query_grad).astype(jnp.bfloat16)
    memory_proj_grad = jnp.einsum(
        "rsd,rse->de", memory, memory_pair_grad, preferred_element_type=jnp.float32
    )
    memory_grad = jnp.dot(memory_pair_grad, mproj_whole.T, preferred_element_type=jnp.float32)
    cross_proj_grad = jnp.einsum(
        "rnd,rne->de", first_low, cross_query_low, preferred_element_type=jnp.float32
    )
    first_grad, gain_one, offset_one = first_pull(
        second_grad + jnp.dot(cross_query_low, cproj_whole.T, preferred_element_type=jnp.float32)
    )
    self_out_low = first_grad.astype(jnp.bfloat16)
    self_out_grad = jnp.einsum(
        "rnc,rnd->cd", self_mix, self_out_low, preferred_element_type=jnp.float32
    )
    self_mix_grad = jnp.dot(self_out_low, sout_whole.T, preferred_element_type=jnp.float32).astype(
        jnp.bfloat16
    )
    self_query_grad, self_key_grad, self_value_grad = attend_backward(
        self_query, self_key, self_value, self_allowed, self_logs, split_heads(self_mix_grad)
    )
    pair_terms = jnp.concatenate([merge_heads(self_key_grad), merge_heads(self_value_grad)], axis=2)
    pair_grad = lax.psum_scatter(
        pair_terms.astype(jnp.bfloat16), "narrow", scatter_dimension=1, tiled=True
    )
    packed_grad = jnp.concatenate(
        [merge_heads(self_query_grad).astype(jnp.bfloat16), pair_grad], axis=2
    )
    self_proj_grad = jnp.einsum(
        "rnd,rne->de", target_states, packed_grad, preferred_element_type=jnp.float32
    )
    states_grad = first_grad + jnp.dot(
        packed_grad, self_whole.T, preferred_element_type=jnp.float32
    )
    gain_grad = jnp.stack([gain_one, gain_two, gain_three])
    offset_grad = jnp.stack([offset_one, offset_two, offset_three])
    settled = settle_grads(
        self_proj_grad,
        self_out_grad,
        cross_proj_grad,
        memory_proj_grad,
        cross_out_grad,
        expand_grad,
        contract_grad,
        gain_grad,
        offset_grad,
    )
    return (
        output,
        states_grad,
        memory_grad,
        settled[0],
        settled[1],
        settled[2],
        settled[3],
        settled[4],
        settled[5],
        settled[6],
        settled[7],
        settled[8],
    )


def solution(mesh):
    in_specs = (
        P("wide", "narrow", None),
        P("wide", "narrow", None),
        P("wide", None),
        P("wide", None),
        P(("wide", "narrow"), None),
        P(("wide", "narrow"), None),
        P(("wide", "narrow"), None),
        P(("wide", "narrow"), None),
        P(("wide", "narrow"), None),
        P(("wide", "narrow"), None),
        P(("wide", "narrow"), None),
        P(None, ("wide", "narrow")),
        P(None, ("wide", "narrow")),
        P("wide", "narrow", None),
    )
    out_specs = (
        P("wide", "narrow", None),
        P("wide", "narrow", None),
        P("wide", "narrow", None),
        P(("wide", "narrow"), None),
        P(("wide", "narrow"), None),
        P(("wide", "narrow"), None),
        P(("wide", "narrow"), None),
        P(("wide", "narrow"), None),
        P(("wide", "narrow"), None),
        P(("wide", "narrow"), None),
        P(None, ("wide", "narrow")),
        P(None, ("wide", "narrow")),
    )
    return jax.shard_map(
        per_device, mesh=mesh, in_specs=in_specs, out_specs=out_specs, check_vma=False
    )
```

```python
import functools

import jax
import jax.numpy as jnp
from jax import lax
from jax.experimental import pallas as pl
from jax.experimental.pallas import tpu as pltpu
from jax.sharding import PartitionSpec as P

HEAD_DIM = 64
LANES = 128
TILE_ROWS = 16
BLOCKS = 32
AXES = ("wide", "narrow")
LOW = jnp.bfloat16
FULL = jnp.float32

ln_eps = 1e-05
score_scale = HEAD_DIM ** (-0.5)
mask_step = -(2.0**30)

BY_LANES = (((1,), (1,)), ((), ()))
PLAIN = (((1,), (0,)), ((), ()))
VMEM_BYTES = 58 * 2**20


def dot(left, right, dims=PLAIN):
    return lax.dot_general(left, right, dims, preferred_element_type=FULL)


def exchange(block, mask):
    device_count = lax.axis_size("wide") * lax.axis_size("narrow")
    pairs = [(device, device ^ mask) for device in range(device_count)]
    return lax.ppermute(block, AXES, pairs)


def device_number():
    return lax.axis_index("wide") * lax.axis_size("narrow") + lax.axis_index("narrow")


def staged():
    return lax.axis_size("wide") * lax.axis_size("narrow") == BLOCKS


FAR = (8, 16, 24)
PLANE = (2, 4, 6)


def gather_far(shard):
    if not staged():
        return shard
    return jnp.stack([shard] + [exchange(shard, mask) for mask in FAR])


def gather_plane(held):
    if not staged():
        return held
    return [held] + [exchange(held, mask) for mask in PLANE]


def gather_core(held, folds=0):
    if staged():
        return held + [exchange(quarter, 1) for quarter in held]
    whole = lax.all_gather(held, AXES, axis=0, tiled=True)
    if folds:
        rows, columns = held.shape
        split = columns - folds * whole.shape[0]
        tall = unfold_rows(held[:, split:], whole.shape[0])
        tall = lax.all_gather(tall, AXES, axis=0, tiled=True)
        tall = tall.reshape(BLOCKS, folds, TILE_ROWS, -1).transpose(0, 2, 1, 3)
        whole = jnp.concatenate([whole[:, :split], tall.reshape(whole.shape[0], -1)], axis=1)
    whole = whole.reshape(4, 4, 2, TILE_ROWS, held.shape[1]).transpose(2, 1, 0, 3, 4)
    return [whole[core, plane] for core in range(2) for plane in range(4)]


def home_number():
    return device_number() if staged() else jnp.zeros((), jnp.int32)


def block_number(home, core, plane, far):
    return home ^ (far * 8 + plane * 2 + core)


def reduce_core(kept, sent):
    if not staged():
        return kept, sent
    other = exchange(sent, 1)
    total = kept.astype(FULL) + other.astype(FULL)
    return total.astype(LOW)


def reduce_plane(held):
    if not staged():
        return held
    total = held[0].astype(FULL)
    for plane, mask in enumerate(PLANE):
        total = total + exchange(held[plane + 1], mask).astype(FULL)
    return total.astype(LOW)


def reduce_far(held, folds=0):
    if staged():
        total = held[0].astype(FULL)
        for far, mask in enumerate(FAR):
            total = total + exchange(held[far + 1], mask).astype(FULL)
        return total
    whole = jnp.stack(held).transpose(2, 1, 0, 3, 4)
    whole = whole.reshape(BLOCKS * TILE_ROWS, -1).astype(FULL)
    if folds:
        split = whole.shape[1] - folds * whole.shape[0]
        tall = whole[:, split:].reshape(BLOCKS, TILE_ROWS, folds, -1).transpose(0, 2, 1, 3)
        tall = tall.reshape(folds * whole.shape[0], -1)
        tall = lax.psum_scatter(tall, AXES, scatter_dimension=0, tiled=True)
        whole = lax.psum_scatter(whole[:, :split], AXES, scatter_dimension=0, tiled=True)
        return jnp.concatenate([whole, fold_rows(tall, whole.shape[0])], axis=1)
    return lax.psum_scatter(whole, AXES, scatter_dimension=0, tiled=True)


def fold_rows(block, rows):
    return jnp.concatenate(
        [block[at : at + rows] for at in range(0, block.shape[0], rows)], axis=1
    )


def unfold_rows(block, width):
    return jnp.concatenate(
        [block[:, at : at + width] for at in range(0, block.shape[1], width)], axis=0
    )


def lane_numbers(shape):
    return lax.broadcasted_iota(jnp.int32, shape, 1)


def segment_bounds(lengths_ref):
    lane = lane_numbers((1, LANES)) & (HEAD_DIM - 1)
    first = jnp.full((1, LANES), 2**30, jnp.int32)
    last = jnp.zeros((1, LANES), jnp.int32)
    start = jnp.int32(0)
    count = lengths_ref.shape[1]
    for segment in range(count + 1):
        end = start + lengths_ref[0, segment] if segment < count else jnp.int32(2**30)
        first = jnp.where(lane == segment, start, first)
        last = jnp.where(lane == segment, end, last)
        start = end
    return first, last


def segment_flags(start, rows, bounds):
    position = start + lax.broadcasted_iota(jnp.int32, (rows, LANES), 0)
    return (position >= bounds[0]) & (position < bounds[1])


def three_parts(value):
    first = value.astype(LOW)
    rest = value - first.astype(FULL)
    second = rest.astype(LOW)
    third = (rest - second.astype(FULL)).astype(LOW)
    return first.astype(FULL), second.astype(FULL), third.astype(FULL)


def with_parts(base, value, lane, slot):
    first, second, third = three_parts(value)
    base = jnp.where(lane == slot, first, base)
    base = jnp.where(lane == slot + 1, second, base)
    return jnp.where(lane == slot + 2, third, base)


def query_flags(lengths_ref, start, rows):
    segments = lengths_ref.shape[1] + 1
    lane = lane_numbers((rows, LANES)) & (HEAD_DIM - 1)
    own = segment_flags(start, rows, segment_bounds(lengths_ref))
    return jnp.where(own | (lane >= segments), 0.0, mask_step)


def key_flags(lengths_ref, start, rows):
    segments = lengths_ref.shape[1] + 1
    lane = lane_numbers((rows, LANES)) & (HEAD_DIM - 1)
    own = segment_flags(start, rows, segment_bounds(lengths_ref))
    return jnp.where(own | ((lane >= segments) & (lane < segments + 3)), 1.0, 0.0).astype(LOW)


def fill_weight(target, quarters, home, columns):
    first, folds = columns
    width = target.shape[1]
    for core in range(2):
        for plane in range(4):
            for far in range(4):
                block = block_number(home, core, plane, far)
                piece = quarters[core * 4 + plane]
                for fold in range(folds):
                    row = pl.multiple_of(block * (TILE_ROWS * folds) + fold * TILE_ROWS, TILE_ROWS)
                    start = first + fold * width
                    target[pl.ds(row, TILE_ROWS), :] = piece[far, :, start : start + width]


def pack_grad(source, kept, sent, home, columns):
    first, folds = columns
    width = source.shape[1]
    for core, target in ((0, kept), (1, sent)):
        for plane in range(4):
            for far in range(4):
                block = block_number(home, core, plane, far)
                for fold in range(folds):
                    row = pl.multiple_of(block * (TILE_ROWS * folds) + fold * TILE_ROWS, TILE_ROWS)
                    start = first + fold * width
                    target[plane, far, :, start : start + width] = source[pl.ds(row, TILE_ROWS), :]


def normalise(states):
    centred = states - jnp.mean(states, axis=1, keepdims=True)
    spread = jnp.mean(centred * centred, axis=1, keepdims=True)
    scale = lax.rsqrt(spread + ln_eps)
    return centred * scale, scale


def norm_backward(cotangent, unit, scale, gain):
    scaled = cotangent * gain
    grad = scale * (
        scaled
        - jnp.mean(scaled, axis=1, keepdims=True)
        - unit * jnp.mean(scaled * unit, axis=1, keepdims=True)
    )
    return (
        grad,
        jnp.sum(cotangent * unit, axis=0, keepdims=True),
        jnp.sum(cotangent, axis=0, keepdims=True),
    )


KEY_STEP = 256


def attend_pair(query, flags, key_aug, value_aug, segments):
    rows = query.shape[0]
    keys = key_aug.shape[1]
    lane = lane_numbers((rows, LANES))
    mixes = []
    kept = []
    for head in range(2):
        mine = (lane < HEAD_DIM) if head == 0 else (lane >= HEAD_DIM)
        slot = segments + (HEAD_DIM if head == 0 else 0)
        base = jnp.where(mine, query, flags)
        plain = base.astype(LOW)
        peak = jnp.full((rows, LANES), -jnp.inf, FULL)
        for start in range(0, keys, KEY_STEP):
            scores = dot(plain, key_aug[head, start : start + KEY_STEP], BY_LANES)
            for at in range(0, KEY_STEP, LANES):
                peak = jnp.maximum(peak, scores[:, at : at + LANES])
        peak = jnp.max(peak, axis=1, keepdims=True)
        shifted = with_parts(base, -peak, lane, slot).astype(LOW)
        total = jnp.zeros((rows, LANES), FULL)
        for start in range(0, keys, KEY_STEP):
            scores = dot(shifted, key_aug[head, start : start + KEY_STEP], BY_LANES)
            weights = jnp.exp(scores).astype(LOW)
            total = total + dot(weights, value_aug[head, start : start + KEY_STEP])
        weight_sum = total[:, HEAD_DIM : HEAD_DIM + 1] if head == 0 else total[:, 0:1]
        kept.append(with_parts(base, -(peak + jnp.log(weight_sum)), lane, slot).astype(LOW))
        mixes.append(total / weight_sum)
    return jnp.where(lane < HEAD_DIM, mixes[0], mixes[1]).astype(LOW), kept


def widen_pair(key, value, flags, key_aug, value_aug, start):
    rows = key.shape[0]
    lane = lane_numbers((rows, LANES))
    ones = jnp.ones((rows, LANES), LOW)
    for head in range(2):
        mine = (lane < HEAD_DIM) if head == 0 else (lane >= HEAD_DIM)
        key_aug[head, start : start + rows] = jnp.where(mine, key, flags)
        value_aug[head, start : start + rows] = jnp.where(mine, value, ones)


def pair_columns(first, pair):
    return pl.ds(pl.multiple_of(first + pair * LANES, LANES), LANES)


def self_forward_kernel(
    info, lengths, rows_0, rows_1, rows_2, rows_3, *refs
):
    quarters = refs[:8]
    mix_ref, query_ref, key_ref, value_ref, weight, flags_q, flags_k, key_aug, value_aug = refs[8:]
    pair = pl.program_id(0)
    home, place = info[0], info[1]
    local, width = rows_0.shape
    segments = lengths.shape[1] + 1

    @pl.when(pair == 0)
    def _():
        fill_weight(weight, quarters, home, (0, 1))
        flags_q[...] = query_flags(lengths, place * local, local)
        for step in range(4):
            flags_k[step * local : (step + 1) * local] = key_flags(
                lengths, (place ^ step) * local, local
            )

    both = jnp.concatenate(
        [weight[:, pair_columns(width, pair)], weight[:, pair_columns(2 * width, pair)]], axis=1
    )
    for step, rows in enumerate((rows_0, rows_1, rows_2, rows_3)):
        start = step * local
        made = dot(rows[...], both).astype(LOW)
        key, value = made[:, :LANES], made[:, LANES:]
        key_ref[start : start + local] = key
        value_ref[start : start + local] = value
        widen_pair(key, value, flags_k[start : start + local], key_aug, value_aug, start)
    query = dot(rows_0[...], weight[:, pair_columns(0, pair)]).astype(LOW).astype(FULL)
    mix, kept = attend_pair(query * score_scale, flags_q[...], key_aug, value_aug, segments)
    mix_ref[...] = mix
    query_ref[0] = kept[0]
    query_ref[1] = kept[1]


def cross_forward_kernel(
    info, target_lengths, source_lengths, mix, states, rows_0, rows_1, rows_2, rows_3, *refs
):
    quarters = refs[:8]
    (
        mix_ref,
        query_ref,
        key_ref,
        value_ref,
        unit_ref,
        scale_ref,
        norms_ref,
        out_weight,
        query_weight,
        pair_weight,
        norm_rows,
        queries,
        flags_q,
        flags_k,
        key_aug,
        value_aug,
    ) = refs[8:]
    pair = pl.program_id(0)
    home, place = info[0], info[1]
    local, width = rows_0.shape
    segments = target_lengths.shape[1] + 1

    @pl.when(pair == 0)
    def _():
        fill_weight(out_weight, quarters, home, (0, 1))
        fill_weight(query_weight, quarters, home, (width, 1))
        fill_weight(pair_weight, quarters, home, (2 * width, 1))
        fill_weight(norm_rows, quarters, home, (4 * width, 1))
        norms = norm_rows[...].astype(FULL).T[0:8]
        norms_ref[...] = norms
        mixed = states[...].astype(FULL) + dot(mix[...], out_weight[...])
        unit, scale = normalise(mixed)
        unit_ref[...] = unit
        scale_ref[...] = jnp.broadcast_to(scale, (local, LANES))
        first_low = (unit * norms[0:1] + norms[3:4]).astype(LOW)
        made = dot(first_low, query_weight[...]).astype(LOW)
        for at in range(queries.shape[0]):
            queries[at] = made[:, at * LANES : (at + 1) * LANES]
        flags_q[...] = query_flags(target_lengths, place * local, local)
        for step in range(4):
            flags_k[step * local : (step + 1) * local] = key_flags(
                source_lengths, (place ^ step) * local, local
            )

    both = jnp.concatenate(
        [pair_weight[:, pair_columns(0, pair)], pair_weight[:, pair_columns(width, pair)]], axis=1
    )
    for step, rows in enumerate((rows_0, rows_1, rows_2, rows_3)):
        start = step * local
        made = dot(rows[...], both).astype(LOW)
        key, value = made[:, :LANES], made[:, LANES:]
        key_ref[start : start + local] = key
        value_ref[start : start + local] = value
        widen_pair(key, value, flags_k[start : start + local], key_aug, value_aug, start)
    query = queries[pair].astype(FULL)
    mixed, kept = attend_pair(query * score_scale, flags_q[...], key_aug, value_aug, segments)
    mix_ref[...] = mixed
    query_ref[0] = kept[0]
    query_ref[1] = kept[1]


gelu_factor = 0.7978845608028654
gelu_cubic = 0.044715


def gelu_and_slope(hidden):
    square = hidden * hidden
    bend = jnp.tanh(gelu_factor * (hidden + gelu_cubic * (square * hidden)))
    half = 0.5 * (1.0 + bend)
    slope = half + (0.5 * hidden) * (1.0 - bend * bend) * (
        gelu_factor * (1.0 + (3.0 * gelu_cubic) * square)
    )
    return hidden * half, slope


def middle_kernel(info, mix, first_unit, norms, out_grad, *refs):
    quarters = refs[:8]
    (
        output_ref,
        second_grad_ref,
        mix_grad_ref,
        norm_sums_ref,
        kept,
        sent,
        out_weight,
        expand,
        contract,
        active,
        slope,
        wide_grad,
        tall_grad,
        out_weight_grad,
    ) = refs[8:]
    home = info[0]
    width = mix.shape[1]
    chunks = active.shape[0]
    span = expand.shape[1] // chunks
    fill_weight(out_weight, quarters, home, (0, 1))
    fill_weight(expand, quarters, home, (width, 1))
    fill_weight(contract, quarters, home, (width + expand.shape[1], contract.shape[0] // 512))
    first_norm = first_unit[...] * norms[0:1] + norms[3:4]
    second_unit, second_scale = normalise(first_norm + dot(mix[...], out_weight[...]))
    second_norm = second_unit * norms[1:2] + norms[4:5]
    second_low = second_norm.astype(LOW)

    def forward(at, total):
        start = pl.multiple_of(at * span, span)
        hidden = dot(second_low, expand[:, pl.ds(start, span)])
        made, bent = gelu_and_slope(hidden)
        made = made.astype(LOW)
        active[at] = made
        slope[at] = bent
        return total + dot(made, contract[pl.ds(start, span)])

    mixed = lax.fori_loop(0, chunks, forward, second_norm)
    third_unit, third_scale = normalise(mixed)
    output_ref[...] = third_unit * norms[2:3] + norms[5:6]
    third_grad, gain_three, bias_three = norm_backward(
        out_grad[...], third_unit, third_scale, norms[2:3]
    )
    ffn_grad = third_grad.astype(LOW)
    second_turned = second_low.T

    def backward(at, total):
        start = pl.multiple_of(at * span, span)
        part = contract[pl.ds(start, span)]
        hidden_grad = (dot(ffn_grad, part, BY_LANES) * slope[at]).astype(LOW)
        tall_grad[pl.ds(start, span)] = dot(active[at].T, ffn_grad).astype(LOW)
        wide_grad[:, pl.ds(start, span)] = dot(second_turned, hidden_grad).astype(LOW)
        return total + dot(hidden_grad, expand[:, pl.ds(start, span)], BY_LANES)

    second_cotangent = lax.fori_loop(0, chunks, backward, third_grad)
    second_grad, gain_two, bias_two = norm_backward(
        second_cotangent, second_unit, second_scale, norms[1:2]
    )
    second_grad_ref[...] = second_grad
    cross_out_low = second_grad.astype(LOW)
    mix_grad_ref[...] = dot(cross_out_low, out_weight[...], BY_LANES).astype(LOW)
    out_weight_grad[...] = dot(mix[...].T, cross_out_low).astype(LOW)
    norm_sums_ref[...] = jnp.zeros(norm_sums_ref.shape, FULL)
    norm_sums_ref[1:2] = gain_two
    norm_sums_ref[2:3] = gain_three
    norm_sums_ref[4:5] = bias_two
    norm_sums_ref[5:6] = bias_three
    pack_grad(out_weight_grad, kept, sent, home, (0, 1))
    pack_grad(wide_grad, kept, sent, home, (width, 1))
    pack_grad(tall_grad, kept, sent, home, (width + expand.shape[1], tall_grad.shape[0] // 512))


def attend_back_pair(queries, key, value, flags, mix, grad, segments, key_aug, value_aug, made):
    rows = grad.shape[0]
    keys = key.shape[0]
    lane = lane_numbers((rows, LANES))
    widen_pair(key, value, flags, key_aug, value_aug, 0)
    grad = grad.astype(FULL)
    product = grad * mix.astype(FULL)
    grads = []
    totals = []
    for head in range(2):
        mine = (lane < HEAD_DIM) if head == 0 else (lane >= HEAD_DIM)
        slot = segments + (HEAD_DIM if head == 0 else 0)
        inner = jnp.sum(jnp.where(mine, product, 0.0), axis=1, keepdims=True)
        grads.append(with_parts(jnp.where(mine, grad, 0.0), -inner, lane, slot).astype(LOW))
        totals.append(jnp.zeros((HEAD_DIM, rows), FULL))
    turned = key.T
    lane = lane_numbers((KEY_STEP, LANES))
    for start in range(0, keys, KEY_STEP):
        span = slice(start, start + KEY_STEP)
        key_parts = []
        value_parts = []
        for head in range(2):
            probs = jnp.exp(dot(key_aug[head, span], queries[head], BY_LANES))
            shifted = dot(value_aug[head, span], grads[head], BY_LANES)
            score_grad = (probs * shifted).astype(LOW)
            value_parts.append(dot(probs.astype(LOW), grads[head]))
            key_parts.append(dot(score_grad, queries[head]))
            part = turned[head * HEAD_DIM : (head + 1) * HEAD_DIM, span]
            totals[head] = totals[head] + dot(part, score_grad)
        made[span, :LANES] = jnp.where(lane < HEAD_DIM, key_parts[0], key_parts[1]).astype(LOW)
        made[span, LANES:] = jnp.where(lane < HEAD_DIM, value_parts[0], value_parts[1]).astype(LOW)
    return (jnp.concatenate(totals, axis=0).T * score_scale).astype(LOW)


def cross_backward_kernel(
    info, source_lengths, queries, key, value, mix, grad, rows_0, rows_1, rows_2, rows_3, *refs
):
    quarters = refs[:8]
    (
        query_grad_ref,
        weight_grad_ref,
        own_ref,
        parts_ref,
        weight,
        flags_k,
        key_aug,
        value_aug,
        made,
    ) = refs[8:]
    pair = pl.program_id(0)
    home, place = info[0], info[1]
    local, width = rows_0.shape
    pairs = made.shape[0]
    segments = source_lengths.shape[1] + 1

    @pl.when(pair == 0)
    def _():
        fill_weight(weight, quarters, home, (2 * width, 1))
        for step in range(4):
            flags_k[step * local : (step + 1) * local] = key_flags(
                source_lengths, (place ^ step) * local, local
            )

    query_grad_ref[...] = attend_back_pair(
        queries, key[...], value[...], flags_k[...], mix[...], grad[...], segments, key_aug, value_aug, made.at[pair]
    )

    @pl.when(pair == pairs - 1)
    def _():
        finish_rows(made, weight, 0, (rows_0, rows_1, rows_2, rows_3), own_ref, parts_ref, weight_grad_ref, 0)


def finish_rows(made, weight, first, row_refs, own_ref, parts_ref, weight_grad_ref, grad_first):
    local, width = row_refs[0].shape
    pairs = made.shape[0]
    turned = [rows[...].T for rows in row_refs]
    for step in range(4):
        total = None
        for pair in range(pairs):
            at = first + pair * LANES
            columns = jnp.concatenate(
                [weight[:, at : at + LANES], weight[:, width + at : width + at + LANES]], axis=1
            )
            term = dot(made[pair, step * local : (step + 1) * local], columns, BY_LANES)
            total = term if total is None else total + term
        if step == 0:
            own_ref[...] = total
        else:
            parts_ref[step - 1] = total.astype(LOW)
    for pair in range(pairs):
        total = None
        for step in range(4):
            term = dot(turned[step], made[pair, step * local : (step + 1) * local])
            total = term if total is None else total + term
        at = grad_first + pair * LANES
        weight_grad_ref[:, at : at + LANES] = total[:, :LANES].astype(LOW)
        weight_grad_ref[:, width + at : width + at + LANES] = total[:, LANES:].astype(LOW)


def between_kernel(
    info, query_grad, second_grad, first_unit, first_scale, norms, norm_sums, self_mix, pair_grad, *refs
):
    quarters = refs[:8]
    (
        first_grad_ref,
        mix_grad_ref,
        kept,
        sent,
        out_weight,
        query_weight,
        out_grad,
        query_weight_grad,
        norm_grad,
        norm_rows,
    ) = refs[8:]
    home = info[0]
    width = self_mix.shape[1]
    fill_weight(out_weight, quarters, home, (0, 1))
    fill_weight(query_weight, quarters, home, (width, 1))
    unit = first_unit[...]
    first_low = (unit * norms[0:1] + norms[3:4]).astype(LOW)
    low_grad = query_grad[...]
    query_weight_grad[...] = dot(first_low.T, low_grad).astype(LOW)
    cotangent = second_grad[...] + dot(low_grad, query_weight[...], BY_LANES)
    first_grad, gain_one, bias_one = norm_backward(
        cotangent, unit, first_scale[:, 0:1], norms[0:1]
    )
    first_grad_ref[...] = first_grad
    self_out_low = first_grad.astype(LOW)
    out_grad[...] = dot(self_mix[...].T, self_out_low).astype(LOW)
    mix_grad_ref[...] = dot(self_out_low, out_weight[...], BY_LANES).astype(LOW)
    norm_rows[...] = jnp.zeros(norm_rows.shape, FULL)
    norm_rows[0:8] = norm_sums[...]
    norm_rows[0:1] = gain_one
    norm_rows[3:4] = bias_one
    norm_grad[...] = norm_rows[...].T.astype(LOW)
    pack_grad(out_grad, kept, sent, home, (0, 1))
    pack_grad(query_weight_grad, kept, sent, home, (width, 1))
    pack_grad(pair_grad, kept, sent, home, (2 * width, 1))
    pack_grad(norm_grad, kept, sent, home, (4 * width, 1))


def self_backward_kernel(
    info, lengths, queries, key, value, mix, grad, first_grad, rows_0, rows_1, rows_2, rows_3, *refs
):
    quarters = refs[:8]
    (
        own_ref,
        parts_ref,
        kept,
        sent,
        weight,
        flags_k,
        key_aug,
        value_aug,
        made,
        query_grads,
        weight_grad,
    ) = refs[8:]
    pair = pl.program_id(0)
    home, place = info[0], info[1]
    local, width = rows_0.shape
    pairs = made.shape[0]
    segments = lengths.shape[1] + 1

    @pl.when(pair == 0)
    def _():
        fill_weight(weight, quarters, home, (0, 1))
        for step in range(4):
            flags_k[step * local : (step + 1) * local] = key_flags(
                lengths, (place ^ step) * local, local
            )

    query_grads[pair] = attend_back_pair(
        queries, key[...], value[...], flags_k[...], mix[...], grad[...], segments, key_aug, value_aug, made.at[pair]
    )

    @pl.when(pair == pairs - 1)
    def _():
        finish_rows(
            made, weight, width, (rows_0, rows_1, rows_2, rows_3), own_ref, parts_ref, weight_grad, width
        )
        low_grad = jnp.concatenate([query_grads[at] for at in range(pairs)], axis=1)
        weight_grad[:, 0:width] = dot(rows_0[...].T, low_grad).astype(LOW)
        own_ref[...] += first_grad[...] + dot(low_grad, weight[:, 0:width], BY_LANES)
        pack_grad(weight_grad, kept, sent, home, (0, 1))


def whole(shape):
    return pl.BlockSpec(shape, lambda *at: (0,) * len(shape))


def call(kernel, inputs, specs, outputs, out_specs, scratch, grid=(), flops=0):
    moved = sum(a.size * a.dtype.itemsize for a in inputs) + sum(
        a.size * a.dtype.itemsize for a in outputs
    )
    return pl.pallas_call(
        kernel,
        out_shape=outputs,
        grid=grid,
        in_specs=specs,
        out_specs=out_specs,
        scratch_shapes=scratch,
        compiler_params=pltpu.CompilerParams(vmem_limit_bytes=VMEM_BYTES),
        cost_estimate=pl.CostEstimate(flops=flops, bytes_accessed=moved, transcendentals=0),
    )(*inputs)


SCALARS = pl.BlockSpec(memory_space=pltpu.SMEM)


def shaped(shape, kind):
    return jax.ShapeDtypeStruct(shape, kind)


def per_device(
    target_states,
    memory,
    target_lengths,
    source_lengths,
    self_project,
    self_output,
    cross_project,
    memory_project,
    cross_output,
    expand_weight,
    contract_weight,
    norm_gain,
    norm_bias,
    out_grad,
):
    _, local, width = target_states.shape
    states = target_states[0]
    own_memory = memory[0]
    rows = self_project.shape[0]
    ff = expand_weight.shape[1]
    keys = local * 4
    pairs = width // LANES
    scores = 2 * local * keys * width * 4
    info = jnp.stack([home_number(), lax.axis_index("narrow")]).astype(jnp.int32)

    norm_shard = jnp.concatenate([norm_gain, norm_bias], axis=0).T
    norm_shard = jnp.pad(norm_shard, ((0, 0), (0, LANES - norm_shard.shape[1])))
    batch_1 = self_project
    batch_2 = jnp.concatenate([self_output, cross_project, memory_project, norm_shard], axis=1)
    batch_3 = jnp.concatenate(
        [cross_output, expand_weight, fold_rows(contract_weight, rows)], axis=1
    )
    far_1 = gather_far(batch_1)
    states_x = exchange(states, 2)
    states_c = exchange(states, 1)
    far_2 = gather_far(batch_2)
    plane_1 = gather_plane(far_1)
    far_3 = gather_far(batch_3)
    states_xc = exchange(states_x, 1)
    weights_1 = gather_core(plane_1)
    row_states = [states, states_c, states_x, states_xc]

    plane_2 = gather_plane(far_2)
    memory_x = exchange(own_memory, 2)
    memory_c = exchange(own_memory, 1)

    row_spec = whole((local, width))
    pair_rows = pl.BlockSpec((local, LANES), lambda pair: (0, pair))
    pair_keys = pl.BlockSpec((keys, LANES), lambda pair: (0, pair))
    pair_heads = pl.BlockSpec((2, local, LANES), lambda pair: (pair, 0, 0))
    quarter_specs_1 = [whole(q.shape) for q in weights_1]
    attend_scratch = [
        pltpu.VMEM((local, LANES), FULL),
        pltpu.VMEM((keys, LANES), LOW),
        pltpu.VMEM((2, keys, LANES), LOW),
        pltpu.VMEM((2, keys, LANES), LOW),
    ]
    self_mix, self_queries, self_key, self_value = call(
        self_forward_kernel,
        [info, target_lengths, *row_states, *weights_1],
        [SCALARS, SCALARS] + [row_spec] * 4 + quarter_specs_1,
        [
            shaped((local, width), LOW),
            shaped((2 * pairs, local, LANES), LOW),
            shaped((keys, width), LOW),
            shaped((keys, width), LOW),
        ],
        [pair_rows, pair_heads, pair_keys, pair_keys],
        [pltpu.VMEM((width, 3 * width), LOW)] + attend_scratch,
        grid=(pairs,),
        flops=scores * 3,
    )

    memory_xc = exchange(memory_x, 1)
    weights_2 = gather_core(plane_2)
    row_memory = [own_memory, memory_c, memory_x, memory_xc]
    plane_3 = gather_plane(far_3)
    quarter_specs_2 = [whole(q.shape) for q in weights_2]
    cross_mix, cross_queries, cross_key, cross_value, first_unit, first_scale, norms = call(
        cross_forward_kernel,
        [info, target_lengths, source_lengths, self_mix, states, *row_memory, *weights_2],
        [SCALARS] * 3 + [row_spec] * 6 + quarter_specs_2,
        [
            shaped((local, width), LOW),
            shaped((2 * pairs, local, LANES), LOW),
            shaped((keys, width), LOW),
            shaped((keys, width), LOW),
            shaped((local, width), FULL),
            shaped((local, LANES), FULL),
            shaped((8, width), FULL),
        ],
        [
            pair_rows,
            pair_heads,
            pair_keys,
            pair_keys,
            row_spec,
            whole((local, LANES)),
            whole((8, width)),
        ],
        [
            pltpu.VMEM((width, width), LOW),
            pltpu.VMEM((width, width), LOW),
            pltpu.VMEM((width, 2 * width), LOW),
            pltpu.VMEM((width, LANES), LOW),
            pltpu.VMEM((pairs, local, LANES), LOW),
        ]
        + attend_scratch,
        grid=(pairs,),
        flops=scores * 3,
    )

    weights_3 = gather_core(plane_3, ff // width)
    quarter_specs_3 = [whole(q.shape) for q in weights_3]
    columns_3 = width + 2 * ff
    chunk_count = ff // 512
    packed_3 = (4, 4, TILE_ROWS, columns_3)
    output, second_grad, cross_mix_grad, norm_sums, kept_3, sent_3 = call(
        middle_kernel,
        [info, cross_mix, first_unit, norms, out_grad[0], *weights_3],
        [SCALARS, row_spec, row_spec, whole((8, width)), row_spec] + quarter_specs_3,
        [
            shaped((local, width), FULL),
            shaped((local, width), FULL),
            shaped((local, width), LOW),
            shaped((8, width), FULL),
            shaped(packed_3, LOW),
            shaped(packed_3, LOW),
        ],
        [
            row_spec,
            row_spec,
            row_spec,
            whole((8, width)),
            whole(packed_3),
            whole(packed_3),
        ],
        [
            pltpu.VMEM((width, width), LOW),
            pltpu.VMEM((width, ff), LOW),
            pltpu.VMEM((ff, width), LOW),
            pltpu.VMEM((chunk_count, local, 512), LOW),
            pltpu.VMEM((chunk_count, local, 512), FULL),
            pltpu.VMEM((width, ff), LOW),
            pltpu.VMEM((ff, width), LOW),
            pltpu.VMEM((width, width), LOW),
        ],
        flops=2 * local * width * ff * 6,
    )
    core_3 = reduce_core(kept_3, sent_3)

    back_scratch = [
        pltpu.VMEM((keys, LANES), LOW),
        pltpu.VMEM((2, keys, LANES), LOW),
        pltpu.VMEM((2, keys, LANES), LOW),
        pltpu.VMEM((pairs, keys, 2 * LANES), LOW),
    ]
    parts_shape = (3, local, width)
    cross_query_grad, pair_weight_grad, memory_own, memory_parts = call(
        cross_backward_kernel,
        [
            info,
            source_lengths,
            cross_queries,
            cross_key,
            cross_value,
            cross_mix,
            cross_mix_grad,
            *row_memory,
            *weights_2,
        ],
        [SCALARS] * 2
        + [pair_heads, pair_keys, pair_keys, pair_rows, pair_rows]
        + [row_spec] * 4
        + quarter_specs_2,
        [
            shaped((local, width), LOW),
            shaped((width, 2 * width), LOW),
            shaped((local, width), FULL),
            shaped(parts_shape, LOW),
        ],
        [pair_rows, whole((width, 2 * width)), row_spec, whole(parts_shape)],
        [pltpu.VMEM((width, 2 * width), LOW)] + back_scratch,
        grid=(pairs,),
        flops=scores * 5,
    )
    plane_sum_3 = reduce_plane(core_3)
    memory_grad = reduce_row(memory_own, memory_parts)

    packed_2 = (4, 4, TILE_ROWS, 4 * width + LANES)
    first_grad, self_mix_grad, kept_2, sent_2 = call(
        between_kernel,
        [
            info,
            cross_query_grad,
            second_grad,
            first_unit,
            first_scale,
            norms,
            norm_sums,
            self_mix,
            pair_weight_grad,
            *weights_2,
        ],
        [SCALARS, row_spec, row_spec, row_spec, whole((local, LANES))]
        + [whole((8, width))] * 2
        + [row_spec, whole((width, 2 * width))]
        + quarter_specs_2,
        [
            shaped((local, width), FULL),
            shaped((local, width), LOW),
            shaped(packed_2, LOW),
            shaped(packed_2, LOW),
        ],
        [row_spec, row_spec, whole(packed_2), whole(packed_2)],
        [
            pltpu.VMEM((width, width), LOW),
            pltpu.VMEM((width, width), LOW),
            pltpu.VMEM((width, width), LOW),
            pltpu.VMEM((width, width), LOW),
            pltpu.VMEM((width, LANES), LOW),
            pltpu.VMEM((LANES, width), FULL),
        ],
        flops=2 * local * width * width * 4,
    )
    core_2 = reduce_core(kept_2, sent_2)

    packed_1 = (4, 4, TILE_ROWS, 3 * width)
    states_own, states_parts, kept_1, sent_1 = call(
        self_backward_kernel,
        [
            info,
            target_lengths,
            self_queries,
            self_key,
            self_value,
            self_mix,
            self_mix_grad,
            first_grad,
            *row_states,
            *weights_1,
        ],
        [SCALARS] * 2
        + [pair_heads, pair_keys, pair_keys, pair_rows, pair_rows]
        + [row_spec] * 5
        + quarter_specs_1,
        [
            shaped((local, width), FULL),
            shaped(parts_shape, LOW),
            shaped(packed_1, LOW),
            shaped(packed_1, LOW),
        ],
        [row_spec, whole(parts_shape), whole(packed_1), whole(packed_1)],
        [pltpu.VMEM((width, 3 * width), LOW)]
        + back_scratch
        + [pltpu.VMEM((pairs, local, LANES), LOW), pltpu.VMEM((width, 3 * width), LOW)],
        grid=(pairs,),
        flops=scores * 5,
    )
    core_1 = reduce_core(kept_1, sent_1)
    plane_sum_1 = reduce_plane(core_1)
    plane_sum_2 = reduce_plane(core_2)
    states_grad = reduce_row(states_own, states_parts)
    grad_3 = reduce_far(plane_sum_3, ff // width)
    grad_2 = reduce_far(plane_sum_2)
    grad_1 = reduce_far(plane_sum_1)
    count = norm_gain.shape[0]
    norm_grads = grad_2[:, 4 * width :].T
    return (
        output[None],
        states_grad[None],
        memory_grad[None],
        grad_1,
        grad_2[:, :width],
        grad_2[:, width : 2 * width],
        grad_2[:, 2 * width : 4 * width],
        grad_3[:, :width],
        grad_3[:, width : width + ff],
        unfold_rows(grad_3[:, width + ff :], width),
        norm_grads[:count],
        norm_grads[count : 2 * count],
    )


def reduce_row(own, parts):
    from_core = exchange(parts[0], 1)
    from_far = exchange(parts[2], 1)
    other = (parts[1].astype(FULL) + from_far.astype(FULL)).astype(LOW)
    return own + from_core.astype(FULL) + exchange(other, 2).astype(FULL)


def solution(mesh):
    in_specs = (
        P("wide", "narrow", None),
        P("wide", "narrow", None),
        P("wide", None),
        P("wide", None),
        P(("wide", "narrow"), None),
        P(("wide", "narrow"), None),
        P(("wide", "narrow"), None),
        P(("wide", "narrow"), None),
        P(("wide", "narrow"), None),
        P(("wide", "narrow"), None),
        P(("wide", "narrow"), None),
        P(None, ("wide", "narrow")),
        P(None, ("wide", "narrow")),
        P("wide", "narrow", None),
    )
    out_specs = (
        P("wide", "narrow", None),
        P("wide", "narrow", None),
        P("wide", "narrow", None),
        P(("wide", "narrow"), None),
        P(("wide", "narrow"), None),
        P(("wide", "narrow"), None),
        P(("wide", "narrow"), None),
        P(("wide", "narrow"), None),
        P(("wide", "narrow"), None),
        P(("wide", "narrow"), None),
        P(None, ("wide", "narrow")),
        P(None, ("wide", "narrow")),
    )
    return jax.shard_map(
        per_device, mesh=mesh, in_specs=in_specs, out_specs=out_specs, check_vma=False
    )
```

```python
import functools
import math

import jax
import jax.numpy as jnp
from jax import lax
from jax.experimental import pallas as pl
from jax.experimental.pallas import tpu as pltpu
from jax.sharding import PartitionSpec as P

HEAD_DIM = 64
LANES = 128
TILE_ROWS = 16
BLOCKS = 32
AXES = ("wide", "narrow")
LOW = jnp.bfloat16
FULL = jnp.float32

ln_eps = 1e-05
score_scale = HEAD_DIM ** (-0.5)
mask_step = -(2.0**30)

BY_LANES = (((1,), (1,)), ((), ()))
PLAIN = (((1,), (0,)), ((), ()))


def dot(left, right, dims=PLAIN):
    return lax.dot_general(left, right, dims, preferred_element_type=FULL)


def exchange(block, mask):
    device_count = lax.axis_size("wide") * lax.axis_size("narrow")
    pairs = [(device, device ^ mask) for device in range(device_count)]
    return lax.ppermute(block, AXES, pairs)


def device_number():
    return lax.axis_index("wide") * lax.axis_size("narrow") + lax.axis_index("narrow")


def staged():
    return lax.axis_size("wide") * lax.axis_size("narrow") == BLOCKS


FAR = (8, 16, 24)
PLANE = (2, 4, 6)


def gather_far(shard):
    if not staged():
        return shard
    return [shard] + [exchange(shard, mask) for mask in FAR]


def gather_plane(held):
    if not staged():
        return held
    return [held] + [exchange(held, mask) for mask in PLANE]


def gather_core(held, folds=0):
    if staged():
        return held + [exchange(quarter, 1) for quarter in held]
    whole = lax.all_gather(held, AXES, axis=0, tiled=True)
    if folds:
        rows, columns = held.shape
        split = columns - folds * whole.shape[0]
        tall = unfold_rows(held[:, split:], whole.shape[0])
        tall = lax.all_gather(tall, AXES, axis=0, tiled=True)
        tall = tall.reshape(BLOCKS, folds, TILE_ROWS, -1).transpose(0, 2, 1, 3)
        whole = jnp.concatenate([whole[:, :split], tall.reshape(whole.shape[0], -1)], axis=1)
    whole = whole.reshape(4, 4, 2, TILE_ROWS, held.shape[1]).transpose(2, 1, 0, 3, 4)
    return [whole[core, plane] for core in range(2) for plane in range(4)]


def home_number():
    return device_number() if staged() else jnp.zeros((), jnp.int32)


def block_number(home, core, plane, far):
    return home ^ (far * 8 + plane * 2 + core)


def add_all(first, others):
    total = first.astype(FULL)
    for other in others:
        total = total + other.astype(FULL)
    return total


def exchange_core(sent):
    return exchange(sent, 1) if staged() else sent


def reduce_core(kept, other):
    return add_all(kept, [other]).astype(LOW) if staged() else (kept, other)


def exchange_plane(held):
    if not staged():
        return held
    return [held[0]] + [exchange(held[plane + 1], mask) for plane, mask in enumerate(PLANE)]


def reduce_plane(planes):
    return add_all(planes[0], planes[1:]).astype(LOW) if staged() else planes


def exchange_far(held):
    if not staged():
        return held
    return [held[0]] + [exchange(held[far + 1], mask) for far, mask in enumerate(FAR)]


def exchange_half(held):
    return exchange(held[2:], FAR[1]) if staged() else held


def reduce_half(held, other):
    return add_all(held[:2], [other]).astype(LOW) if staged() else held


def exchange_near(held):
    return [held[0], exchange(held[1], FAR[0])] if staged() else held


def reduce_far(held, folds=0):
    if staged():
        return add_all(held[0], held[1:])
    whole = jnp.stack(held).transpose(2, 1, 0, 3, 4)
    whole = whole.reshape(BLOCKS * TILE_ROWS, -1).astype(FULL)
    if folds:
        split = whole.shape[1] - folds * whole.shape[0]
        tall = whole[:, split:].reshape(BLOCKS, TILE_ROWS, folds, -1).transpose(0, 2, 1, 3)
        tall = tall.reshape(folds * whole.shape[0], -1)
        tall = lax.psum_scatter(tall, AXES, scatter_dimension=0, tiled=True)
        whole = lax.psum_scatter(whole[:, :split], AXES, scatter_dimension=0, tiled=True)
        return jnp.concatenate([whole, fold_rows(tall, whole.shape[0])], axis=1)
    return lax.psum_scatter(whole, AXES, scatter_dimension=0, tiled=True)


def after(values, token):
    return lax.optimization_barrier((values, token))


def fold_rows(block, rows):
    return jnp.concatenate(
        [block[at : at + rows] for at in range(0, block.shape[0], rows)], axis=1
    )


def unfold_rows(block, width):
    return jnp.concatenate(
        [block[:, at : at + width] for at in range(0, block.shape[1], width)], axis=0
    )


def lane_numbers(shape):
    return lax.broadcasted_iota(jnp.int32, shape, 1)


def segment_bounds(lengths_ref):
    lane = lane_numbers((1, LANES)) & (HEAD_DIM - 1)
    first = jnp.full((1, LANES), 2**30, jnp.int32)
    last = jnp.zeros((1, LANES), jnp.int32)
    start = jnp.int32(0)
    count = lengths_ref.shape[1]
    for segment in range(count + 1):
        end = start + lengths_ref[0, segment] if segment < count else jnp.int32(2**30)
        first = jnp.where(lane == segment, start, first)
        last = jnp.where(lane == segment, end, last)
        start = end
    return first, last


def segment_flags(start, rows, bounds):
    position = start + lax.broadcasted_iota(jnp.int32, (rows, LANES), 0)
    return (position >= bounds[0]) & (position < bounds[1])


def three_parts(value):
    first = value.astype(LOW)
    rest = value - first.astype(FULL)
    second = rest.astype(LOW)
    third = (rest - second.astype(FULL)).astype(LOW)
    return first.astype(FULL), second.astype(FULL), third.astype(FULL)


def with_parts(base, value, lane, slot):
    first, second, third = three_parts(value)
    base = jnp.where(lane == slot, first, base)
    base = jnp.where(lane == slot + 1, second, base)
    return jnp.where(lane == slot + 2, third, base)


def query_flags(lengths_ref, start, rows):
    segments = lengths_ref.shape[1] + 1
    lane = lane_numbers((rows, LANES)) & (HEAD_DIM - 1)
    own = segment_flags(start, rows, segment_bounds(lengths_ref))
    return jnp.where(own | (lane >= segments), 0.0, mask_step)


def key_flags(lengths_ref, start, rows):
    segments = lengths_ref.shape[1] + 1
    lane = lane_numbers((rows, LANES)) & (HEAD_DIM - 1)
    own = segment_flags(start, rows, segment_bounds(lengths_ref))
    return jnp.where(own | ((lane >= segments) & (lane < segments + 3)), 1.0, 0.0).astype(LOW)


def fill_weight(target, quarters, home, columns):
    first, folds = columns
    width = target.shape[1]
    for core in range(2):
        for plane in range(4):
            for far in range(4):
                block = block_number(home, core, plane, far)
                piece = quarters[core * 4 + plane]
                for fold in range(folds):
                    row = pl.multiple_of(block * (TILE_ROWS * folds) + fold * TILE_ROWS, TILE_ROWS)
                    start = first + fold * width
                    target[pl.ds(row, TILE_ROWS), :] = piece[far, :, start : start + width]


def pack_grad(source, kept, sent, home, columns):
    first, folds = columns
    width = source.shape[1]
    for core, target in ((0, kept), (1, sent)):
        for plane in range(4):
            for far in range(4):
                block = block_number(home, core, plane, far)
                for fold in range(folds):
                    row = pl.multiple_of(block * (TILE_ROWS * folds) + fold * TILE_ROWS, TILE_ROWS)
                    start = first + fold * width
                    target[plane, far, :, start : start + width] = source[pl.ds(row, TILE_ROWS), :]


def normalise(states):
    centred = states - jnp.mean(states, axis=1, keepdims=True)
    spread = jnp.mean(centred * centred, axis=1, keepdims=True)
    scale = lax.rsqrt(spread + ln_eps)
    return centred * scale, scale


def norm_backward(cotangent, unit, scale, gain):
    scaled = cotangent * gain
    grad = scale * (
        scaled
        - jnp.mean(scaled, axis=1, keepdims=True)
        - unit * jnp.mean(scaled * unit, axis=1, keepdims=True)
    )
    return (
        grad,
        jnp.sum(cotangent * unit, axis=0, keepdims=True),
        jnp.sum(cotangent, axis=0, keepdims=True),
    )


KEY_STEP = 256


def pack_kernel(*refs):
    ins, (first_ref, second_ref, square) = refs[:9], refs[9:]
    self_project, self_output, cross_project, memory_project, cross_output, expand, contract, gain, bias = ins
    rows, width = self_output.shape
    at = 0
    for part in (self_project, self_output, cross_project, memory_project):
        first_ref[:, at : at + part.shape[1]] = part[...]
        at += part.shape[1]
    count = gain.shape[0]
    square[...] = jnp.zeros(square.shape, FULL)
    square[0:count, 0:rows] = gain[...].astype(FULL)
    square[count : 2 * count, 0:rows] = bias[...].astype(FULL)
    first_ref[:, at : at + LANES] = square[...].T[0:rows].astype(LOW)
    at = 0
    for part in (cross_output, expand):
        second_ref[:, at : at + part.shape[1]] = part[...]
        at += part.shape[1]
    for fold in range(contract.shape[0] // rows):
        second_ref[:, at : at + width] = contract[fold * rows : (fold + 1) * rows]
        at += width


def settle_kernel(first_0, first_1, first_2, first_3, second_0, second_1, *refs):
    project_ref, output_ref, cross_ref, memory_ref, cross_out_ref, gain_ref, bias_ref, square = refs
    rows, width = output_ref.shape

    def total(parts, start, span):
        return add_all(parts[0][:, start : start + span], [p[:, start : start + span] for p in parts[1:]])

    project_ref[...] = total((first_0, first_1, first_2, first_3), 0, project_ref.shape[1])
    seconds = (second_0, second_1)
    at = 0
    for ref in (output_ref, cross_ref, memory_ref, cross_out_ref):
        ref[...] = total(seconds, at, ref.shape[1])
        at += ref.shape[1]
    square[...] = jnp.zeros(square.shape, FULL)
    square[0:rows] = total(seconds, at, LANES)
    turned = square[...].T
    count = gain_ref.shape[0]
    gain_ref[...] = turned[0:count, 0:rows]
    bias_ref[...] = turned[count : 2 * count, 0:rows]


def settle_wide_kernel(part_0, part_1, expand_ref, contract_ref):
    total = add_all(part_0[...], [part_1[...]])
    span = expand_ref.shape[1]
    rows = expand_ref.shape[0]
    width = contract_ref.shape[1]
    expand_ref[...] = total[:, :span]
    for fold in range(contract_ref.shape[0] // rows):
        at = span + fold * width
        contract_ref[fold * rows : (fold + 1) * rows] = total[:, at : at + width]


def attend_pair(query, flags, key_aug, value_aug, segments):
    rows = query.shape[0]
    keys = key_aug.shape[1]
    lane = lane_numbers((rows, LANES))
    mixes = []
    kept = []
    for head in range(2):
        mine = (lane < HEAD_DIM) if head == 0 else (lane >= HEAD_DIM)
        slot = segments + (HEAD_DIM if head == 0 else 0)
        base = jnp.where(mine, query, flags)
        plain = base.astype(LOW)
        peak = jnp.full((rows, LANES), -jnp.inf, FULL)
        for start in range(0, keys, KEY_STEP):
            scores = dot(plain, key_aug[head, start : start + KEY_STEP], BY_LANES)
            for at in range(0, KEY_STEP, LANES):
                peak = jnp.maximum(peak, scores[:, at : at + LANES])
        peak = jnp.max(peak, axis=1, keepdims=True)
        shifted = with_parts(base, -peak, lane, slot).astype(LOW)
        total = jnp.zeros((rows, LANES), FULL)
        for start in range(0, keys, KEY_STEP):
            scores = dot(shifted, key_aug[head, start : start + KEY_STEP], BY_LANES)
            weights = jnp.exp(scores).astype(LOW)
            total = total + dot(weights, value_aug[head, start : start + KEY_STEP])
        weight_sum = total[:, HEAD_DIM : HEAD_DIM + 1] if head == 0 else total[:, 0:1]
        kept.append(with_parts(base, -(peak + jnp.log(weight_sum)), lane, slot).astype(LOW))
        mixes.append(total / weight_sum)
    return jnp.where(lane < HEAD_DIM, mixes[0], mixes[1]).astype(LOW), kept


def widen_pair(key, value, flags, key_aug, value_aug, start):
    rows = key.shape[0]
    lane = lane_numbers((rows, LANES))
    ones = jnp.ones((rows, LANES), LOW)
    for head in range(2):
        mine = (lane < HEAD_DIM) if head == 0 else (lane >= HEAD_DIM)
        key_aug[head, start : start + rows] = jnp.where(mine, key, flags)
        value_aug[head, start : start + rows] = jnp.where(mine, value, ones)


def pair_columns(first, pair):
    return pl.ds(pl.multiple_of(first + pair * LANES, LANES), LANES)


def self_forward_kernel(
    info, lengths, rows_0, rows_1, rows_2, rows_3, *refs
):
    quarters = refs[:8]
    mix_ref, query_ref, key_ref, value_ref, weight, flags_q, flags_k, key_aug, value_aug = refs[8:]
    pair = pl.program_id(0)
    home, place = info[0], info[1]
    local, width = rows_0.shape
    segments = lengths.shape[1] + 1

    @pl.when(pair == 0)
    def _():
        fill_weight(weight, quarters, home, (0, 1))
        flags_q[...] = query_flags(lengths, place * local, local)
        for step in range(4):
            flags_k[step * local : (step + 1) * local] = key_flags(
                lengths, (place ^ step) * local, local
            )

    both = jnp.concatenate(
        [weight[:, pair_columns(width, pair)], weight[:, pair_columns(2 * width, pair)]], axis=1
    )
    for step, rows in enumerate((rows_0, rows_1, rows_2, rows_3)):
        start = step * local
        made = dot(rows[...], both).astype(LOW)
        key, value = made[:, :LANES], made[:, LANES:]
        key_ref[start : start + local] = key
        value_ref[start : start + local] = value
        widen_pair(key, value, flags_k[start : start + local], key_aug, value_aug, start)
    query = dot(rows_0[...], weight[:, pair_columns(0, pair)]).astype(LOW).astype(FULL)
    mix, kept = attend_pair(query * score_scale, flags_q[...], key_aug, value_aug, segments)
    mix_ref[...] = mix
    query_ref[0] = kept[0]
    query_ref[1] = kept[1]


def cross_forward_kernel(
    info, target_lengths, source_lengths, mix, states, rows_0, rows_1, rows_2, rows_3, *refs
):
    quarters = refs[:8]
    (
        mix_ref,
        query_ref,
        key_ref,
        value_ref,
        unit_ref,
        scale_ref,
        norms_ref,
        out_weight,
        query_weight,
        pair_weight,
        norm_rows,
        queries,
        flags_q,
        flags_k,
        key_aug,
        value_aug,
    ) = refs[8:]
    pair = pl.program_id(0)
    home, place = info[0], info[1]
    local, width = rows_0.shape
    segments = target_lengths.shape[1] + 1

    @pl.when(pair == 0)
    def _():
        fill_weight(out_weight, quarters, home, (0, 1))
        fill_weight(query_weight, quarters, home, (width, 1))
        fill_weight(pair_weight, quarters, home, (2 * width, 1))
        fill_weight(norm_rows, quarters, home, (4 * width, 1))
        norms = norm_rows[...].astype(FULL).T[0:8]
        norms_ref[...] = norms
        mixed = states[...].astype(FULL) + dot(mix[...], out_weight[...])
        unit, scale = normalise(mixed)
        unit_ref[...] = unit
        scale_ref[...] = jnp.broadcast_to(scale, (local, LANES))
        first_low = (unit * norms[0:1] + norms[3:4]).astype(LOW)
        made = dot(first_low, query_weight[...]).astype(LOW)
        for at in range(queries.shape[0]):
            queries[at] = made[:, at * LANES : (at + 1) * LANES]
        flags_q[...] = query_flags(target_lengths, place * local, local)
        for step in range(4):
            flags_k[step * local : (step + 1) * local] = key_flags(
                source_lengths, (place ^ step) * local, local
            )

    both = jnp.concatenate(
        [pair_weight[:, pair_columns(0, pair)], pair_weight[:, pair_columns(width, pair)]], axis=1
    )
    for step, rows in enumerate((rows_0, rows_1, rows_2, rows_3)):
        start = step * local
        made = dot(rows[...], both).astype(LOW)
        key, value = made[:, :LANES], made[:, LANES:]
        key_ref[start : start + local] = key
        value_ref[start : start + local] = value
        widen_pair(key, value, flags_k[start : start + local], key_aug, value_aug, start)
    query = queries[pair].astype(FULL)
    mixed, kept = attend_pair(query * score_scale, flags_q[...], key_aug, value_aug, segments)
    mix_ref[...] = mixed
    query_ref[0] = kept[0]
    query_ref[1] = kept[1]


gelu_factor = 0.7978845608028654
gelu_cubic = 0.044715


def gelu_and_slope(hidden):
    square = hidden * hidden
    bend = jnp.tanh(gelu_factor * (hidden + gelu_cubic * (square * hidden)))
    half = 0.5 * (1.0 + bend)
    slope = half + (0.5 * hidden) * (1.0 - bend * bend) * (
        gelu_factor * (1.0 + (3.0 * gelu_cubic) * square)
    )
    return hidden * half, slope


def middle_kernel(info, mix, first_unit, norms, out_grad, *refs):
    quarters = refs[:8]
    (
        output_ref,
        cotangent_ref,
        unit_ref,
        scale_ref,
        norm_sums_ref,
        kept,
        sent,
        out_weight,
        expand,
        contract,
        active,
        slope,
        wide_grad,
        tall_grad,
    ) = refs[8:]
    home = info[0]
    width = mix.shape[1]
    chunks = active.shape[0]
    span = expand.shape[1] // chunks
    fill_weight(out_weight, quarters, home, (0, 1))
    fill_weight(expand, quarters, home, (width, 1))
    fill_weight(contract, quarters, home, (width + expand.shape[1], contract.shape[0] // width))
    first_norm = first_unit[...] * norms[0:1] + norms[3:4]
    second_unit, second_scale = normalise(first_norm + dot(mix[...], out_weight[...]))
    unit_ref[...] = second_unit
    scale_ref[...] = jnp.broadcast_to(second_scale, scale_ref.shape)
    second_norm = second_unit * norms[1:2] + norms[4:5]
    second_low = second_norm.astype(LOW)

    def forward(at, total):
        start = pl.multiple_of(at * span, span)
        hidden = dot(second_low, expand[:, pl.ds(start, span)])
        made, bent = gelu_and_slope(hidden)
        made = made.astype(LOW)
        active[at] = made
        slope[at] = bent
        return total + dot(made, contract[pl.ds(start, span)])

    mixed = lax.fori_loop(0, chunks, forward, second_norm)
    third_unit, third_scale = normalise(mixed)
    output_ref[...] = third_unit * norms[2:3] + norms[5:6]
    third_grad, gain_three, bias_three = norm_backward(
        out_grad[...], third_unit, third_scale, norms[2:3]
    )
    ffn_grad = third_grad.astype(LOW)
    second_turned = second_low.T

    def backward(at, total):
        start = pl.multiple_of(at * span, span)
        part = contract[pl.ds(start, span)]
        hidden_grad = (dot(ffn_grad, part, BY_LANES) * slope[at]).astype(LOW)
        tall_grad[pl.ds(start, span)] = dot(active[at].T, ffn_grad).astype(LOW)
        wide_grad[:, pl.ds(start, span)] = dot(second_turned, hidden_grad).astype(LOW)
        return total + dot(hidden_grad, expand[:, pl.ds(start, span)], BY_LANES)

    cotangent_ref[...] = lax.fori_loop(0, chunks, backward, third_grad)
    norm_sums_ref[...] = jnp.zeros(norm_sums_ref.shape, FULL)
    norm_sums_ref[2:3] = gain_three
    norm_sums_ref[5:6] = bias_three
    pack_grad(wide_grad, kept, sent, home, (0, 1))
    pack_grad(tall_grad, kept, sent, home, (expand.shape[1], tall_grad.shape[0] // width))


def second_back_kernel(
    cotangent,
    second_unit,
    second_scale,
    norms,
    sums,
    mix,
    out_weight,
    second_grad_ref,
    mix_grad_ref,
    out_weight_grad,
    norm_sums_ref,
):
    second_grad, gain_two, bias_two = norm_backward(
        cotangent[...], second_unit[...], second_scale[:, 0:1], norms[1:2]
    )
    second_grad_ref[...] = second_grad
    cross_out_low = second_grad.astype(LOW)
    mix_grad_ref[...] = dot(cross_out_low, out_weight[...], BY_LANES).astype(LOW)
    out_weight_grad[...] = dot(mix[...].T, cross_out_low).astype(LOW)
    norm_sums_ref[...] = sums[...]
    norm_sums_ref[1:2] = gain_two
    norm_sums_ref[4:5] = bias_two


def attend_back_pair(queries, key, value, flags, mix, grad, segments, key_aug, value_aug, made):
    rows = grad.shape[0]
    keys = key.shape[0]
    lane = lane_numbers((rows, LANES))
    widen_pair(key, value, flags, key_aug, value_aug, 0)
    grad = grad.astype(FULL)
    product = grad * mix.astype(FULL)
    grads = []
    totals = []
    for head in range(2):
        mine = (lane < HEAD_DIM) if head == 0 else (lane >= HEAD_DIM)
        slot = segments + (HEAD_DIM if head == 0 else 0)
        inner = jnp.sum(jnp.where(mine, product, 0.0), axis=1, keepdims=True)
        grads.append(with_parts(jnp.where(mine, grad, 0.0), -inner, lane, slot).astype(LOW))
        totals.append(jnp.zeros((HEAD_DIM, rows), FULL))
    turned = key.T
    lane = lane_numbers((KEY_STEP, LANES))
    for start in range(0, keys, KEY_STEP):
        span = slice(start, start + KEY_STEP)
        key_parts = []
        value_parts = []
        for head in range(2):
            probs = jnp.exp(dot(key_aug[head, span], queries[head], BY_LANES))
            shifted = dot(value_aug[head, span], grads[head], BY_LANES)
            score_grad = (probs * shifted).astype(LOW)
            value_parts.append(dot(probs.astype(LOW), grads[head]))
            key_parts.append(dot(score_grad, queries[head]))
            part = turned[head * HEAD_DIM : (head + 1) * HEAD_DIM, span]
            totals[head] = totals[head] + dot(part, score_grad)
        made[span, :LANES] = jnp.where(lane < HEAD_DIM, key_parts[0], key_parts[1]).astype(LOW)
        made[span, LANES:] = jnp.where(lane < HEAD_DIM, value_parts[0], value_parts[1]).astype(LOW)
    return (jnp.concatenate(totals, axis=0).T * score_scale).astype(LOW)


def cross_backward_kernel(
    info, source_lengths, queries, key, value, mix, grad, rows_0, rows_1, rows_2, rows_3, *refs
):
    quarters = refs[:8]
    (
        query_grad_ref,
        weight_grad_ref,
        own_ref,
        parts_ref,
        weight,
        flags_k,
        key_aug,
        value_aug,
        made,
    ) = refs[8:]
    pair = pl.program_id(0)
    home, place = info[0], info[1]
    local, width = rows_0.shape
    pairs = made.shape[0]
    segments = source_lengths.shape[1] + 1

    @pl.when(pair == 0)
    def _():
        fill_weight(weight, quarters, home, (2 * width, 1))
        for step in range(4):
            flags_k[step * local : (step + 1) * local] = key_flags(
                source_lengths, (place ^ step) * local, local
            )

    query_grad_ref[...] = attend_back_pair(
        queries, key[...], value[...], flags_k[...], mix[...], grad[...], segments, key_aug, value_aug, made.at[pair]
    )

    @pl.when(pair == pairs - 1)
    def _():
        finish_rows(made, weight, 0, (rows_0, rows_1, rows_2, rows_3), own_ref, parts_ref, weight_grad_ref, 0)


def finish_rows(made, weight, first, row_refs, own_ref, parts_ref, weight_grad_ref, grad_first):
    local, width = row_refs[0].shape
    pairs = made.shape[0]
    turned = [rows[...].T for rows in row_refs]
    for step in range(4):
        total = None
        for pair in range(pairs):
            at = first + pair * LANES
            columns = jnp.concatenate(
                [weight[:, at : at + LANES], weight[:, width + at : width + at + LANES]], axis=1
            )
            term = dot(made[pair, step * local : (step + 1) * local], columns, BY_LANES)
            total = term if total is None else total + term
        if step == 0:
            own_ref[...] = total
        else:
            parts_ref[step - 1] = total.astype(LOW)
    for pair in range(pairs):
        total = None
        for step in range(4):
            term = dot(turned[step], made[pair, step * local : (step + 1) * local])
            total = term if total is None else total + term
        at = grad_first + pair * LANES
        weight_grad_ref[:, at : at + LANES] = total[:, :LANES].astype(LOW)
        weight_grad_ref[:, width + at : width + at + LANES] = total[:, LANES:].astype(LOW)


def between_kernel(
    info, query_grad, second_grad, first_unit, first_scale, norms, norm_sums, self_mix, pair_grad, cross_out_grad, *refs
):
    quarters = refs[:8]
    (
        first_grad_ref,
        mix_grad_ref,
        kept,
        sent,
        out_weight,
        query_weight,
        out_grad,
        query_weight_grad,
        norm_grad,
        norm_rows,
    ) = refs[8:]
    home = info[0]
    width = self_mix.shape[1]
    fill_weight(out_weight, quarters, home, (0, 1))
    fill_weight(query_weight, quarters, home, (width, 1))
    unit = first_unit[...]
    first_low = (unit * norms[0:1] + norms[3:4]).astype(LOW)
    low_grad = query_grad[...]
    query_weight_grad[...] = dot(first_low.T, low_grad).astype(LOW)
    cotangent = second_grad[...] + dot(low_grad, query_weight[...], BY_LANES)
    first_grad, gain_one, bias_one = norm_backward(
        cotangent, unit, first_scale[:, 0:1], norms[0:1]
    )
    first_grad_ref[...] = first_grad
    self_out_low = first_grad.astype(LOW)
    out_grad[...] = dot(self_mix[...].T, self_out_low).astype(LOW)
    mix_grad_ref[...] = dot(self_out_low, out_weight[...], BY_LANES).astype(LOW)
    norm_rows[...] = jnp.zeros(norm_rows.shape, FULL)
    norm_rows[0:8] = norm_sums[...]
    norm_rows[0:1] = gain_one
    norm_rows[3:4] = bias_one
    norm_grad[...] = norm_rows[...].T.astype(LOW)
    pack_grad(out_grad, kept, sent, home, (0, 1))
    pack_grad(query_weight_grad, kept, sent, home, (width, 1))
    pack_grad(pair_grad, kept, sent, home, (2 * width, 1))
    pack_grad(cross_out_grad, kept, sent, home, (4 * width, 1))
    pack_grad(norm_grad, kept, sent, home, (5 * width, 1))


def self_backward_kernel(
    info, lengths, queries, key, value, mix, grad, first_grad, rows_0, rows_1, rows_2, rows_3, *refs
):
    quarters = refs[:8]
    (
        own_ref,
        parts_ref,
        kept,
        sent,
        weight,
        flags_k,
        key_aug,
        value_aug,
        made,
        query_grads,
        weight_grad,
    ) = refs[8:]
    pair = pl.program_id(0)
    home, place = info[0], info[1]
    local, width = rows_0.shape
    pairs = made.shape[0]
    segments = lengths.shape[1] + 1

    @pl.when(pair == 0)
    def _():
        fill_weight(weight, quarters, home, (0, 1))
        for step in range(4):
            flags_k[step * local : (step + 1) * local] = key_flags(
                lengths, (place ^ step) * local, local
            )

    query_grads[pair] = attend_back_pair(
        queries, key[...], value[...], flags_k[...], mix[...], grad[...], segments, key_aug, value_aug, made.at[pair]
    )

    @pl.when(pair == pairs - 1)
    def _():
        finish_rows(
            made, weight, width, (rows_0, rows_1, rows_2, rows_3), own_ref, parts_ref, weight_grad, width
        )
        low_grad = jnp.concatenate([query_grads[at] for at in range(pairs)], axis=1)
        weight_grad[:, 0:width] = dot(rows_0[...].T, low_grad).astype(LOW)
        own_ref[...] += first_grad[...] + dot(low_grad, weight[:, 0:width], BY_LANES)
        pack_grad(weight_grad, kept, sent, home, (0, 1))


def whole(shape):
    return pl.BlockSpec(shape, lambda *at: (0,) * len(shape))


def call(kernel, inputs, specs, outputs, out_specs, scratch, grid=(), micros=1, mib=58):
    moved = sum(math.prod(a.shape) * a.dtype.itemsize for a in list(inputs) + list(outputs))
    return pl.pallas_call(
        kernel,
        out_shape=outputs,
        grid=grid,
        in_specs=specs,
        out_specs=out_specs,
        scratch_shapes=scratch,
        compiler_params=pltpu.CompilerParams(vmem_limit_bytes=mib * 2**20),
        cost_estimate=pl.CostEstimate(flops=micros * 10**9, bytes_accessed=moved, transcendentals=0),
    )(*inputs)


SCALARS = pl.BlockSpec(memory_space=pltpu.SMEM)


def shaped(shape, kind):
    return jax.ShapeDtypeStruct(shape, kind)


def per_device(
    target_states,
    memory,
    target_lengths,
    source_lengths,
    self_project,
    self_output,
    cross_project,
    memory_project,
    cross_output,
    expand_weight,
    contract_weight,
    norm_gain,
    norm_bias,
    out_grad,
):
    _, local, width = target_states.shape
    states = target_states[0]
    own_memory = memory[0]
    rows = self_project.shape[0]
    ff = expand_weight.shape[1]
    keys = local * 4
    pairs = width // LANES
    info = jnp.stack([home_number(), lax.axis_index("narrow")]).astype(jnp.int32)

    batches = 3 * width, 4 * width + LANES, width + 2 * ff
    if staged():
        shards = (
            self_project,
            self_output,
            cross_project,
            memory_project,
            cross_output,
            expand_weight,
            contract_weight,
            norm_gain,
            norm_bias,
        )
        first_batches, batch_3 = call(
            pack_kernel,
            list(shards),
            [whole(shard.shape) for shard in shards],
            [shaped((rows, batches[0] + batches[1]), LOW), shaped((rows, batches[2]), LOW)],
            [whole((rows, batches[0] + batches[1])), whole((rows, batches[2]))],
            [pltpu.VMEM((LANES, LANES), FULL)],
        )
        far_12 = gather_far(first_batches)
        states_x = exchange(states, 2)
        far_1 = jnp.stack([held[:, : batches[0]] for held in far_12])
        (states_x, batch_3), far_1 = after((states_x, batch_3), far_1)
        plane_1 = gather_plane(far_1)
        near_3 = exchange(batch_3, FAR[0])
        half_3 = jnp.stack([batch_3, near_3])
        rest_3 = exchange(half_3, FAR[1])
        states_c = exchange(states, 1)
        memory_c = exchange(own_memory, 1)
        (own_memory, far_12), plane_1 = after((own_memory, far_12), plane_1)
        far_2 = jnp.stack([held[:, batches[0] :] for held in far_12])
    else:
        norm_shard = jnp.concatenate([norm_gain, norm_bias], axis=0).T
        norm_shard = jnp.pad(norm_shard, ((0, 0), (0, LANES - norm_shard.shape[1])))
        folded = fold_rows(contract_weight, rows)
        plane_1 = self_project
        far_2 = jnp.concatenate([self_output, cross_project, memory_project, norm_shard], axis=1)
        far_3 = jnp.concatenate([cross_output, expand_weight, folded], axis=1)
        states_x = exchange(states, 2)
        states_c = exchange(states, 1)
        memory_c = exchange(own_memory, 1)
    states_xc = exchange(states_x, 1)
    (own_memory, far_2), plane_1 = after((own_memory, far_2), plane_1)
    weights_1 = gather_core(plane_1)
    row_states = [states, states_c, states_x, states_xc]
    plane_2 = gather_plane(far_2)
    memory_x = exchange(own_memory, 2)

    row_spec = whole((local, width))
    pair_rows = pl.BlockSpec((local, LANES), lambda pair: (0, pair))
    pair_keys = pl.BlockSpec((keys, LANES), lambda pair: (0, pair))
    pair_heads = pl.BlockSpec((2, local, LANES), lambda pair: (pair, 0, 0))
    quarter_specs_1 = [whole(q.shape) for q in weights_1]
    attend_scratch = [
        pltpu.VMEM((local, LANES), FULL),
        pltpu.VMEM((keys, LANES), LOW),
        pltpu.VMEM((2, keys, LANES), LOW),
        pltpu.VMEM((2, keys, LANES), LOW),
    ]
    self_mix, self_queries, self_key, self_value = call(
        self_forward_kernel,
        [info, target_lengths, *row_states, *weights_1],
        [SCALARS, SCALARS] + [row_spec] * 4 + quarter_specs_1,
        [
            shaped((local, width), LOW),
            shaped((2 * pairs, local, LANES), LOW),
            pltpu.HBM((keys, width), LOW),
            pltpu.HBM((keys, width), LOW),
        ],
        [pair_rows, pair_heads, pair_keys, pair_keys],
        [pltpu.VMEM((width, 3 * width), LOW)] + attend_scratch,
        grid=(pairs,),
        micros=25, mib=20,
    )

    if staged():
        (memory_x, memory_c, rest_3), self_mix = after((memory_x, memory_c, rest_3), self_mix)
        far_3 = jnp.concatenate([half_3, rest_3])
    plane_2, self_mix = after(plane_2, self_mix)
    memory_xc = exchange(memory_x, 1)
    weights_2 = gather_core(plane_2)
    row_memory = [own_memory, memory_c, memory_x, memory_xc]
    plane_3 = gather_plane(far_3)
    quarter_specs_2 = [whole(q.shape) for q in weights_2]
    cross_mix, cross_queries, cross_key, cross_value, first_unit, first_scale, norms = call(
        cross_forward_kernel,
        [info, target_lengths, source_lengths, self_mix, states, *row_memory, *weights_2],
        [SCALARS] * 3 + [row_spec] * 6 + quarter_specs_2,
        [
            shaped((local, width), LOW),
            shaped((2 * pairs, local, LANES), LOW),
            pltpu.HBM((keys, width), LOW),
            pltpu.HBM((keys, width), LOW),
            shaped((local, width), FULL),
            shaped((local, LANES), FULL),
            shaped((8, width), FULL),
        ],
        [
            pair_rows,
            pair_heads,
            pair_keys,
            pair_keys,
            row_spec,
            whole((local, LANES)),
            whole((8, width)),
        ],
        [
            pltpu.VMEM((width, width), LOW),
            pltpu.VMEM((width, width), LOW),
            pltpu.VMEM((width, 2 * width), LOW),
            pltpu.VMEM((width, LANES), LOW),
            pltpu.VMEM((pairs, local, LANES), LOW),
        ]
        + attend_scratch,
        grid=(pairs,),
        micros=25, mib=20,
    )

    plane_3, cross_mix = after(plane_3, cross_mix)
    weights_3 = gather_core(plane_3, ff // width)
    quarter_specs_3 = [whole(q.shape) for q in weights_3]
    chunk_count = ff // width
    packed_3 = (4, 4, TILE_ROWS, 2 * ff)
    wide_scale = whole((local, LANES))
    norm_spec = whole((8, width))
    square = whole((width, width))
    output, cotangent, second_unit, second_scale, norm_sums, kept_3, sent_3, cross_out_weight = call(
        middle_kernel,
        [info, cross_mix, first_unit, norms, out_grad[0], *weights_3],
        [SCALARS, row_spec, row_spec, norm_spec, row_spec] + quarter_specs_3,
        [
            shaped((local, width), FULL),
            shaped((local, width), FULL),
            shaped((local, width), FULL),
            shaped((local, LANES), FULL),
            shaped((8, width), FULL),
            shaped(packed_3, LOW),
            shaped(packed_3, LOW),
            shaped((width, width), LOW),
        ],
        [row_spec, row_spec, row_spec, wide_scale, norm_spec, whole(packed_3), whole(packed_3), square],
        [
            pltpu.VMEM((width, ff), LOW),
            pltpu.VMEM((ff, width), LOW),
            pltpu.VMEM((chunk_count, local, width), LOW),
            pltpu.VMEM((chunk_count, local, width), FULL),
            pltpu.VMEM((width, ff), LOW),
            pltpu.VMEM((ff, width), LOW),
        ],
        micros=17, mib=36,
    )
    other_3 = exchange_core(sent_3)
    second_grad, cross_mix_grad, cross_out_grad, norm_sums = call(
        second_back_kernel,
        [cotangent, second_unit, second_scale, norms, norm_sums, cross_mix, cross_out_weight],
        [row_spec, row_spec, wide_scale, norm_spec, norm_spec, row_spec, square],
        [
            shaped((local, width), FULL),
            shaped((local, width), LOW),
            shaped((width, width), LOW),
            shaped((8, width), FULL),
        ],
        [row_spec, row_spec, square, norm_spec],
        [],
        micros=4, mib=8,
    )
    other_3, cross_mix_grad = after(other_3, cross_mix_grad)
    core_3 = reduce_core(kept_3, other_3)
    core_3, cross_mix_grad = after(core_3, cross_mix_grad)
    planes_3 = exchange_plane(core_3)

    back_scratch = [
        pltpu.VMEM((keys, LANES), LOW),
        pltpu.VMEM((2, keys, LANES), LOW),
        pltpu.VMEM((2, keys, LANES), LOW),
        pltpu.VMEM((pairs, keys, 2 * LANES), LOW),
    ]
    parts_shape = (3, local, width)
    cross_query_grad, pair_weight_grad, memory_own, memory_parts = call(
        cross_backward_kernel,
        [
            info,
            source_lengths,
            cross_queries,
            cross_key,
            cross_value,
            cross_mix,
            cross_mix_grad,
            *row_memory,
            *weights_2,
        ],
        [SCALARS] * 2
        + [pair_heads, pair_keys, pair_keys, pair_rows, pair_rows]
        + [row_spec] * 4
        + quarter_specs_2,
        [
            shaped((local, width), LOW),
            shaped((width, 2 * width), LOW),
            shaped((local, width), FULL),
            shaped(parts_shape, LOW),
        ],
        [pair_rows, whole((width, 2 * width)), row_spec, whole(parts_shape)],
        [pltpu.VMEM((width, 2 * width), LOW)] + back_scratch,
        grid=(pairs,),
        micros=33, mib=28,
    )
    (planes_3, memory_parts), cross_query_grad = after((planes_3, memory_parts), cross_query_grad)
    plane_sum_3 = reduce_plane(planes_3)
    memory_sent = exchange_row(memory_parts)
    plane_sum_3, cross_query_grad = after(plane_sum_3, cross_query_grad)
    half_sum_3 = exchange_half(plane_sum_3)

    packed_2 = (4, 4, TILE_ROWS, 5 * width + LANES)
    first_grad, self_mix_grad, kept_2, sent_2 = call(
        between_kernel,
        [
            info,
            cross_query_grad,
            second_grad,
            first_unit,
            first_scale,
            norms,
            norm_sums,
            self_mix,
            pair_weight_grad,
            cross_out_grad,
            *weights_2,
        ],
        [SCALARS, row_spec, row_spec, row_spec, whole((local, LANES))]
        + [whole((8, width))] * 2
        + [row_spec, whole((width, 2 * width)), whole((width, width))]
        + quarter_specs_2,
        [
            shaped((local, width), FULL),
            shaped((local, width), LOW),
            shaped(packed_2, LOW),
            shaped(packed_2, LOW),
        ],
        [row_spec, row_spec, whole(packed_2), whole(packed_2)],
        [
            pltpu.VMEM((width, width), LOW),
            pltpu.VMEM((width, width), LOW),
            pltpu.VMEM((width, width), LOW),
            pltpu.VMEM((width, width), LOW),
            pltpu.VMEM((width, LANES), LOW),
            pltpu.VMEM((LANES, width), FULL),
        ],
        micros=6, mib=14,
    )
    other_2 = exchange_core(sent_2)
    core_2 = reduce_core(kept_2, other_2)
    memory_other = reduce_row_core(memory_parts, memory_sent)
    (core_2, memory_other), self_mix_grad = after((core_2, memory_other), self_mix_grad)
    planes_2 = exchange_plane(core_2)
    memory_far = exchange(memory_other, 2)

    packed_1 = (4, 4, TILE_ROWS, 3 * width)
    states_own, states_parts, kept_1, sent_1 = call(
        self_backward_kernel,
        [
            info,
            target_lengths,
            self_queries,
            self_key,
            self_value,
            self_mix,
            self_mix_grad,
            first_grad,
            *row_states,
            *weights_1,
        ],
        [SCALARS] * 2
        + [pair_heads, pair_keys, pair_keys, pair_rows, pair_rows]
        + [row_spec] * 5
        + quarter_specs_1,
        [
            shaped((local, width), FULL),
            shaped(parts_shape, LOW),
            shaped(packed_1, LOW),
            shaped(packed_1, LOW),
        ],
        [row_spec, whole(parts_shape), whole(packed_1), whole(packed_1)],
        [pltpu.VMEM((width, 3 * width), LOW)]
        + back_scratch
        + [pltpu.VMEM((pairs, local, LANES), LOW), pltpu.VMEM((width, 3 * width), LOW)],
        grid=(pairs,),
        micros=33, mib=28,
    )
    (planes_2, memory_far, half_sum_3), (sent_1, kept_1, states_parts, states_own) = after(
        (planes_2, memory_far, half_sum_3), (sent_1, kept_1, states_parts, states_own)
    )
    other_1 = exchange_core(sent_1)
    states_sent = exchange_row(states_parts)
    core_1 = reduce_core(kept_1, other_1)
    planes_1 = exchange_plane(core_1)
    (planes_2, memory_far, half_sum_3, states_sent), core_1 = after(
        (planes_2, memory_far, half_sum_3, states_sent), core_1
    )
    total_3 = reduce_half(plane_sum_3, half_sum_3)
    fars_3 = exchange_near(total_3)
    plane_sum_2 = reduce_plane(planes_2)
    half_sum_2 = exchange_half(plane_sum_2)
    states_other = reduce_row_core(states_parts, states_sent)
    states_far = exchange(states_other, 2)
    memory_grad = reduce_row(memory_own, memory_sent, memory_far)
    plane_sum_1 = reduce_plane(planes_1)
    fars_1 = exchange_far(plane_sum_1)
    total_2 = reduce_half(plane_sum_2, half_sum_2)
    fars_2 = exchange_near(total_2)
    states_grad = reduce_row(states_own, states_sent, states_far)
    count = norm_gain.shape[0]
    if staged():
        expand_grad, contract_grad = call(
            settle_wide_kernel,
            list(fars_3),
            [whole((rows, 2 * ff))] * len(fars_3),
            [shaped((rows, ff), FULL), shaped((rows * ff // width, width), FULL)],
            [whole((rows, ff)), whole((rows * ff // width, width))],
            [],
        )
        settled = [
            shaped((rows, 3 * width), FULL),
            shaped((rows, width), FULL),
            shaped((rows, width), FULL),
            shaped((rows, 2 * width), FULL),
            shaped((rows, width), FULL),
            shaped(norm_gain.shape, FULL),
            shaped(norm_gain.shape, FULL),
        ]
        project, out, cross, pairs_grad, cross_out, gain, bias = call(
            settle_kernel,
            list(fars_1) + list(fars_2),
            [whole((rows, 3 * width))] * 4 + [whole((rows, 5 * width + LANES))] * 2,
            settled,
            [whole(each.shape) for each in settled],
            [pltpu.VMEM((LANES, LANES), FULL)],
        )
    else:
        grad_3 = reduce_far(fars_3, ff // width)
        grad_2 = reduce_far(fars_2)
        project = reduce_far(fars_1)
        expand_grad, contract_grad = grad_3[:, :ff], unfold_rows(grad_3[:, ff:], width)
        out, cross = grad_2[:, :width], grad_2[:, width : 2 * width]
        pairs_grad, cross_out = grad_2[:, 2 * width : 4 * width], grad_2[:, 4 * width : 5 * width]
        norm_grads = grad_2[:, 5 * width :].T
        gain, bias = norm_grads[:count], norm_grads[count : 2 * count]
    return (
        output[None],
        states_grad[None],
        memory_grad[None],
        project,
        out,
        cross,
        pairs_grad,
        cross_out,
        expand_grad,
        contract_grad,
        gain,
        bias,
    )


def exchange_row(parts):
    return exchange(parts[0], 1), exchange(parts[2], 1)


def reduce_row_core(parts, sent):
    return add_all(parts[1], [sent[1]]).astype(LOW)


def reduce_row(own, sent, far):
    return add_all(own, [sent[0], far])


def solution(mesh):
    in_specs = (
        P("wide", "narrow", None),
        P("wide", "narrow", None),
        P("wide", None),
        P("wide", None),
        P(("wide", "narrow"), None),
        P(("wide", "narrow"), None),
        P(("wide", "narrow"), None),
        P(("wide", "narrow"), None),
        P(("wide", "narrow"), None),
        P(("wide", "narrow"), None),
        P(("wide", "narrow"), None),
        P(None, ("wide", "narrow")),
        P(None, ("wide", "narrow")),
        P("wide", "narrow", None),
    )
    out_specs = (
        P("wide", "narrow", None),
        P("wide", "narrow", None),
        P("wide", "narrow", None),
        P(("wide", "narrow"), None),
        P(("wide", "narrow"), None),
        P(("wide", "narrow"), None),
        P(("wide", "narrow"), None),
        P(("wide", "narrow"), None),
        P(("wide", "narrow"), None),
        P(("wide", "narrow"), None),
        P(None, ("wide", "narrow")),
        P(None, ("wide", "narrow")),
    )
    return jax.shard_map(
        per_device, mesh=mesh, in_specs=in_specs, out_specs=out_specs, check_vma=False
    )
```

```python
import functools
import math

import jax
import jax.numpy as jnp
from jax import lax
from jax.experimental import pallas as pl
from jax.experimental.pallas import tpu as pltpu
from jax.sharding import PartitionSpec as P

HEAD_DIM = 64
LANES = 128
TILE_ROWS = 16
BLOCKS = 32
AXES = ("wide", "narrow")
LOW = jnp.bfloat16
FULL = jnp.float32

ln_eps = 1e-05
score_scale = HEAD_DIM ** (-0.5)
mask_step = -(2.0**30)

BY_LANES = (((1,), (1,)), ((), ()))
PLAIN = (((1,), (0,)), ((), ()))


def dot(left, right, dims=PLAIN):
    return lax.dot_general(left, right, dims, preferred_element_type=FULL)


def exchange(block, mask):
    device_count = lax.axis_size("wide") * lax.axis_size("narrow")
    pairs = [(device, device ^ mask) for device in range(device_count)]
    return lax.ppermute(block, AXES, pairs)


def device_number():
    return lax.axis_index("wide") * lax.axis_size("narrow") + lax.axis_index("narrow")


def staged():
    return lax.axis_size("wide") * lax.axis_size("narrow") == BLOCKS


FAR = (8, 16, 24)
PLANE = (2, 4, 6)


def gather_far(shard):
    if not staged():
        return shard
    return [shard] + [exchange(shard, mask) for mask in FAR]


def gather_plane(held):
    if not staged():
        return held
    return [held] + [exchange(held, mask) for mask in PLANE]


def gather_core(held, folds=0):
    if staged():
        return held + [exchange(quarter, 1) for quarter in held]
    whole = lax.all_gather(held, AXES, axis=0, tiled=True)
    if folds:
        rows, columns = held.shape
        split = columns - folds * whole.shape[0]
        tall = unfold_rows(held[:, split:], whole.shape[0])
        tall = lax.all_gather(tall, AXES, axis=0, tiled=True)
        tall = tall.reshape(BLOCKS, folds, TILE_ROWS, -1).transpose(0, 2, 1, 3)
        whole = jnp.concatenate([whole[:, :split], tall.reshape(whole.shape[0], -1)], axis=1)
    whole = whole.reshape(4, 4, 2, TILE_ROWS, held.shape[1]).transpose(2, 1, 0, 3, 4)
    return [whole[core, plane] for core in range(2) for plane in range(4)]


def home_number():
    return device_number() if staged() else jnp.zeros((), jnp.int32)


def block_number(home, core, plane, far):
    return home ^ (far * 8 + plane * 2 + core)


def add_all(first, others):
    total = first.astype(FULL)
    for other in others:
        total = total + other.astype(FULL)
    return total


def exchange_core(sent):
    return exchange(sent, 1) if staged() else sent


def reduce_core(kept, other):
    return add_all(kept, [other]).astype(LOW) if staged() else (kept, other)


def exchange_plane(held):
    if not staged():
        return held
    return [held[0]] + [exchange(held[plane + 1], mask) for plane, mask in enumerate(PLANE)]


def reduce_plane(planes):
    return add_all(planes[0], planes[1:]).astype(LOW) if staged() else planes


def exchange_far(held):
    if not staged():
        return held
    return [held[0]] + [exchange(held[far + 1], mask) for far, mask in enumerate(FAR)]


def exchange_half(held):
    return exchange(held[2:], FAR[1]) if staged() else held


def reduce_half(held, other):
    return add_all(held[:2], [other]).astype(LOW) if staged() else held


def exchange_near(held):
    return [held[0], exchange(held[1], FAR[0])] if staged() else held


def reduce_far(held, folds=0):
    if staged():
        return add_all(held[0], held[1:])
    whole = jnp.stack(held).transpose(2, 1, 0, 3, 4)
    whole = whole.reshape(BLOCKS * TILE_ROWS, -1).astype(FULL)
    if folds:
        split = whole.shape[1] - folds * whole.shape[0]
        tall = whole[:, split:].reshape(BLOCKS, TILE_ROWS, folds, -1).transpose(0, 2, 1, 3)
        tall = tall.reshape(folds * whole.shape[0], -1)
        tall = lax.psum_scatter(tall, AXES, scatter_dimension=0, tiled=True)
        whole = lax.psum_scatter(whole[:, :split], AXES, scatter_dimension=0, tiled=True)
        return jnp.concatenate([whole, fold_rows(tall, whole.shape[0])], axis=1)
    return lax.psum_scatter(whole, AXES, scatter_dimension=0, tiled=True)


def after(values, token):
    return lax.optimization_barrier((values, token))


def fold_rows(block, rows):
    return jnp.concatenate(
        [block[at : at + rows] for at in range(0, block.shape[0], rows)], axis=1
    )


def unfold_rows(block, width):
    return jnp.concatenate(
        [block[:, at : at + width] for at in range(0, block.shape[1], width)], axis=0
    )


def lane_numbers(shape):
    return lax.broadcasted_iota(jnp.int32, shape, 1)


def segment_bounds(lengths_ref):
    lane = lane_numbers((1, LANES))
    first = jnp.full((1, LANES), 2**30, jnp.int32)
    last = jnp.zeros((1, LANES), jnp.int32)
    start = jnp.int32(0)
    count = lengths_ref.shape[1]
    for segment in range(count + 1):
        end = start + lengths_ref[0, segment] if segment < count else jnp.int32(2**30)
        first = jnp.where(lane == segment, start, first)
        last = jnp.where(lane == segment, end, last)
        start = end
    return first, last


def segment_flags(start, rows, bounds):
    position = start + lax.broadcasted_iota(jnp.int32, (rows, LANES), 0)
    return (position >= bounds[0]) & (position < bounds[1])


def three_parts(value):
    first = value.astype(LOW)
    rest = value - first.astype(FULL)
    second = rest.astype(LOW)
    third = (rest - second.astype(FULL)).astype(LOW)
    return first.astype(FULL), second.astype(FULL), third.astype(FULL)


def query_flags(lengths_ref, start, rows):
    segments = lengths_ref.shape[1] + 1
    own = segment_flags(start, rows, segment_bounds(lengths_ref))
    return jnp.where(own | (lane_numbers((rows, LANES)) >= segments), 0.0, mask_step).astype(LOW)


def key_flags(lengths_ref, start, rows):
    own = segment_flags(start, rows, segment_bounds(lengths_ref))
    return jnp.where(own, 1.0, 0.0).astype(LOW)


def fill_weight(target, quarters, home, columns):
    first, folds = columns
    width = target.shape[1]
    for core in range(2):
        for plane in range(4):
            for far in range(4):
                block = block_number(home, core, plane, far)
                piece = quarters[core * 4 + plane]
                for fold in range(folds):
                    row = pl.multiple_of(block * (TILE_ROWS * folds) + fold * TILE_ROWS, TILE_ROWS)
                    start = first + fold * width
                    target[pl.ds(row, TILE_ROWS), :] = piece[far, :, start : start + width]


def pack_grad(source, kept, sent, home, columns):
    first, folds = columns
    width = source.shape[1]
    for core, target in ((0, kept), (1, sent)):
        for plane in range(4):
            for far in range(4):
                block = block_number(home, core, plane, far)
                for fold in range(folds):
                    row = pl.multiple_of(block * (TILE_ROWS * folds) + fold * TILE_ROWS, TILE_ROWS)
                    start = first + fold * width
                    target[plane, far, :, start : start + width] = source[pl.ds(row, TILE_ROWS), :]


def normalise(states):
    centred = states - jnp.mean(states, axis=1, keepdims=True)
    spread = jnp.mean(centred * centred, axis=1, keepdims=True)
    scale = lax.rsqrt(spread + ln_eps)
    return centred * scale, scale


def norm_backward(cotangent, unit, scale, gain):
    scaled = cotangent * gain
    grad = scale * (
        scaled
        - jnp.mean(scaled, axis=1, keepdims=True)
        - unit * jnp.mean(scaled * unit, axis=1, keepdims=True)
    )
    return (
        grad,
        jnp.sum(cotangent * unit, axis=0, keepdims=True),
        jnp.sum(cotangent, axis=0, keepdims=True),
    )


KEY_STEP = 256


def pack_kernel(*refs):
    ins, (packed, square) = refs[:8], refs[8:]
    self_output, cross_project, memory_project, cross_output, expand, contract, gain, bias = ins
    rows, width = self_output.shape
    at = 0
    for part in (self_output, cross_project, memory_project):
        packed[:, at : at + part.shape[1]] = part[...]
        at += part.shape[1]
    count = gain.shape[0]
    square[...] = jnp.zeros(square.shape, FULL)
    square[0:count, 0:rows] = gain[...].astype(FULL)
    square[count : 2 * count, 0:rows] = bias[...].astype(FULL)
    packed[:, at : at + LANES] = square[...].T[0:rows].astype(LOW)
    at += LANES
    for part in (cross_output, expand):
        packed[:, at : at + part.shape[1]] = part[...]
        at += part.shape[1]
    for fold in range(contract.shape[0] // rows):
        packed[:, at : at + width] = contract[fold * rows : (fold + 1) * rows]
        at += width


def settle_kernel(first_0, first_1, first_2, first_3, second_0, second_1, *refs):
    project_ref, output_ref, cross_ref, memory_ref, cross_out_ref, gain_ref, bias_ref, square = refs
    rows, width = output_ref.shape

    def total(parts, start, span):
        return add_all(parts[0][:, start : start + span], [p[:, start : start + span] for p in parts[1:]])

    project_ref[...] = total((first_0, first_1, first_2, first_3), 0, project_ref.shape[1])
    seconds = (second_0, second_1)
    at = 0
    for ref in (output_ref, cross_ref, memory_ref, cross_out_ref):
        ref[...] = total(seconds, at, ref.shape[1])
        at += ref.shape[1]
    square[...] = jnp.zeros(square.shape, FULL)
    square[0:rows] = total(seconds, at, LANES)
    turned = square[...].T
    count = gain_ref.shape[0]
    gain_ref[...] = turned[0:count, 0:rows]
    bias_ref[...] = turned[count : 2 * count, 0:rows]


def settle_wide_kernel(part_0, part_1, expand_ref, contract_ref):
    total = add_all(part_0[...], [part_1[...]])
    span = expand_ref.shape[1]
    rows = expand_ref.shape[0]
    width = contract_ref.shape[1]
    expand_ref[...] = total[:, :span]
    for fold in range(contract_ref.shape[0] // rows):
        at = span + fold * width
        contract_ref[fold * rows : (fold + 1) * rows] = total[:, at : at + width]


def attend_pair(query, flags, key_wide, value_wide, scores, kept):
    rows = query.shape[0]
    keys = key_wide.shape[0]
    left = lane_numbers((rows, LANES)) < HEAD_DIM
    zero = jnp.zeros_like(query)
    queries = [
        jnp.concatenate([jnp.where(left, query, zero), flags], axis=1),
        jnp.concatenate([jnp.where(left, zero, query), flags], axis=1),
    ]

    def score(head, start, peak):
        made = dot(queries[head], key_wide[start : start + KEY_STEP], BY_LANES)
        scores[head, :, start : start + KEY_STEP] = made
        for at in range(0, KEY_STEP, LANES):
            peak = jnp.maximum(peak, made[:, at : at + LANES])
        return peak

    def weigh(head, start, peak, total):
        span = slice(start, start + KEY_STEP)
        weights = jnp.exp(scores[head, :, span] - peak).astype(LOW)
        kept[head, :, span] = weights
        return total + dot(weights, value_wide[span])

    steps = range(0, keys, KEY_STEP)
    lowest = jnp.full((rows, LANES), -jnp.inf, FULL)
    empty = jnp.zeros((rows, 2 * LANES), FULL)
    peak = lowest
    for start in steps:
        peak = score(0, start, peak)
    first_peak = jnp.max(peak, axis=1, keepdims=True)
    peak, first = lowest, empty
    for start in steps:
        peak = score(1, start, peak)
        first = weigh(0, start, first_peak, first)
    second_peak = jnp.max(peak, axis=1, keepdims=True)
    second = empty
    for start in steps:
        second = weigh(1, start, second_peak, second)
    inverse = 1.0 / jnp.where(left, first[:, LANES:], second[:, LANES:])
    mix = jnp.where(left, first[:, :LANES], second[:, :LANES]) * inverse
    return mix.astype(LOW), inverse


def pair_columns(first, pair):
    return pl.ds(pl.multiple_of(first + pair * LANES, LANES), LANES)


def prepare_wide(lengths, key_wide, value_wide, place):
    pairs, keys, _ = key_wide.shape
    local = keys // 4
    ones = jnp.ones((local, LANES), LOW)
    for step in range(4):
        span = slice(step * local, (step + 1) * local)
        flags = key_flags(lengths, (place ^ step) * local, local)
        for pair in range(pairs):
            key_wide[pair, span, LANES:] = flags
            value_wide[pair, span, LANES:] = ones


def project_rows(rows, weight, key_wide, value_wide):
    pairs = key_wide.shape[0]
    local = rows[0].shape[0]
    for step, part in enumerate(rows):
        span = slice(step * local, (step + 1) * local)
        for wide, first in ((key_wide, 0), (value_wide, pairs * LANES)):
            made = dot(part[...], weight[:, first : first + pairs * LANES]).astype(LOW)
            for pair in range(pairs):
                wide[pair, span, :LANES] = made[:, pair * LANES : (pair + 1) * LANES]


def project_queries(rows, weight, queries):
    made = dot(rows, weight).astype(LOW).astype(FULL) * score_scale
    for pair in range(queries.shape[0]):
        queries[pair] = made[:, pair * LANES : (pair + 1) * LANES].astype(LOW)


def self_forward_kernel(info, lengths, rows_0, rows_1, rows_2, rows_3, *refs):
    quarters = refs[:8]
    (
        mix_ref,
        query_ref,
        inverse_ref,
        key_ref,
        value_ref,
        kept,
        weight,
        queries,
        flags_q,
        key_wide,
        value_wide,
        scores,
    ) = refs[8:]
    pair = pl.program_id(0)
    home, place = info[0], info[1]
    local, width = rows_0.shape

    @pl.when(pair == 0)
    def _():
        fill_weight(weight, quarters, home, (0, 1))
        flags_q[...] = query_flags(lengths, place * local, local)
        prepare_wide(lengths, key_wide, value_wide, place)
        project_rows((rows_0, rows_1, rows_2, rows_3), weight.at[:, width:], key_wide, value_wide)
        project_queries(rows_0[...], weight[:, :width], queries)

    query = queries[pair]
    query_ref[...] = query
    key_ref[...] = key_wide[pair, :, :LANES]
    value_ref[...] = value_wide[pair, :, :LANES]
    mix, inverse = attend_pair(
        query, flags_q[...], key_wide.at[pair], value_wide.at[pair], scores, kept
    )
    mix_ref[...] = mix
    inverse_ref[...] = inverse


def cross_forward_kernel(
    info, target_lengths, source_lengths, mix, states, rows_0, rows_1, rows_2, rows_3, *refs
):
    quarters = refs[:8]
    (
        mix_ref,
        query_ref,
        inverse_ref,
        key_ref,
        value_ref,
        kept,
        unit_ref,
        scale_ref,
        norms_ref,
        out_weight,
        query_weight,
        pair_weight,
        norm_rows,
        queries,
        flags_q,
        key_wide,
        value_wide,
        scores,
    ) = refs[8:]
    pair = pl.program_id(0)
    home, place = info[0], info[1]
    local, width = rows_0.shape

    @pl.when(pair == 0)
    def _():
        fill_weight(out_weight, quarters, home, (0, 1))
        fill_weight(query_weight, quarters, home, (width, 1))
        fill_weight(pair_weight, quarters, home, (2 * width, 1))
        fill_weight(norm_rows, quarters, home, (4 * width, 1))
        norms = norm_rows[...].astype(FULL).T[0:8]
        norms_ref[...] = norms
        mixed = states[...].astype(FULL) + dot(mix[...], out_weight[...])
        unit, scale = normalise(mixed)
        unit_ref[...] = unit
        scale_ref[...] = jnp.broadcast_to(scale, (local, LANES))
        first_low = (unit * norms[0:1] + norms[3:4]).astype(LOW)
        project_queries(first_low, query_weight[...], queries)
        flags_q[...] = query_flags(target_lengths, place * local, local)
        prepare_wide(source_lengths, key_wide, value_wide, place)
        project_rows((rows_0, rows_1, rows_2, rows_3), pair_weight, key_wide, value_wide)

    query = queries[pair]
    query_ref[...] = query
    key_ref[...] = key_wide[pair, :, :LANES]
    value_ref[...] = value_wide[pair, :, :LANES]
    mixed, inverse = attend_pair(
        query, flags_q[...], key_wide.at[pair], value_wide.at[pair], scores, kept
    )
    mix_ref[...] = mixed
    inverse_ref[...] = inverse


gelu_factor = 0.7978845608028654
gelu_cubic = 0.044715


def gelu_and_slope(hidden):
    square = hidden * hidden
    bend = jnp.tanh(gelu_factor * (hidden + gelu_cubic * (square * hidden)))
    half = 0.5 * (1.0 + bend)
    slope = half + (0.5 * hidden) * (1.0 - bend * bend) * (
        gelu_factor * (1.0 + (3.0 * gelu_cubic) * square)
    )
    return hidden * half, slope


def middle_kernel(info, mix, first_unit, norms, out_grad, *refs):
    quarters = refs[:8]
    (
        output_ref,
        cotangent_ref,
        unit_ref,
        scale_ref,
        norm_sums_ref,
        kept,
        sent,
        out_weight,
        expand,
        contract,
        active,
        slope,
        wide_grad,
        tall_grad,
    ) = refs[8:]
    home = info[0]
    width = mix.shape[1]
    chunks = active.shape[0]
    span = expand.shape[1] // chunks
    fill_weight(out_weight, quarters, home, (0, 1))
    fill_weight(expand, quarters, home, (width, 1))
    fill_weight(contract, quarters, home, (width + expand.shape[1], contract.shape[0] // width))
    first_norm = first_unit[...] * norms[0:1] + norms[3:4]
    second_unit, second_scale = normalise(first_norm + dot(mix[...], out_weight[...]))
    unit_ref[...] = second_unit
    scale_ref[...] = jnp.broadcast_to(second_scale, scale_ref.shape)
    second_norm = second_unit * norms[1:2] + norms[4:5]
    second_low = second_norm.astype(LOW)

    def forward(at, total):
        start = pl.multiple_of(at * span, span)
        hidden = dot(second_low, expand[:, pl.ds(start, span)])
        made, bent = gelu_and_slope(hidden)
        made = made.astype(LOW)
        active[at] = made
        slope[at] = bent
        return total + dot(made, contract[pl.ds(start, span)])

    mixed = lax.fori_loop(0, chunks, forward, second_norm)
    third_unit, third_scale = normalise(mixed)
    output_ref[...] = third_unit * norms[2:3] + norms[5:6]
    third_grad, gain_three, bias_three = norm_backward(
        out_grad[...], third_unit, third_scale, norms[2:3]
    )
    ffn_grad = third_grad.astype(LOW)
    second_turned = second_low.T

    def backward(at, total):
        start = pl.multiple_of(at * span, span)
        part = contract[pl.ds(start, span)]
        hidden_grad = (dot(ffn_grad, part, BY_LANES) * slope[at]).astype(LOW)
        tall_grad[pl.ds(start, span)] = dot(active[at].T, ffn_grad).astype(LOW)
        wide_grad[:, pl.ds(start, span)] = dot(second_turned, hidden_grad).astype(LOW)
        return total + dot(hidden_grad, expand[:, pl.ds(start, span)], BY_LANES)

    cotangent_ref[...] = lax.fori_loop(0, chunks, backward, third_grad)
    norm_sums_ref[...] = jnp.zeros(norm_sums_ref.shape, FULL)
    norm_sums_ref[2:3] = gain_three
    norm_sums_ref[5:6] = bias_three
    pack_grad(wide_grad, kept, sent, home, (0, 1))
    pack_grad(tall_grad, kept, sent, home, (expand.shape[1], tall_grad.shape[0] // width))


def second_back_kernel(
    cotangent,
    second_unit,
    second_scale,
    norms,
    sums,
    mix,
    out_weight,
    second_grad_ref,
    mix_grad_ref,
    out_weight_grad,
    norm_sums_ref,
):
    second_grad, gain_two, bias_two = norm_backward(
        cotangent[...], second_unit[...], second_scale[:, 0:1], norms[1:2]
    )
    second_grad_ref[...] = second_grad
    cross_out_low = second_grad.astype(LOW)
    mix_grad_ref[...] = dot(cross_out_low, out_weight[...], BY_LANES).astype(LOW)
    out_weight_grad[...] = dot(mix[...].T, cross_out_low).astype(LOW)
    norm_sums_ref[...] = sums[...]
    norm_sums_ref[1:2] = gain_two
    norm_sums_ref[4:5] = bias_two


def attend_back_pair(query, key, value, kept, inverse, mix, grad, value_wide, made):
    rows = grad.shape[0]
    left = lane_numbers((rows, LANES)) < HEAD_DIM
    lane = lane_numbers((rows, LANES))
    value_wide[:, :LANES] = value
    grad = grad.astype(FULL) * inverse
    product = grad * mix.astype(FULL)
    low_grad = grad.astype(LOW)
    query_turned = query.T
    grad_turned = low_grad.T
    query_grads = []
    for head in range(2):
        mine = left if head == 0 else ~left
        inner = -jnp.sum(jnp.where(mine, product, 0.0), axis=1, keepdims=True)
        first, second, third = three_parts(inner)
        parts = jnp.where(lane == 0, first, jnp.where(lane == 1, second, jnp.where(lane == 2, third, 0.0)))
        wide = jnp.concatenate([jnp.where(mine, low_grad, jnp.zeros_like(low_grad)), parts.astype(LOW)], axis=1)
        weights = kept[head]
        shifted = dot(wide, value_wide[...], BY_LANES)
        score_grad = (weights.astype(FULL) * shifted).astype(LOW)
        query_grads.append(dot(score_grad, key))
        span = slice(head * HEAD_DIM, (head + 1) * HEAD_DIM)
        made[span] = dot(query_turned[span], score_grad).astype(LOW)
        made[LANES + head * HEAD_DIM : LANES + (head + 1) * HEAD_DIM] = dot(
            grad_turned[span], weights
        ).astype(LOW)
    return (jnp.where(left, query_grads[0], query_grads[1]) * score_scale).astype(LOW)


def cross_backward_kernel(
    info, query, key, value, kept, inverse, mix, grad, rows_0, rows_1, rows_2, rows_3, *refs
):
    quarters = refs[:8]
    query_grad_ref, weight_grad_ref, own_ref, parts_ref, weight, value_wide, made = refs[8:]
    pair = pl.program_id(0)
    width = rows_0.shape[1]

    @pl.when(pair == 0)
    def _():
        fill_weight(weight, quarters, info[0], (2 * width, 1))
        value_wide[:, LANES:] = jnp.ones((value_wide.shape[0], LANES), LOW)

    query_grad_ref[...] = attend_back_pair(
        query[...], key[...], value[...], kept, inverse[...], mix[...], grad[...], value_wide, made.at[pair]
    )

    @pl.when(pair == made.shape[0] - 1)
    def _():
        finish_rows(made, weight, 0, (rows_0, rows_1, rows_2, rows_3), own_ref, parts_ref, weight_grad_ref, 0)


def finish_rows(made, weight, first, row_refs, own_ref, parts_ref, weight_grad_ref, grad_first):
    local, width = row_refs[0].shape
    pairs = made.shape[0]
    for step in range(4):
        total = None
        for pair in range(pairs):
            at = first + pair * LANES
            columns = jnp.concatenate(
                [weight[:, at : at + LANES], weight[:, width + at : width + at + LANES]], axis=1
            )
            part = made[pair, :, step * local : (step + 1) * local].T
            term = dot(part, columns, BY_LANES)
            total = term if total is None else total + term
        if step == 0:
            own_ref[...] = total
        else:
            parts_ref[step - 1] = total.astype(LOW)
    for pair in range(pairs):
        total = None
        for step in range(4):
            term = dot(made[pair, :, step * local : (step + 1) * local], row_refs[step][...])
            total = term if total is None else total + term
        total = total.T.astype(LOW)
        at = grad_first + pair * LANES
        weight_grad_ref[:, at : at + LANES] = total[:, :LANES]
        weight_grad_ref[:, width + at : width + at + LANES] = total[:, LANES:]


def between_kernel(
    info, query_grad, second_grad, first_unit, first_scale, norms, norm_sums, self_mix, pair_grad, cross_out_grad, *refs
):
    quarters = refs[:8]
    (
        first_grad_ref,
        mix_grad_ref,
        kept,
        sent,
        out_weight,
        query_weight,
        out_grad,
        query_weight_grad,
        norm_grad,
        norm_rows,
    ) = refs[8:]
    home = info[0]
    width = self_mix.shape[1]
    fill_weight(out_weight, quarters, home, (0, 1))
    fill_weight(query_weight, quarters, home, (width, 1))
    unit = first_unit[...]
    first_low = (unit * norms[0:1] + norms[3:4]).astype(LOW)
    low_grad = query_grad[...]
    query_weight_grad[...] = dot(first_low.T, low_grad).astype(LOW)
    cotangent = second_grad[...] + dot(low_grad, query_weight[...], BY_LANES)
    first_grad, gain_one, bias_one = norm_backward(
        cotangent, unit, first_scale[:, 0:1], norms[0:1]
    )
    first_grad_ref[...] = first_grad
    self_out_low = first_grad.astype(LOW)
    out_grad[...] = dot(self_mix[...].T, self_out_low).astype(LOW)
    mix_grad_ref[...] = dot(self_out_low, out_weight[...], BY_LANES).astype(LOW)
    norm_rows[...] = jnp.zeros(norm_rows.shape, FULL)
    norm_rows[0:8] = norm_sums[...]
    norm_rows[0:1] = gain_one
    norm_rows[3:4] = bias_one
    norm_grad[...] = norm_rows[...].T.astype(LOW)
    pack_grad(out_grad, kept, sent, home, (0, 1))
    pack_grad(query_weight_grad, kept, sent, home, (width, 1))
    pack_grad(pair_grad, kept, sent, home, (2 * width, 1))
    pack_grad(cross_out_grad, kept, sent, home, (4 * width, 1))
    pack_grad(norm_grad, kept, sent, home, (5 * width, 1))


def self_backward_kernel(
    info, query, key, value, kept_weights, inverse, mix, grad, first_grad, rows_0, rows_1, rows_2, rows_3, *refs
):
    quarters = refs[:8]
    own_ref, parts_ref, kept, sent, weight, value_wide, made, query_grads, weight_grad = refs[8:]
    pair = pl.program_id(0)
    home = info[0]
    width = rows_0.shape[1]
    pairs = made.shape[0]

    @pl.when(pair == 0)
    def _():
        fill_weight(weight, quarters, home, (0, 1))
        value_wide[:, LANES:] = jnp.ones((value_wide.shape[0], LANES), LOW)

    query_grads[pair] = attend_back_pair(
        query[...], key[...], value[...], kept_weights, inverse[...], mix[...], grad[...], value_wide, made.at[pair]
    )

    @pl.when(pair == pairs - 1)
    def _():
        finish_rows(
            made, weight, width, (rows_0, rows_1, rows_2, rows_3), own_ref, parts_ref, weight_grad, width
        )
        low_grad = jnp.concatenate([query_grads[at] for at in range(pairs)], axis=1)
        weight_grad[:, 0:width] = dot(rows_0[...].T, low_grad).astype(LOW)
        own_ref[...] += first_grad[...] + dot(low_grad, weight[:, 0:width], BY_LANES)
        pack_grad(weight_grad, kept, sent, home, (0, 1))


def whole(shape):
    return pl.BlockSpec(shape, lambda *at: (0,) * len(shape))


def call(kernel, inputs, specs, outputs, out_specs, scratch, grid=(), micros=1, mib=58):
    moved = sum(math.prod(a.shape) * a.dtype.itemsize for a in list(inputs) + list(outputs))
    return pl.pallas_call(
        kernel,
        out_shape=outputs,
        grid=grid,
        in_specs=specs,
        out_specs=out_specs,
        scratch_shapes=scratch,
        compiler_params=pltpu.CompilerParams(vmem_limit_bytes=mib * 2**20),
        cost_estimate=pl.CostEstimate(flops=micros * 10**9, bytes_accessed=moved, transcendentals=0),
    )(*inputs)


SCALARS = pl.BlockSpec(memory_space=pltpu.SMEM)


def shaped(shape, kind):
    return jax.ShapeDtypeStruct(shape, kind)


def per_device(
    target_states,
    memory,
    target_lengths,
    source_lengths,
    self_project,
    self_output,
    cross_project,
    memory_project,
    cross_output,
    expand_weight,
    contract_weight,
    norm_gain,
    norm_bias,
    out_grad,
):
    _, local, width = target_states.shape
    states = target_states[0]
    own_memory = memory[0]
    rows = self_project.shape[0]
    ff = expand_weight.shape[1]
    keys = local * 4
    pairs = width // LANES
    info = jnp.stack([home_number(), lax.axis_index("narrow")]).astype(jnp.int32)

    batches = 3 * width, 4 * width + LANES, width + 2 * ff
    if staged():
        shards = (
            self_output,
            cross_project,
            memory_project,
            cross_output,
            expand_weight,
            contract_weight,
            norm_gain,
            norm_bias,
        )
        later = batches[1] + batches[2]
        batch_23 = call(
            pack_kernel,
            list(shards),
            [whole(shard.shape) for shard in shards],
            [shaped((rows, later), LOW)],
            [whole((rows, later))],
            [pltpu.VMEM((LANES, LANES), FULL)],
        )[0]
        far_1 = jnp.stack(gather_far(self_project))
        states_x = exchange(states, 2)
        states_c = exchange(states, 1)
        batch_23, far_1 = after(batch_23, far_1)
        near_23 = exchange(batch_23, FAR[0])
        plane_1 = gather_plane(far_1)
        (own_memory, near_23), states_x = after((own_memory, near_23), states_x)
        half_2 = jnp.stack([batch_23[:, : batches[1]], near_23[:, : batches[1]]])
        half_3 = jnp.stack([batch_23[:, batches[1] :], near_23[:, batches[1] :]])
        rest_2 = exchange(half_2, FAR[1])
        memory_x = exchange(own_memory, 2)
        half_3, rest_2 = after(half_3, rest_2)
        far_2 = jnp.concatenate([half_2, rest_2])
        rest_3 = exchange(half_3, FAR[1])
    else:
        norm_shard = jnp.concatenate([norm_gain, norm_bias], axis=0).T
        norm_shard = jnp.pad(norm_shard, ((0, 0), (0, LANES - norm_shard.shape[1])))
        folded = fold_rows(contract_weight, rows)
        plane_1 = self_project
        far_2 = jnp.concatenate([self_output, cross_project, memory_project, norm_shard], axis=1)
        far_3 = jnp.concatenate([cross_output, expand_weight, folded], axis=1)
        states_x = exchange(states, 2)
        states_c = exchange(states, 1)
        memory_c = exchange(own_memory, 1)
        memory_x = exchange(own_memory, 2)
    states_xc = exchange(states_x, 1)
    far_2, plane_1 = after(far_2, plane_1)
    weights_1 = gather_core(plane_1)
    row_states = [states, states_c, states_x, states_xc]
    plane_2 = gather_plane(far_2)

    row_spec = whole((local, width))
    pair_rows = pl.BlockSpec((local, LANES), lambda pair: (0, pair))
    pair_keys = pl.BlockSpec((keys, LANES), lambda pair: (0, pair))
    pair_kept = pl.BlockSpec((2, local, keys), lambda pair: (pair, 0, 0))
    quarter_specs_1 = [whole(q.shape) for q in weights_1]
    attend_scratch = [
        pltpu.VMEM((pairs, local, LANES), LOW),
        pltpu.VMEM((local, LANES), LOW),
        pltpu.VMEM((pairs, keys, 2 * LANES), LOW),
        pltpu.VMEM((pairs, keys, 2 * LANES), LOW),
        pltpu.VMEM((2, local, keys), FULL),
    ]
    attend_outputs = [
        shaped((local, width), LOW),
        shaped((local, width), LOW),
        shaped((local, width), FULL),
        pltpu.HBM((keys, width), LOW),
        pltpu.HBM((keys, width), LOW),
        pltpu.HBM((2 * pairs, local, keys), LOW),
    ]
    attend_specs = [pair_rows, pair_rows, pair_rows, pair_keys, pair_keys, pair_kept]
    self_mix, self_query, self_inverse, self_key, self_value, self_kept = call(
        self_forward_kernel,
        [info, target_lengths, *row_states, *weights_1],
        [SCALARS, SCALARS] + [row_spec] * 4 + quarter_specs_1,
        attend_outputs,
        attend_specs,
        [pltpu.VMEM((width, 3 * width), LOW)] + attend_scratch,
        grid=(pairs,),
        micros=25, mib=38,
    )

    if staged():
        (memory_x, own_memory, rest_3), self_mix = after((memory_x, own_memory, rest_3), self_mix)
        memory_c = exchange(own_memory, 1)
        far_3 = jnp.concatenate([half_3, rest_3])
    plane_2, self_mix = after(plane_2, self_mix)
    memory_xc = exchange(memory_x, 1)
    weights_2 = gather_core(plane_2)
    row_memory = [own_memory, memory_c, memory_x, memory_xc]
    plane_3 = gather_plane(far_3)
    quarter_specs_2 = [whole(q.shape) for q in weights_2]
    cross_mix, cross_query, cross_inverse, cross_key, cross_value, cross_kept, first_unit, first_scale, norms = call(
        cross_forward_kernel,
        [info, target_lengths, source_lengths, self_mix, states, *row_memory, *weights_2],
        [SCALARS] * 3 + [row_spec] * 6 + quarter_specs_2,
        attend_outputs
        + [
            shaped((local, width), FULL),
            shaped((local, LANES), FULL),
            shaped((8, width), FULL),
        ],
        attend_specs + [row_spec, whole((local, LANES)), whole((8, width))],
        [
            pltpu.VMEM((width, width), LOW),
            pltpu.VMEM((width, width), LOW),
            pltpu.VMEM((width, 2 * width), LOW),
            pltpu.VMEM((width, LANES), LOW),
        ]
        + attend_scratch,
        grid=(pairs,),
        micros=25, mib=42,
    )

    plane_3, cross_mix = after(plane_3, cross_mix)
    weights_3 = gather_core(plane_3, ff // width)
    quarter_specs_3 = [whole(q.shape) for q in weights_3]
    chunk_count = ff // width
    packed_3 = (4, 4, TILE_ROWS, 2 * ff)
    wide_scale = whole((local, LANES))
    norm_spec = whole((8, width))
    square = whole((width, width))
    output, cotangent, second_unit, second_scale, norm_sums, kept_3, sent_3, cross_out_weight = call(
        middle_kernel,
        [info, cross_mix, first_unit, norms, out_grad[0], *weights_3],
        [SCALARS, row_spec, row_spec, norm_spec, row_spec] + quarter_specs_3,
        [
            shaped((local, width), FULL),
            shaped((local, width), FULL),
            shaped((local, width), FULL),
            shaped((local, LANES), FULL),
            shaped((8, width), FULL),
            shaped(packed_3, LOW),
            shaped(packed_3, LOW),
            shaped((width, width), LOW),
        ],
        [row_spec, row_spec, row_spec, wide_scale, norm_spec, whole(packed_3), whole(packed_3), square],
        [
            pltpu.VMEM((width, ff), LOW),
            pltpu.VMEM((ff, width), LOW),
            pltpu.VMEM((chunk_count, local, width), LOW),
            pltpu.VMEM((chunk_count, local, width), FULL),
            pltpu.VMEM((width, ff), LOW),
            pltpu.VMEM((ff, width), LOW),
        ],
        micros=17, mib=36,
    )
    other_3 = exchange_core(sent_3)
    second_grad, cross_mix_grad, cross_out_grad, norm_sums = call(
        second_back_kernel,
        [cotangent, second_unit, second_scale, norms, norm_sums, cross_mix, cross_out_weight],
        [row_spec, row_spec, wide_scale, norm_spec, norm_spec, row_spec, square],
        [
            shaped((local, width), FULL),
            shaped((local, width), LOW),
            shaped((width, width), LOW),
            shaped((8, width), FULL),
        ],
        [row_spec, row_spec, square, norm_spec],
        [],
        micros=4, mib=8,
    )
    other_3, cross_mix_grad = after(other_3, cross_mix_grad)
    core_3 = reduce_core(kept_3, other_3)
    core_3, cross_mix_grad = after(core_3, cross_mix_grad)
    planes_3 = exchange_plane(core_3)

    back_scratch = [
        pltpu.VMEM((keys, 2 * LANES), LOW),
        pltpu.VMEM((pairs, 2 * LANES, keys), LOW),
    ]
    back_specs = [pair_rows, pair_keys, pair_keys, pair_kept, pair_rows, pair_rows, pair_rows]
    parts_shape = (3, local, width)
    cross_query_grad, pair_weight_grad, memory_own, memory_parts = call(
        cross_backward_kernel,
        [
            info,
            cross_query,
            cross_key,
            cross_value,
            cross_kept,
            cross_inverse,
            cross_mix,
            cross_mix_grad,
            *row_memory,
            *weights_2,
        ],
        [SCALARS] + back_specs + [row_spec] * 4 + quarter_specs_2,
        [
            shaped((local, width), LOW),
            shaped((width, 2 * width), LOW),
            shaped((local, width), FULL),
            shaped(parts_shape, LOW),
        ],
        [pair_rows, whole((width, 2 * width)), row_spec, whole(parts_shape)],
        [pltpu.VMEM((width, 2 * width), LOW)] + back_scratch,
        grid=(pairs,),
        micros=33, mib=36,
    )
    (planes_3, memory_parts), cross_query_grad = after((planes_3, memory_parts), cross_query_grad)
    plane_sum_3 = reduce_plane(planes_3)
    memory_sent = exchange_row(memory_parts)
    plane_sum_3, cross_query_grad = after(plane_sum_3, cross_query_grad)
    half_sum_3 = exchange_half(plane_sum_3)

    packed_2 = (4, 4, TILE_ROWS, 5 * width + LANES)
    first_grad, self_mix_grad, kept_2, sent_2 = call(
        between_kernel,
        [
            info,
            cross_query_grad,
            second_grad,
            first_unit,
            first_scale,
            norms,
            norm_sums,
            self_mix,
            pair_weight_grad,
            cross_out_grad,
            *weights_2,
        ],
        [SCALARS, row_spec, row_spec, row_spec, whole((local, LANES))]
        + [whole((8, width))] * 2
        + [row_spec, whole((width, 2 * width)), whole((width, width))]
        + quarter_specs_2,
        [
            shaped((local, width), FULL),
            shaped((local, width), LOW),
            shaped(packed_2, LOW),
            shaped(packed_2, LOW),
        ],
        [row_spec, row_spec, whole(packed_2), whole(packed_2)],
        [
            pltpu.VMEM((width, width), LOW),
            pltpu.VMEM((width, width), LOW),
            pltpu.VMEM((width, width), LOW),
            pltpu.VMEM((width, width), LOW),
            pltpu.VMEM((width, LANES), LOW),
            pltpu.VMEM((LANES, width), FULL),
        ],
        micros=6, mib=14,
    )
    other_2 = exchange_core(sent_2)
    core_2 = reduce_core(kept_2, other_2)
    memory_other = reduce_row_core(memory_parts, memory_sent)
    (core_2, memory_other), self_mix_grad = after((core_2, memory_other), self_mix_grad)
    planes_2 = exchange_plane(core_2)
    memory_far = exchange(memory_other, 2)

    packed_1 = (4, 4, TILE_ROWS, 3 * width)
    states_own, states_parts, kept_1, sent_1 = call(
        self_backward_kernel,
        [
            info,
            self_query,
            self_key,
            self_value,
            self_kept,
            self_inverse,
            self_mix,
            self_mix_grad,
            first_grad,
            *row_states,
            *weights_1,
        ],
        [SCALARS] + back_specs + [row_spec] * 5 + quarter_specs_1,
        [
            shaped((local, width), FULL),
            shaped(parts_shape, LOW),
            shaped(packed_1, LOW),
            shaped(packed_1, LOW),
        ],
        [row_spec, whole(parts_shape), whole(packed_1), whole(packed_1)],
        [pltpu.VMEM((width, 3 * width), LOW)]
        + back_scratch
        + [pltpu.VMEM((pairs, local, LANES), LOW), pltpu.VMEM((width, 3 * width), LOW)],
        grid=(pairs,),
        micros=33, mib=36,
    )
    (planes_2, memory_far, half_sum_3), (sent_1, kept_1, states_parts, states_own) = after(
        (planes_2, memory_far, half_sum_3), (sent_1, kept_1, states_parts, states_own)
    )
    other_1 = exchange_core(sent_1)
    states_sent = exchange_row(states_parts)
    core_1 = reduce_core(kept_1, other_1)
    planes_1 = exchange_plane(core_1)
    (planes_2, memory_far, half_sum_3, states_sent), core_1 = after(
        (planes_2, memory_far, half_sum_3, states_sent), core_1
    )
    total_3 = reduce_half(plane_sum_3, half_sum_3)
    fars_3 = exchange_near(total_3)
    plane_sum_2 = reduce_plane(planes_2)
    half_sum_2 = exchange_half(plane_sum_2)
    states_other = reduce_row_core(states_parts, states_sent)
    states_far = exchange(states_other, 2)
    memory_grad = reduce_row(memory_own, memory_sent, memory_far)
    plane_sum_1 = reduce_plane(planes_1)
    fars_1 = exchange_far(plane_sum_1)
    total_2 = reduce_half(plane_sum_2, half_sum_2)
    fars_2 = exchange_near(total_2)
    states_grad = reduce_row(states_own, states_sent, states_far)
    count = norm_gain.shape[0]
    if staged():
        expand_grad, contract_grad = call(
            settle_wide_kernel,
            list(fars_3),
            [whole((rows, 2 * ff))] * len(fars_3),
            [shaped((rows, ff), FULL), shaped((rows * ff // width, width), FULL)],
            [whole((rows, ff)), whole((rows * ff // width, width))],
            [],
        )
        settled = [
            shaped((rows, 3 * width), FULL),
            shaped((rows, width), FULL),
            shaped((rows, width), FULL),
            shaped((rows, 2 * width), FULL),
            shaped((rows, width), FULL),
            shaped(norm_gain.shape, FULL),
            shaped(norm_gain.shape, FULL),
        ]
        project, out, cross, pairs_grad, cross_out, gain, bias = call(
            settle_kernel,
            list(fars_1) + list(fars_2),
            [whole((rows, 3 * width))] * 4 + [whole((rows, 5 * width + LANES))] * 2,
            settled,
            [whole(each.shape) for each in settled],
            [pltpu.VMEM((LANES, LANES), FULL)],
        )
    else:
        grad_3 = reduce_far(fars_3, ff // width)
        grad_2 = reduce_far(fars_2)
        project = reduce_far(fars_1)
        expand_grad, contract_grad = grad_3[:, :ff], unfold_rows(grad_3[:, ff:], width)
        out, cross = grad_2[:, :width], grad_2[:, width : 2 * width]
        pairs_grad, cross_out = grad_2[:, 2 * width : 4 * width], grad_2[:, 4 * width : 5 * width]
        norm_grads = grad_2[:, 5 * width :].T
        gain, bias = norm_grads[:count], norm_grads[count : 2 * count]
    return (
        output[None],
        states_grad[None],
        memory_grad[None],
        project,
        out,
        cross,
        pairs_grad,
        cross_out,
        expand_grad,
        contract_grad,
        gain,
        bias,
    )


def exchange_row(parts):
    return exchange(parts[0], 1), exchange(parts[2], 1)


def reduce_row_core(parts, sent):
    return add_all(parts[1], [sent[1]]).astype(LOW)


def reduce_row(own, sent, far):
    return add_all(own, [sent[0], far])


def solution(mesh):
    in_specs = (
        P("wide", "narrow", None),
        P("wide", "narrow", None),
        P("wide", None),
        P("wide", None),
        P(("wide", "narrow"), None),
        P(("wide", "narrow"), None),
        P(("wide", "narrow"), None),
        P(("wide", "narrow"), None),
        P(("wide", "narrow"), None),
        P(("wide", "narrow"), None),
        P(("wide", "narrow"), None),
        P(None, ("wide", "narrow")),
        P(None, ("wide", "narrow")),
        P("wide", "narrow", None),
    )
    out_specs = (
        P("wide", "narrow", None),
        P("wide", "narrow", None),
        P("wide", "narrow", None),
        P(("wide", "narrow"), None),
        P(("wide", "narrow"), None),
        P(("wide", "narrow"), None),
        P(("wide", "narrow"), None),
        P(("wide", "narrow"), None),
        P(("wide", "narrow"), None),
        P(("wide", "narrow"), None),
        P(None, ("wide", "narrow")),
        P(None, ("wide", "narrow")),
    )
    return jax.shard_map(
        per_device, mesh=mesh, in_specs=in_specs, out_specs=out_specs, check_vma=False
    )
```

```python
import functools
import math

import jax
import jax.numpy as jnp
from jax import lax
from jax.experimental import pallas as pl
from jax.experimental.pallas import tpu as pltpu
from jax.sharding import PartitionSpec as P

HEAD_DIM = 64
LANES = 128
TILE_ROWS = 16
BLOCKS = 32
AXES = ("wide", "narrow")
LOW = jnp.bfloat16
FULL = jnp.float32

ln_eps = 1e-05
score_scale = HEAD_DIM ** (-0.5)
mask_step = -(2.0**30)

BY_LANES = (((1,), (1,)), ((), ()))
PLAIN = (((1,), (0,)), ((), ()))


def dot(left, right, dims=PLAIN):
    return lax.dot_general(left, right, dims, preferred_element_type=FULL)


def exchange(block, mask):
    device_count = lax.axis_size("wide") * lax.axis_size("narrow")
    pairs = [(device, device ^ mask) for device in range(device_count)]
    return lax.ppermute(block, AXES, pairs)


def device_number():
    return lax.axis_index("wide") * lax.axis_size("narrow") + lax.axis_index("narrow")


def staged():
    return lax.axis_size("wide") * lax.axis_size("narrow") == BLOCKS


FAR = (8, 16, 24)
PLANE = (2, 4, 6)


def gather_far(shard):
    if not staged():
        return shard
    return [shard] + [exchange(shard, mask) for mask in FAR]


def gather_plane(held):
    if not staged():
        return held
    return [held] + [exchange(held, mask) for mask in PLANE]


def gather_core(held, own=None, folds=0):
    if staged():
        first = exchange(held[0], 1) if own is None else own
        return held + [first] + [exchange(quarter, 1) for quarter in held[1:]]
    whole = lax.all_gather(held, AXES, axis=0, tiled=True)
    if folds:
        rows, columns = held.shape
        split = columns - folds * whole.shape[0]
        tall = unfold_rows(held[:, split:], whole.shape[0])
        tall = lax.all_gather(tall, AXES, axis=0, tiled=True)
        tall = tall.reshape(BLOCKS, folds, TILE_ROWS, -1).transpose(0, 2, 1, 3)
        whole = jnp.concatenate([whole[:, :split], tall.reshape(whole.shape[0], -1)], axis=1)
    whole = whole.reshape(4, 4, 2, TILE_ROWS, held.shape[1]).transpose(2, 1, 0, 3, 4)
    return [whole[core, plane] for core in range(2) for plane in range(4)]


def home_number():
    return device_number() if staged() else jnp.zeros((), jnp.int32)


def block_number(home, core, plane, far):
    return home ^ (far * 8 + plane * 2 + core)


def add_all(first, others):
    total = first.astype(FULL)
    for other in others:
        total = total + other.astype(FULL)
    return total


def exchange_core(sent):
    return exchange(sent, 1) if staged() else sent


def reduce_core(kept, other):
    return add_all(kept, [other]).astype(LOW) if staged() else (kept, other)


def exchange_plane(held):
    if not staged():
        return held
    return [held[0]] + [exchange(held[plane + 1], mask) for plane, mask in enumerate(PLANE)]


def reduce_plane(planes):
    return add_all(planes[0], planes[1:]).astype(LOW) if staged() else planes


def exchange_far(held):
    if not staged():
        return held
    return [held[0]] + [exchange(held[far + 1], mask) for far, mask in enumerate(FAR)]


def exchange_half(held):
    return exchange(held[2:], FAR[1]) if staged() else held


def reduce_half(held, other):
    return add_all(held[:2], [other]).astype(LOW) if staged() else held


def reduce_far(held, folds=0):
    if staged():
        return add_all(held[0], held[1:])
    whole = jnp.stack(held).transpose(2, 1, 0, 3, 4)
    whole = whole.reshape(BLOCKS * TILE_ROWS, -1).astype(FULL)
    if folds:
        split = whole.shape[1] - folds * whole.shape[0]
        tall = whole[:, split:].reshape(BLOCKS, TILE_ROWS, folds, -1).transpose(0, 2, 1, 3)
        tall = tall.reshape(folds * whole.shape[0], -1)
        tall = lax.psum_scatter(tall, AXES, scatter_dimension=0, tiled=True)
        whole = lax.psum_scatter(whole[:, :split], AXES, scatter_dimension=0, tiled=True)
        return jnp.concatenate([whole, fold_rows(tall, whole.shape[0])], axis=1)
    return lax.psum_scatter(whole, AXES, scatter_dimension=0, tiled=True)


def after(values, token):
    return lax.optimization_barrier((values, token))


def fold_rows(block, rows):
    return jnp.concatenate(
        [block[at : at + rows] for at in range(0, block.shape[0], rows)], axis=1
    )


def unfold_rows(block, width):
    return jnp.concatenate(
        [block[:, at : at + width] for at in range(0, block.shape[1], width)], axis=0
    )


def lane_numbers(shape):
    return lax.broadcasted_iota(jnp.int32, shape, 1)


def segment_bounds(lengths_ref):
    lane = lane_numbers((1, LANES))
    first = jnp.full((1, LANES), 2**30, jnp.int32)
    last = jnp.zeros((1, LANES), jnp.int32)
    start = jnp.int32(0)
    count = lengths_ref.shape[1]
    for segment in range(count + 1):
        end = start + lengths_ref[0, segment] if segment < count else jnp.int32(2**30)
        first = jnp.where(lane == segment, start, first)
        last = jnp.where(lane == segment, end, last)
        start = end
    return first, last


def segment_flags(start, rows, bounds):
    position = start + lax.broadcasted_iota(jnp.int32, (rows, LANES), 0)
    return (position >= bounds[0]) & (position < bounds[1])


def three_parts(value):
    first = value.astype(LOW)
    rest = value - first.astype(FULL)
    second = rest.astype(LOW)
    third = (rest - second.astype(FULL)).astype(LOW)
    return first.astype(FULL), second.astype(FULL), third.astype(FULL)


def query_flags(lengths_ref, start, rows):
    segments = lengths_ref.shape[1] + 1
    own = segment_flags(start, rows, segment_bounds(lengths_ref))
    return jnp.where(own | (lane_numbers((rows, LANES)) >= segments), 0.0, mask_step).astype(LOW)


def key_flags(lengths_ref, start, rows):
    own = segment_flags(start, rows, segment_bounds(lengths_ref))
    return jnp.where(own, 1.0, 0.0).astype(LOW)


def fill_weight(target, quarters, home, columns):
    first, folds = columns
    width = target.shape[1]
    for core in range(2):
        for plane in range(4):
            for far in range(4):
                block = block_number(home, core, plane, far)
                piece = quarters[core * 4 + plane]
                for fold in range(folds):
                    row = pl.multiple_of(block * (TILE_ROWS * folds) + fold * TILE_ROWS, TILE_ROWS)
                    start = first + fold * width
                    target[pl.ds(row, TILE_ROWS), :] = piece[far, :, start : start + width]


def pack_grad(source, kept, sent, home, columns):
    first, folds = columns
    width = source.shape[1]
    for core, target in ((0, kept), (1, sent)):
        for plane in range(4):
            for far in range(4):
                block = block_number(home, core, plane, far)
                for fold in range(folds):
                    row = pl.multiple_of(block * (TILE_ROWS * folds) + fold * TILE_ROWS, TILE_ROWS)
                    start = first + fold * width
                    target[plane, far, :, start : start + width] = source[pl.ds(row, TILE_ROWS), :]


def normalise(states):
    centred = states - jnp.mean(states, axis=1, keepdims=True)
    spread = jnp.mean(centred * centred, axis=1, keepdims=True)
    scale = lax.rsqrt(spread + ln_eps)
    return centred * scale, scale


def norm_backward(cotangent, unit, scale, gain):
    scaled = cotangent * gain
    grad = scale * (
        scaled
        - jnp.mean(scaled, axis=1, keepdims=True)
        - unit * jnp.mean(scaled * unit, axis=1, keepdims=True)
    )
    return (
        grad,
        jnp.sum(cotangent * unit, axis=0, keepdims=True),
        jnp.sum(cotangent, axis=0, keepdims=True),
    )


KEY_STEP = 256


def pack_kernel(*refs):
    ins, (packed, square) = refs[:8], refs[8:]
    self_output, cross_project, memory_project, cross_output, expand, contract, gain, bias = ins
    rows, width = self_output.shape
    at = 0
    for part in (self_output, cross_project, memory_project, cross_output):
        packed[:, at : at + part.shape[1]] = part[...]
        at += part.shape[1]
    count = gain.shape[0]
    square[...] = jnp.zeros(square.shape, FULL)
    square[0:count, 0:rows] = gain[...].astype(FULL)
    square[count : 2 * count, 0:rows] = bias[...].astype(FULL)
    packed[:, at : at + LANES] = square[...].T[0:rows].astype(LOW)
    at += LANES
    packed[:, at : at + expand.shape[1]] = expand[...]
    at += expand.shape[1]
    for fold in range(contract.shape[0] // rows):
        packed[:, at : at + width] = contract[fold * rows : (fold + 1) * rows]
        at += width


def settle_kernel(part_2, part_3, other, *refs):
    output_ref, cross_ref, memory_ref, cross_out_ref, expand_ref, contract_ref, gain_ref, bias_ref, square = refs
    rows, width = output_ref.shape
    split = part_2.shape[1]
    total = add_all(part_2[...], [other[:, :split]])
    at = 0
    for ref in (output_ref, cross_ref, memory_ref, cross_out_ref):
        ref[...] = total[:, at : at + ref.shape[1]]
        at += ref.shape[1]
    square[...] = jnp.zeros(square.shape, FULL)
    square[0:rows] = total[:, at : at + LANES]
    turned = square[...].T
    count = gain_ref.shape[0]
    gain_ref[...] = turned[0:count, 0:rows]
    bias_ref[...] = turned[count : 2 * count, 0:rows]
    total = add_all(part_3[...], [other[:, split:]])
    span = expand_ref.shape[1]
    expand_ref[...] = total[:, :span]
    for fold in range(contract_ref.shape[0] // rows):
        at = span + fold * width
        contract_ref[fold * rows : (fold + 1) * rows] = total[:, at : at + width]


def attend_pair(query, flags, key_wide, value_wide, scores, kept):
    rows = query.shape[0]
    keys = key_wide.shape[0]
    left = lane_numbers((rows, LANES)) < HEAD_DIM
    zero = jnp.zeros_like(query)
    queries = [
        jnp.concatenate([jnp.where(left, query, zero), flags], axis=1),
        jnp.concatenate([jnp.where(left, zero, query), flags], axis=1),
    ]

    def score(head, start, peak):
        made = dot(queries[head], key_wide[start : start + KEY_STEP], BY_LANES)
        scores[head, :, start : start + KEY_STEP] = made
        for at in range(0, KEY_STEP, LANES):
            peak = jnp.maximum(peak, made[:, at : at + LANES])
        return peak

    def weigh(head, start, peak, total):
        span = slice(start, start + KEY_STEP)
        weights = jnp.exp(scores[head, :, span] - peak).astype(LOW)
        kept[head, :, span] = weights
        return total + dot(weights, value_wide[span])

    steps = range(0, keys, KEY_STEP)
    lowest = jnp.full((rows, LANES), -jnp.inf, FULL)
    empty = jnp.zeros((rows, 2 * LANES), FULL)
    peak = lowest
    for start in steps:
        peak = score(0, start, peak)
    first_peak = jnp.max(peak, axis=1, keepdims=True)
    peak, first = lowest, empty
    for start in steps:
        peak = score(1, start, peak)
        first = weigh(0, start, first_peak, first)
    second_peak = jnp.max(peak, axis=1, keepdims=True)
    second = empty
    for start in steps:
        second = weigh(1, start, second_peak, second)
    inverse = 1.0 / jnp.where(left, first[:, LANES:], second[:, LANES:])
    mix = jnp.where(left, first[:, :LANES], second[:, :LANES]) * inverse
    return mix.astype(LOW), inverse


def pair_columns(first, pair):
    return pl.ds(pl.multiple_of(first + pair * LANES, LANES), LANES)


def prepare_wide(lengths, key_wide, value_wide, place):
    pairs, keys, _ = key_wide.shape
    local = keys // 4
    ones = jnp.ones((local, LANES), LOW)
    for step in range(4):
        span = slice(step * local, (step + 1) * local)
        flags = key_flags(lengths, (place ^ step) * local, local)
        for pair in range(pairs):
            key_wide[pair, span, LANES:] = flags
            value_wide[pair, span, LANES:] = ones


def project_rows(rows, weight, key_wide, value_wide):
    pairs = key_wide.shape[0]
    local = rows[0].shape[0]
    for step, part in enumerate(rows):
        span = slice(step * local, (step + 1) * local)
        for wide, first in ((key_wide, 0), (value_wide, pairs * LANES)):
            made = dot(part[...], weight[:, first : first + pairs * LANES]).astype(LOW)
            for pair in range(pairs):
                wide[pair, span, :LANES] = made[:, pair * LANES : (pair + 1) * LANES]


def project_queries(rows, weight, queries):
    made = dot(rows, weight).astype(LOW).astype(FULL) * score_scale
    for pair in range(queries.shape[0]):
        queries[pair] = made[:, pair * LANES : (pair + 1) * LANES].astype(LOW)


def self_forward_kernel(info, lengths, rows_0, rows_1, rows_2, rows_3, *refs):
    quarters = refs[:8]
    (
        mix_ref,
        query_ref,
        inverse_ref,
        key_ref,
        value_ref,
        kept,
        weight_ref,
        weight,
        saved,
        queries,
        flags_q,
        key_wide,
        value_wide,
        scores,
    ) = refs[8:]
    pair = pl.program_id(0)
    home, place = info[0], info[1]
    local, width = rows_0.shape

    @pl.when(pair == 0)
    def _():
        fill_weight(weight, quarters, home, (0, 1))
        pltpu.make_async_copy(weight, weight_ref, saved).start()
        flags_q[...] = query_flags(lengths, place * local, local)
        prepare_wide(lengths, key_wide, value_wide, place)
        project_rows((rows_0, rows_1, rows_2, rows_3), weight.at[:, width:], key_wide, value_wide)
        project_queries(rows_0[...], weight[:, :width], queries)

    query = queries[pair]
    query_ref[...] = query
    key_ref[...] = key_wide[pair, :, :LANES]
    value_ref[...] = value_wide[pair, :, :LANES]
    mix, inverse = attend_pair(
        query, flags_q[...], key_wide.at[pair], value_wide.at[pair], scores, kept
    )
    mix_ref[...] = mix
    inverse_ref[...] = inverse

    @pl.when(pair == queries.shape[0] - 1)
    def _():
        pltpu.make_async_copy(weight, weight_ref, saved).wait()


def cross_forward_kernel(
    info, target_lengths, source_lengths, mix, states, rows_0, rows_1, rows_2, rows_3, *refs
):
    quarters = refs[:8]
    (
        mix_ref,
        query_ref,
        inverse_ref,
        key_ref,
        value_ref,
        kept,
        unit_ref,
        scale_ref,
        norms_ref,
        second_unit_ref,
        second_scale_ref,
        cross_out_ref,
        out_weight_ref,
        query_weight_ref,
        pair_weight_ref,
        out_weight,
        query_weight,
        pair_weight,
        norm_rows,
        saved,
        mixes,
        queries,
        flags_q,
        key_wide,
        value_wide,
        scores,
    ) = refs[8:]
    pair = pl.program_id(0)
    home, place = info[0], info[1]
    local, width = rows_0.shape

    copies = [
        pltpu.make_async_copy(source, target, saved.at[at])
        for at, (source, target) in enumerate(
            (
                (out_weight, out_weight_ref),
                (query_weight, query_weight_ref),
                (pair_weight, pair_weight_ref),
            )
        )
    ]

    @pl.when(pair == 0)
    def _():
        fill_weight(out_weight, quarters, home, (0, 1))
        fill_weight(query_weight, quarters, home, (width, 1))
        fill_weight(pair_weight, quarters, home, (2 * width, 1))
        for copy in copies:
            copy.start()
        fill_weight(cross_out_ref, quarters, home, (4 * width, 1))
        fill_weight(norm_rows, quarters, home, (5 * width, 1))
        norms = norm_rows[...].astype(FULL).T[0:8]
        norms_ref[...] = norms
        mixed = states[...].astype(FULL) + dot(mix[...], out_weight[...])
        unit, scale = normalise(mixed)
        unit_ref[...] = unit
        scale_ref[...] = jnp.broadcast_to(scale, (local, LANES))
        first_low = (unit * norms[0:1] + norms[3:4]).astype(LOW)
        project_queries(first_low, query_weight[...], queries)
        flags_q[...] = query_flags(target_lengths, place * local, local)
        prepare_wide(source_lengths, key_wide, value_wide, place)
        project_rows((rows_0, rows_1, rows_2, rows_3), pair_weight, key_wide, value_wide)

    query = queries[pair]
    query_ref[...] = query
    key_ref[...] = key_wide[pair, :, :LANES]
    value_ref[...] = value_wide[pair, :, :LANES]
    mixed, inverse = attend_pair(
        query, flags_q[...], key_wide.at[pair], value_wide.at[pair], scores, kept
    )
    mix_ref[...] = mixed
    inverse_ref[...] = inverse
    mixes[pair] = mixed

    @pl.when(pair == mixes.shape[0] - 1)
    def _():
        first_norm = unit_ref[...] * norms_ref[0:1] + norms_ref[3:4]
        whole_mix = jnp.concatenate([mixes[at] for at in range(mixes.shape[0])], axis=1)
        second_unit, second_scale = normalise(first_norm + dot(whole_mix, cross_out_ref[...]))
        second_unit_ref[...] = second_unit
        second_scale_ref[...] = jnp.broadcast_to(second_scale, (local, LANES))
        for copy in copies:
            copy.wait()


gelu_factor = 0.7978845608028654
gelu_cubic = 0.044715


def gelu_and_slope(hidden):
    square = hidden * hidden
    bend = jnp.tanh(gelu_factor * (hidden + gelu_cubic * (square * hidden)))
    half = 0.5 * (1.0 + bend)
    slope = half + (0.5 * hidden) * (1.0 - bend * bend) * (
        gelu_factor * (1.0 + (3.0 * gelu_cubic) * square)
    )
    return hidden * half, slope


def middle_kernel(info, second_unit, norms, out_grad, *refs):
    quarters = refs[:8]
    (
        output_ref,
        third_grad_ref,
        hidden_grads,
        expand,
        norm_sums_ref,
        kept,
        sent,
        contract,
        active,
        slope,
        wide_grad,
        tall_grad,
    ) = refs[8:]
    home = info[0]
    width = second_unit.shape[1]
    chunks = active.shape[0]
    span = expand.shape[1] // chunks
    fill_weight(expand, quarters, home, (0, 1))
    fill_weight(contract, quarters, home, (expand.shape[1], contract.shape[0] // width))
    second_norm = second_unit[...] * norms[1:2] + norms[4:5]
    second_low = second_norm.astype(LOW)

    def forward(at, total):
        start = pl.multiple_of(at * span, span)
        hidden = dot(second_low, expand[:, pl.ds(start, span)])
        made, bent = gelu_and_slope(hidden)
        made = made.astype(LOW)
        active[at] = made
        slope[at] = bent
        return total + dot(made, contract[pl.ds(start, span)])

    mixed = lax.fori_loop(0, chunks, forward, second_norm)
    third_unit, third_scale = normalise(mixed)
    output_ref[...] = third_unit * norms[2:3] + norms[5:6]
    third_grad, gain_three, bias_three = norm_backward(
        out_grad[...], third_unit, third_scale, norms[2:3]
    )
    third_grad_ref[...] = third_grad
    ffn_grad = third_grad.astype(LOW)
    second_turned = second_low.T

    def backward(at, carry):
        start = pl.multiple_of(at * span, span)
        part = contract[pl.ds(start, span)]
        hidden_grad = (dot(ffn_grad, part, BY_LANES) * slope[at]).astype(LOW)
        hidden_grads[at] = hidden_grad
        tall_grad[pl.ds(start, span)] = dot(active[at].T, ffn_grad).astype(LOW)
        wide_grad[:, pl.ds(start, span)] = dot(second_turned, hidden_grad).astype(LOW)
        return carry

    lax.fori_loop(0, chunks, backward, 0)
    norm_sums_ref[...] = jnp.zeros(norm_sums_ref.shape, FULL)
    norm_sums_ref[2:3] = gain_three
    norm_sums_ref[5:6] = bias_three
    pack_grad(wide_grad, kept, sent, home, (0, 1))
    pack_grad(tall_grad, kept, sent, home, (expand.shape[1], tall_grad.shape[0] // width))


def second_back_kernel(
    third_grad,
    hidden_grads,
    expand,
    second_unit,
    second_scale,
    norms,
    sums,
    mix,
    out_weight,
    second_grad_ref,
    mix_grad_ref,
    out_weight_grad,
    norm_sums_ref,
):
    cotangent = third_grad[...]
    chunks = hidden_grads.shape[0]
    span = expand.shape[1] // chunks
    for at in range(chunks):
        part = expand[:, at * span : (at + 1) * span]
        cotangent = cotangent + dot(hidden_grads[at], part, BY_LANES)
    second_grad, gain_two, bias_two = norm_backward(
        cotangent, second_unit[...], second_scale[:, 0:1], norms[1:2]
    )
    second_grad_ref[...] = second_grad
    cross_out_low = second_grad.astype(LOW)
    mix_grad_ref[...] = dot(cross_out_low, out_weight[...], BY_LANES).astype(LOW)
    out_weight_grad[...] = dot(mix[...].T, cross_out_low).astype(LOW)
    norm_sums_ref[...] = sums[...]
    norm_sums_ref[1:2] = gain_two
    norm_sums_ref[4:5] = bias_two


def attend_back_pair(query, key, value, kept, inverse, mix, grad, value_wide, made):
    rows = grad.shape[0]
    left = lane_numbers((rows, LANES)) < HEAD_DIM
    lane = lane_numbers((rows, LANES))
    value_wide[:, :LANES] = value
    grad = grad.astype(FULL) * inverse
    product = grad * mix.astype(FULL)
    low_grad = grad.astype(LOW)
    query_turned = query.T
    grad_turned = low_grad.T
    query_grads = []
    for head in range(2):
        mine = left if head == 0 else ~left
        inner = -jnp.sum(jnp.where(mine, product, 0.0), axis=1, keepdims=True)
        first, second, third = three_parts(inner)
        parts = jnp.where(lane == 0, first, jnp.where(lane == 1, second, jnp.where(lane == 2, third, 0.0)))
        wide = jnp.concatenate([jnp.where(mine, low_grad, jnp.zeros_like(low_grad)), parts.astype(LOW)], axis=1)
        weights = kept[head]
        shifted = dot(wide, value_wide[...], BY_LANES)
        score_grad = (weights.astype(FULL) * shifted).astype(LOW)
        query_grads.append(dot(score_grad, key))
        span = slice(head * HEAD_DIM, (head + 1) * HEAD_DIM)
        made[span] = dot(query_turned[span], score_grad).astype(LOW)
        made[LANES + head * HEAD_DIM : LANES + (head + 1) * HEAD_DIM] = dot(
            grad_turned[span], weights
        ).astype(LOW)
    return (jnp.where(left, query_grads[0], query_grads[1]) * score_scale).astype(LOW)


def cross_backward_kernel(
    query,
    key,
    value,
    kept,
    inverse,
    mix,
    grad,
    rows_0,
    rows_1,
    rows_2,
    rows_3,
    weight,
    query_grad_ref,
    weight_grad_ref,
    own_ref,
    far_ref,
    core_ref,
    value_wide,
    made,
):
    pair = pl.program_id(0)

    @pl.when(pair == 0)
    def _():
        value_wide[:, LANES:] = jnp.ones((value_wide.shape[0], LANES), LOW)

    query_grad_ref[...] = attend_back_pair(
        query[...], key[...], value[...], kept, inverse[...], mix[...], grad[...], value_wide, made.at[pair]
    )

    @pl.when(pair == made.shape[0] - 1)
    def _():
        finish_rows(made, weight, 0, own_ref, far_ref, core_ref)
        finish_weight(made, (rows_0, rows_1, rows_2, rows_3), weight_grad_ref, 0)


def finish_rows(made, weight, first, own_ref, far_ref, core_ref):
    pairs, _, keys = made.shape
    local = keys // 4
    width = own_ref.shape[1]
    for step in range(4):
        total = None
        for pair in range(pairs):
            at = first + pair * LANES
            columns = jnp.concatenate(
                [weight[:, at : at + LANES], weight[:, width + at : width + at + LANES]], axis=1
            )
            part = made[pair, :, step * local : (step + 1) * local].T
            term = dot(part, columns, BY_LANES)
            total = term if total is None else total + term
        if step == 0:
            own_ref[...] = total
        elif step == 2:
            far_ref[...] = total.astype(LOW)
        else:
            core_ref[step // 2] = total.astype(LOW)


def finish_weight(made, row_refs, weight_grad_ref, first):
    local, width = row_refs[0].shape
    for pair in range(made.shape[0]):
        total = None
        for step in range(4):
            term = dot(made[pair, :, step * local : (step + 1) * local], row_refs[step][...])
            total = term if total is None else total + term
        total = total.T.astype(LOW)
        at = first + pair * LANES
        weight_grad_ref[:, at : at + LANES] = total[:, :LANES]
        weight_grad_ref[:, width + at : width + at + LANES] = total[:, LANES:]


def between_kernel(
    info, query_grad, second_grad, first_unit, first_scale, norms, norm_sums, self_mix, pair_grad, cross_out_grad, out_weight, query_weight, *refs
):
    (
        first_grad_ref,
        mix_grad_ref,
        kept,
        sent,
        out_grad,
        query_weight_grad,
        norm_grad,
        norm_rows,
    ) = refs
    home = info[0]
    width = self_mix.shape[1]
    unit = first_unit[...]
    first_low = (unit * norms[0:1] + norms[3:4]).astype(LOW)
    low_grad = query_grad[...]
    query_weight_grad[...] = dot(first_low.T, low_grad).astype(LOW)
    cotangent = second_grad[...] + dot(low_grad, query_weight[...], BY_LANES)
    first_grad, gain_one, bias_one = norm_backward(
        cotangent, unit, first_scale[:, 0:1], norms[0:1]
    )
    first_grad_ref[...] = first_grad
    self_out_low = first_grad.astype(LOW)
    out_grad[...] = dot(self_mix[...].T, self_out_low).astype(LOW)
    mix_grad_ref[...] = dot(self_out_low, out_weight[...], BY_LANES).astype(LOW)
    norm_rows[...] = jnp.zeros(norm_rows.shape, FULL)
    norm_rows[0:8] = norm_sums[...]
    norm_rows[0:1] = gain_one
    norm_rows[3:4] = bias_one
    norm_grad[...] = norm_rows[...].T.astype(LOW)
    pack_grad(out_grad, kept, sent, home, (0, 1))
    pack_grad(query_weight_grad, kept, sent, home, (width, 1))
    pack_grad(pair_grad, kept, sent, home, (2 * width, 1))
    pack_grad(cross_out_grad, kept, sent, home, (4 * width, 1))
    pack_grad(norm_grad, kept, sent, home, (5 * width, 1))


def self_backward_kernel(
    info,
    query,
    key,
    value,
    kept_weights,
    inverse,
    mix,
    grad,
    rows_0,
    rows_1,
    rows_2,
    rows_3,
    made,
    query_grad_ref,
    kept,
    sent,
    value_wide,
    query_grads,
    weight_grad,
):
    pair = pl.program_id(0)
    width = rows_0.shape[1]
    pairs = made.shape[0]

    @pl.when(pair == 0)
    def _():
        value_wide[:, LANES:] = jnp.ones((value_wide.shape[0], LANES), LOW)

    query_grads[pair] = attend_back_pair(
        query[...], key[...], value[...], kept_weights, inverse[...], mix[...], grad[...], value_wide, made.at[pair]
    )

    @pl.when(pair == pairs - 1)
    def _():
        finish_weight(made, (rows_0, rows_1, rows_2, rows_3), weight_grad, width)
        low_grad = jnp.concatenate([query_grads[at] for at in range(pairs)], axis=1)
        query_grad_ref[...] = low_grad
        weight_grad[:, 0:width] = dot(rows_0[...].T, low_grad).astype(LOW)
        pack_grad(weight_grad, kept, sent, info[0], (0, 1))


def states_kernel(made, query_grad, first_grad, weight, own_ref, far_ref, core_ref):
    width = own_ref.shape[1]
    finish_rows(made, weight, width, own_ref, far_ref, core_ref)
    own_ref[...] += first_grad[...] + dot(query_grad[...], weight[:, 0:width], BY_LANES)


def whole(shape):
    return pl.BlockSpec(shape, lambda *at: (0,) * len(shape))


def call(kernel, inputs, specs, outputs, out_specs, scratch, grid=(), micros=1, mib=58):
    moved = sum(math.prod(a.shape) * a.dtype.itemsize for a in list(inputs) + list(outputs))
    return pl.pallas_call(
        kernel,
        out_shape=outputs,
        grid=grid,
        in_specs=specs,
        out_specs=out_specs,
        scratch_shapes=scratch,
        compiler_params=pltpu.CompilerParams(vmem_limit_bytes=mib * 2**20),
        cost_estimate=pl.CostEstimate(flops=micros * 10**9, bytes_accessed=moved, transcendentals=0),
    )(*inputs)


SCALARS = pl.BlockSpec(memory_space=pltpu.SMEM)


def shaped(shape, kind):
    return jax.ShapeDtypeStruct(shape, kind)


def per_device(
    target_states,
    memory,
    target_lengths,
    source_lengths,
    self_project,
    self_output,
    cross_project,
    memory_project,
    cross_output,
    expand_weight,
    contract_weight,
    norm_gain,
    norm_bias,
    out_grad,
):
    _, local, width = target_states.shape
    states = target_states[0]
    own_memory = memory[0]
    rows = self_project.shape[0]
    ff = expand_weight.shape[1]
    keys = local * 4
    pairs = width // LANES
    info = jnp.stack([home_number(), lax.axis_index("narrow")]).astype(jnp.int32)

    batches = 3 * width, 5 * width + LANES, 2 * ff
    if staged():
        shards = (
            self_output,
            cross_project,
            memory_project,
            cross_output,
            expand_weight,
            contract_weight,
            norm_gain,
            norm_bias,
        )
        later = batches[1] + batches[2]
        batch_23 = call(
            pack_kernel,
            list(shards),
            [whole(shard.shape) for shard in shards],
            [shaped((rows, later), LOW)],
            [whole((rows, later))],
            [pltpu.VMEM((LANES, LANES), FULL)],
        )[0]
        far_1 = jnp.stack(gather_far(self_project))
        states_x = exchange(states, 2)
        states_c = exchange(states, 1)
        (batch_23, states_c), far_1 = after((batch_23, states_c), far_1)
        near_23 = exchange(batch_23, FAR[0])
        plane_1 = gather_plane(far_1)
        (own_memory, near_23), states_x = after((own_memory, near_23), states_x)
        half_2 = jnp.stack([batch_23[:, : batches[1]], near_23[:, : batches[1]]])
        half_3 = jnp.stack([batch_23[:, batches[1] :], near_23[:, batches[1] :]])
        rest_2 = exchange(half_2, FAR[1])
        memory_x = exchange(own_memory, 2)
        half_3, rest_2 = after(half_3, rest_2)
        far_2 = jnp.concatenate([half_2, rest_2])
        rest_3 = exchange(half_3, FAR[1])
    else:
        norm_shard = jnp.concatenate([norm_gain, norm_bias], axis=0).T
        norm_shard = jnp.pad(norm_shard, ((0, 0), (0, LANES - norm_shard.shape[1])))
        folded = fold_rows(contract_weight, rows)
        plane_1 = self_project
        far_2 = jnp.concatenate(
            [self_output, cross_project, memory_project, cross_output, norm_shard], axis=1
        )
        far_3 = jnp.concatenate([expand_weight, folded], axis=1)
        states_x = exchange(states, 2)
        states_c = exchange(states, 1)
        memory_c = exchange(own_memory, 1)
        memory_x = exchange(own_memory, 2)
    states_xc = exchange(states_x, 1)
    far_2, plane_1 = after(far_2, plane_1)
    weights_1 = gather_core(plane_1)
    row_states = [states, states_c, states_x, states_xc]
    own_2 = exchange(far_2, 1) if staged() else None
    if staged():
        weights_1, own_2 = after(weights_1, own_2)
    plane_2 = gather_plane(far_2)

    row_spec = whole((local, width))
    pair_rows = pl.BlockSpec((local, LANES), lambda pair: (0, pair))
    pair_keys = pl.BlockSpec((keys, LANES), lambda pair: (0, pair))
    pair_kept = pl.BlockSpec((2, local, keys), lambda pair: (pair, 0, 0))
    quarter_specs_1 = [whole(q.shape) for q in weights_1]
    attend_scratch = [
        pltpu.VMEM((pairs, local, LANES), LOW),
        pltpu.VMEM((local, LANES), LOW),
        pltpu.VMEM((pairs, keys, 2 * LANES), LOW),
        pltpu.VMEM((pairs, keys, 2 * LANES), LOW),
        pltpu.VMEM((2, local, keys), FULL),
    ]
    attend_outputs = [
        shaped((local, width), LOW),
        pltpu.HBM((local, width), LOW),
        pltpu.HBM((local, width), FULL),
        pltpu.HBM((keys, width), LOW),
        pltpu.HBM((keys, width), LOW),
        pltpu.HBM((2 * pairs, local, keys), LOW),
    ]
    attend_specs = [pair_rows, pair_rows, pair_rows, pair_keys, pair_keys, pair_kept]
    in_place = pl.BlockSpec(memory_space=pl.ANY)
    self_mix, self_query, self_inverse, self_key, self_value, self_kept, self_weight = call(
        self_forward_kernel,
        [info, target_lengths, *row_states, *weights_1],
        [SCALARS, SCALARS] + [row_spec] * 4 + quarter_specs_1,
        attend_outputs + [pltpu.HBM((width, 3 * width), LOW)],
        attend_specs + [in_place],
        [pltpu.VMEM((width, 3 * width), LOW), pltpu.SemaphoreType.DMA] + attend_scratch,
        grid=(pairs,),
        micros=25, mib=38,
    )

    if staged():
        (memory_x, own_memory, rest_3), self_mix = after((memory_x, own_memory, rest_3), self_mix)
        memory_c = exchange(own_memory, 1)
        far_3 = jnp.concatenate([half_3, rest_3])
    plane_2, self_mix = after(plane_2, self_mix)
    own_3 = exchange(far_3, 1) if staged() else None
    memory_xc = exchange(memory_x, 1)
    weights_2 = gather_core(plane_2, own_2)
    row_memory = [own_memory, memory_c, memory_x, memory_xc]
    plane_3 = gather_plane(far_3)
    quarter_specs_2 = [whole(q.shape) for q in weights_2]
    wide_scale = whole((local, LANES))
    norm_spec = whole((8, width))
    square = whole((width, width))
    (
        cross_mix,
        cross_query,
        cross_inverse,
        cross_key,
        cross_value,
        cross_kept,
        first_unit,
        first_scale,
        norms,
        second_unit,
        second_scale,
        cross_out_weight,
        out_weight,
        query_weight,
        pair_weight,
    ) = call(
        cross_forward_kernel,
        [info, target_lengths, source_lengths, self_mix, states, *row_memory, *weights_2],
        [SCALARS] * 3 + [row_spec] * 6 + quarter_specs_2,
        attend_outputs
        + [
            pltpu.HBM((local, width), FULL),
            pltpu.HBM((local, LANES), FULL),
            shaped((8, width), FULL),
            shaped((local, width), FULL),
            shaped((local, LANES), FULL),
            shaped((width, width), LOW),
            pltpu.HBM((width, width), LOW),
            pltpu.HBM((width, width), LOW),
            pltpu.HBM((width, 2 * width), LOW),
        ],
        attend_specs + [row_spec, wide_scale, norm_spec, row_spec, wide_scale, square] + [in_place] * 3,
        [
            pltpu.VMEM((width, width), LOW),
            pltpu.VMEM((width, width), LOW),
            pltpu.VMEM((width, 2 * width), LOW),
            pltpu.VMEM((width, LANES), LOW),
            pltpu.SemaphoreType.DMA((3,)),
            pltpu.VMEM((pairs, local, LANES), LOW),
        ]
        + attend_scratch,
        grid=(pairs,),
        micros=25, mib=46,
    )

    plane_3, second_unit = after(plane_3, second_unit)
    weights_3 = gather_core(plane_3, own_3, ff // width)
    quarter_specs_3 = [whole(q.shape) for q in weights_3]
    chunk_count = ff // width
    packed_3 = (4, 4, TILE_ROWS, 2 * ff)
    hidden_shape = (chunk_count, local, width)
    output, third_grad, hidden_grads, expand_whole, norm_sums, kept_3, sent_3 = call(
        middle_kernel,
        [info, second_unit, norms, out_grad[0], *weights_3],
        [SCALARS, row_spec, norm_spec, row_spec] + quarter_specs_3,
        [
            shaped((local, width), FULL),
            shaped((local, width), FULL),
            shaped(hidden_shape, LOW),
            shaped((width, ff), LOW),
            shaped((8, width), FULL),
            shaped(packed_3, LOW),
            shaped(packed_3, LOW),
        ],
        [row_spec, row_spec, whole(hidden_shape), whole((width, ff)), norm_spec]
        + [whole(packed_3), whole(packed_3)],
        [
            pltpu.VMEM((ff, width), LOW),
            pltpu.VMEM(hidden_shape, LOW),
            pltpu.VMEM(hidden_shape, FULL),
            pltpu.VMEM((width, ff), LOW),
            pltpu.VMEM((ff, width), LOW),
        ],
        micros=14, mib=36,
    )
    other_3 = exchange_core(sent_3)
    second_grad, cross_mix_grad, cross_out_grad, norm_sums = call(
        second_back_kernel,
        [
            third_grad,
            hidden_grads,
            expand_whole,
            second_unit,
            second_scale,
            norms,
            norm_sums,
            cross_mix,
            cross_out_weight,
        ],
        [row_spec, whole(hidden_shape), whole((width, ff))]
        + [row_spec, wide_scale, norm_spec, norm_spec, row_spec, square],
        [
            shaped((local, width), FULL),
            shaped((local, width), LOW),
            shaped((width, width), LOW),
            shaped((8, width), FULL),
        ],
        [row_spec, row_spec, square, norm_spec],
        [],
        micros=4, mib=12,
    )
    other_3, cross_mix_grad = after(other_3, cross_mix_grad)
    core_3 = reduce_core(kept_3, other_3)
    core_3, cross_mix_grad = after(core_3, cross_mix_grad)
    planes_3 = exchange_plane(core_3)

    back_scratch = [
        pltpu.VMEM((keys, 2 * LANES), LOW),
        pltpu.VMEM((pairs, 2 * LANES, keys), LOW),
    ]
    back_specs = [pair_rows, pair_keys, pair_keys, pair_kept, pair_rows, pair_rows, pair_rows]
    parts_shape = (2, local, width)
    cross_query_grad, pair_weight_grad, memory_own, memory_far_part, memory_parts = call(
        cross_backward_kernel,
        [
            cross_query,
            cross_key,
            cross_value,
            cross_kept,
            cross_inverse,
            cross_mix,
            cross_mix_grad,
            *row_memory,
            pair_weight,
        ],
        back_specs + [row_spec] * 4 + [whole((width, 2 * width))],
        [
            shaped((local, width), LOW),
            shaped((width, 2 * width), LOW),
            shaped((local, width), FULL),
            shaped((local, width), LOW),
            shaped(parts_shape, LOW),
        ],
        [pair_rows, whole((width, 2 * width)), row_spec, row_spec, whole(parts_shape)],
        back_scratch,
        grid=(pairs,),
        micros=33, mib=36,
    )
    (planes_3, memory_parts), cross_query_grad = after((planes_3, memory_parts), cross_query_grad)
    plane_sum_3 = reduce_plane(planes_3)
    memory_sent = exchange(memory_parts, 1)
    plane_sum_3, cross_query_grad = after(plane_sum_3, cross_query_grad)
    half_sum_3 = exchange_half(plane_sum_3)

    packed_2 = (4, 4, TILE_ROWS, 5 * width + LANES)
    first_grad, self_mix_grad, kept_2, sent_2 = call(
        between_kernel,
        [
            info,
            cross_query_grad,
            second_grad,
            first_unit,
            first_scale,
            norms,
            norm_sums,
            self_mix,
            pair_weight_grad,
            cross_out_grad,
            out_weight,
            query_weight,
        ],
        [SCALARS, row_spec, row_spec, row_spec, whole((local, LANES))]
        + [whole((8, width))] * 2
        + [row_spec, whole((width, 2 * width)), whole((width, width))]
        + [square] * 2,
        [
            shaped((local, width), FULL),
            shaped((local, width), LOW),
            shaped(packed_2, LOW),
            shaped(packed_2, LOW),
        ],
        [row_spec, row_spec, whole(packed_2), whole(packed_2)],
        [
            pltpu.VMEM((width, width), LOW),
            pltpu.VMEM((width, width), LOW),
            pltpu.VMEM((width, LANES), LOW),
            pltpu.VMEM((LANES, width), FULL),
        ],
        micros=6, mib=14,
    )
    other_2 = exchange_core(sent_2)
    core_2 = reduce_core(kept_2, other_2)
    memory_other = reduce_row_core(memory_far_part, memory_sent)
    (core_2, memory_other), self_mix_grad = after((core_2, memory_other), self_mix_grad)
    planes_2 = exchange_plane(core_2)
    memory_far = exchange(memory_other, 2)

    packed_1 = (4, 4, TILE_ROWS, 3 * width)
    made_shape = (pairs, 2 * LANES, keys)
    made, self_query_grad, kept_1, sent_1 = call(
        self_backward_kernel,
        [
            info,
            self_query,
            self_key,
            self_value,
            self_kept,
            self_inverse,
            self_mix,
            self_mix_grad,
            *row_states,
        ],
        [SCALARS] + back_specs + [row_spec] * 4,
        [
            shaped(made_shape, LOW),
            shaped((local, width), LOW),
            shaped(packed_1, LOW),
            shaped(packed_1, LOW),
        ],
        [whole(made_shape), row_spec, whole(packed_1), whole(packed_1)],
        [
            pltpu.VMEM((keys, 2 * LANES), LOW),
            pltpu.VMEM((pairs, local, LANES), LOW),
            pltpu.VMEM((width, 3 * width), LOW),
        ],
        grid=(pairs,),
        micros=33, mib=36,
    )
    (planes_2, memory_far, half_sum_3), (sent_1, kept_1) = after(
        (planes_2, memory_far, half_sum_3), (sent_1, kept_1)
    )
    other_1 = exchange_core(sent_1)
    states_own, states_far_part, states_parts = call(
        states_kernel,
        [made, self_query_grad, first_grad, self_weight],
        [whole(made_shape), row_spec, row_spec, whole((width, 3 * width))],
        [
            shaped((local, width), FULL),
            shaped((local, width), LOW),
            shaped(parts_shape, LOW),
        ],
        [row_spec, row_spec, whole(parts_shape)],
        [],
        micros=4, mib=20,
    )
    other_1, states_parts = after(other_1, states_parts)
    core_1 = reduce_core(kept_1, other_1)
    planes_1 = exchange_plane(core_1)
    states_sent = exchange(states_parts, 1)
    (planes_2, half_sum_3, memory_far), core_1 = after((planes_2, half_sum_3, memory_far), core_1)
    plane_sum_2 = reduce_plane(planes_2)
    half_sum_2 = exchange_half(plane_sum_2)
    states_other = reduce_row_core(states_far_part, states_sent)
    (half_sum_2, half_sum_3), states_other = after((half_sum_2, half_sum_3), states_other)
    states_far = exchange(states_other, 2)
    total_3 = reduce_half(plane_sum_3, half_sum_3)
    total_2 = reduce_half(plane_sum_2, half_sum_2)
    planes_1, (total_2, total_3, states_other) = after(planes_1, (total_2, total_3, states_other))
    plane_sum_1 = reduce_plane(planes_1)
    fars_1 = exchange_far(plane_sum_1)
    memory_grad = reduce_row(memory_own, memory_sent, memory_far)
    states_grad = reduce_row(states_own, states_sent, states_far)
    count = norm_gain.shape[0]
    if staged():
        near = exchange(jnp.concatenate([total_2[1], total_3[1]], axis=1), FAR[0])
        settled = [
            shaped((rows, width), FULL),
            shaped((rows, width), FULL),
            shaped((rows, 2 * width), FULL),
            shaped((rows, width), FULL),
            shaped((rows, ff), FULL),
            shaped((rows * ff // width, width), FULL),
            shaped(norm_gain.shape, FULL),
            shaped(norm_gain.shape, FULL),
        ]
        out, cross, pairs_grad, cross_out, expand_grad, contract_grad, gain, bias = call(
            settle_kernel,
            [total_2[0], total_3[0], near],
            [whole((rows, batches[1])), whole((rows, batches[2])), whole((rows, later))],
            settled,
            [whole(each.shape) for each in settled],
            [pltpu.VMEM((LANES, LANES), FULL)],
        )
        fars_1, out = after(fars_1, out)
        project = reduce_far(fars_1)
    else:
        grad_3 = reduce_far(total_3, ff // width)
        grad_2 = reduce_far(total_2)
        project = reduce_far(fars_1)
        expand_grad, contract_grad = grad_3[:, :ff], unfold_rows(grad_3[:, ff:], width)
        out, cross = grad_2[:, :width], grad_2[:, width : 2 * width]
        pairs_grad, cross_out = grad_2[:, 2 * width : 4 * width], grad_2[:, 4 * width : 5 * width]
        norm_grads = grad_2[:, 5 * width :].T
        gain, bias = norm_grads[:count], norm_grads[count : 2 * count]
    return (
        output[None],
        states_grad[None],
        memory_grad[None],
        project,
        out,
        cross,
        pairs_grad,
        cross_out,
        expand_grad,
        contract_grad,
        gain,
        bias,
    )


def reduce_row_core(part, sent):
    return add_all(part, [sent[1]]).astype(LOW)


def reduce_row(own, sent, far):
    return add_all(own, [sent[0], far])


def solution(mesh):
    in_specs = (
        P("wide", "narrow", None),
        P("wide", "narrow", None),
        P("wide", None),
        P("wide", None),
        P(("wide", "narrow"), None),
        P(("wide", "narrow"), None),
        P(("wide", "narrow"), None),
        P(("wide", "narrow"), None),
        P(("wide", "narrow"), None),
        P(("wide", "narrow"), None),
        P(("wide", "narrow"), None),
        P(None, ("wide", "narrow")),
        P(None, ("wide", "narrow")),
        P("wide", "narrow", None),
    )
    out_specs = (
        P("wide", "narrow", None),
        P("wide", "narrow", None),
        P("wide", "narrow", None),
        P(("wide", "narrow"), None),
        P(("wide", "narrow"), None),
        P(("wide", "narrow"), None),
        P(("wide", "narrow"), None),
        P(("wide", "narrow"), None),
        P(("wide", "narrow"), None),
        P(("wide", "narrow"), None),
        P(None, ("wide", "narrow")),
        P(None, ("wide", "narrow")),
    )
    return jax.shard_map(
        per_device, mesh=mesh, in_specs=in_specs, out_specs=out_specs, check_vma=False
    )
```

```python
import functools
import math

import jax
import jax.numpy as jnp
from jax import lax
from jax.experimental import pallas as pl
from jax.experimental.pallas import tpu as pltpu
from jax.sharding import PartitionSpec as P

HEAD_DIM = 64
LANES = 128
TILE_ROWS = 16
BLOCKS = 32
AXES = ("wide", "narrow")
LOW = jnp.bfloat16
FULL = jnp.float32

ln_eps = 1e-05
score_scale = HEAD_DIM ** (-0.5)
mask_step = -(2.0**30)

BY_LANES = (((1,), (1,)), ((), ()))
PLAIN = (((1,), (0,)), ((), ()))


def dot(left, right, dims=PLAIN):
    return lax.dot_general(left, right, dims, preferred_element_type=FULL)


def exchange(block, mask):
    device_count = lax.axis_size("wide") * lax.axis_size("narrow")
    pairs = [(device, device ^ mask) for device in range(device_count)]
    return lax.ppermute(block, AXES, pairs)


def device_number():
    return lax.axis_index("wide") * lax.axis_size("narrow") + lax.axis_index("narrow")


def staged():
    return lax.axis_size("wide") * lax.axis_size("narrow") == BLOCKS


FAR = (8, 16, 24)
PLANE = (2, 4, 6)


def gather_far(shard):
    if not staged():
        return shard
    return [shard] + [exchange(shard, mask) for mask in FAR]


def gather_plane(held):
    if not staged():
        return held
    return [held] + [exchange(held, mask) for mask in PLANE]


def gather_core(held, own=None, folds=0):
    if staged():
        first = exchange(held[0], 1) if own is None else own
        return held + [first] + [exchange(quarter, 1) for quarter in held[1:]]
    whole = lax.all_gather(held, AXES, axis=0, tiled=True)
    if folds:
        rows, columns = held.shape
        split = columns - folds * whole.shape[0]
        tall = unfold_rows(held[:, split:], whole.shape[0])
        tall = lax.all_gather(tall, AXES, axis=0, tiled=True)
        tall = tall.reshape(BLOCKS, folds, TILE_ROWS, -1).transpose(0, 2, 1, 3)
        whole = jnp.concatenate([whole[:, :split], tall.reshape(whole.shape[0], -1)], axis=1)
    whole = whole.reshape(4, 4, 2, TILE_ROWS, held.shape[1]).transpose(2, 1, 0, 3, 4)
    return [whole[core, plane] for core in range(2) for plane in range(4)]


def home_number():
    return device_number() if staged() else jnp.zeros((), jnp.int32)


def block_number(home, core, plane, far):
    return home ^ (far * 8 + plane * 2 + core)


def add_all(first, others):
    total = first.astype(FULL)
    for other in others:
        total = total + other.astype(FULL)
    return total


def exchange_core(sent):
    return exchange(sent, 1) if staged() else sent


def reduce_core(kept, other):
    return add_all(kept, [other]).astype(LOW) if staged() else (kept, other)


def exchange_plane(held):
    if not staged():
        return held
    return [held[0]] + [exchange(held[plane + 1], mask) for plane, mask in enumerate(PLANE)]


def reduce_plane(planes):
    return add_all(planes[0], planes[1:]).astype(LOW) if staged() else planes


def exchange_far(held):
    if not staged():
        return held
    return [held[0]] + [exchange(held[far + 1], mask) for far, mask in enumerate(FAR)]


def exchange_half(held):
    return exchange(held[2:], FAR[1]) if staged() else held


def reduce_half(held, other):
    return add_all(held[:2], [other]).astype(LOW) if staged() else held


def reduce_far(held, folds=0):
    if staged():
        return add_all(held[0], held[1:])
    whole = jnp.stack(held).transpose(2, 1, 0, 3, 4)
    whole = whole.reshape(BLOCKS * TILE_ROWS, -1).astype(FULL)
    if folds:
        split = whole.shape[1] - folds * whole.shape[0]
        tall = whole[:, split:].reshape(BLOCKS, TILE_ROWS, folds, -1).transpose(0, 2, 1, 3)
        tall = tall.reshape(folds * whole.shape[0], -1)
        tall = lax.psum_scatter(tall, AXES, scatter_dimension=0, tiled=True)
        whole = lax.psum_scatter(whole[:, :split], AXES, scatter_dimension=0, tiled=True)
        return jnp.concatenate([whole, fold_rows(tall, whole.shape[0])], axis=1)
    return lax.psum_scatter(whole, AXES, scatter_dimension=0, tiled=True)


def after(values, token):
    return lax.optimization_barrier((values, token))


def fold_rows(block, rows):
    return jnp.concatenate(
        [block[at : at + rows] for at in range(0, block.shape[0], rows)], axis=1
    )


def unfold_rows(block, width):
    return jnp.concatenate(
        [block[:, at : at + width] for at in range(0, block.shape[1], width)], axis=0
    )


def lane_numbers(shape):
    return lax.broadcasted_iota(jnp.int32, shape, 1)


def segment_bounds(lengths_ref):
    lane = lane_numbers((1, LANES))
    first = jnp.full((1, LANES), 2**30, jnp.int32)
    last = jnp.zeros((1, LANES), jnp.int32)
    start = jnp.int32(0)
    count = lengths_ref.shape[1]
    for segment in range(count + 1):
        end = start + lengths_ref[0, segment] if segment < count else jnp.int32(2**30)
        first = jnp.where(lane == segment, start, first)
        last = jnp.where(lane == segment, end, last)
        start = end
    return first, last


def segment_flags(start, rows, bounds):
    position = start + lax.broadcasted_iota(jnp.int32, (rows, LANES), 0)
    return (position >= bounds[0]) & (position < bounds[1])


def three_parts(value):
    first = value.astype(LOW)
    rest = value - first.astype(FULL)
    second = rest.astype(LOW)
    third = (rest - second.astype(FULL)).astype(LOW)
    return first.astype(FULL), second.astype(FULL), third.astype(FULL)


def query_flags(lengths_ref, start, rows):
    segments = lengths_ref.shape[1] + 1
    own = segment_flags(start, rows, segment_bounds(lengths_ref))
    return jnp.where(own | (lane_numbers((rows, LANES)) >= segments), 0.0, mask_step).astype(LOW)


def key_flags(lengths_ref, start, rows):
    own = segment_flags(start, rows, segment_bounds(lengths_ref))
    return jnp.where(own, 1.0, 0.0).astype(LOW)


def fill_weight(target, quarters, home, columns):
    first, folds = columns
    width = target.shape[1]
    for core in range(2):
        for plane in range(4):
            for far in range(4):
                block = block_number(home, core, plane, far)
                piece = quarters[core * 4 + plane]
                for fold in range(folds):
                    row = pl.multiple_of(block * (TILE_ROWS * folds) + fold * TILE_ROWS, TILE_ROWS)
                    start = first + fold * width
                    target[pl.ds(row, TILE_ROWS), :] = piece[far, :, start : start + width]


def pack_grad(source, kept, sent, home, columns):
    first, folds = columns
    width = source.shape[1]
    for core, target in ((0, kept), (1, sent)):
        for plane in range(4):
            for far in range(4):
                block = block_number(home, core, plane, far)
                for fold in range(folds):
                    row = pl.multiple_of(block * (TILE_ROWS * folds) + fold * TILE_ROWS, TILE_ROWS)
                    start = first + fold * width
                    target[plane, far, :, start : start + width] = source[pl.ds(row, TILE_ROWS), :]


def normalise(states):
    centred = states - jnp.mean(states, axis=1, keepdims=True)
    spread = jnp.mean(centred * centred, axis=1, keepdims=True)
    scale = lax.rsqrt(spread + ln_eps)
    return centred * scale, scale


def norm_backward(cotangent, unit, scale, gain):
    scaled = cotangent * gain
    grad = scale * (
        scaled
        - jnp.mean(scaled, axis=1, keepdims=True)
        - unit * jnp.mean(scaled * unit, axis=1, keepdims=True)
    )
    return (
        grad,
        jnp.sum(cotangent * unit, axis=0, keepdims=True),
        jnp.sum(cotangent, axis=0, keepdims=True),
    )


KEY_STEP = 256


def pack_kernel(*refs):
    ins, (packed, square) = refs[:8], refs[8:]
    self_output, cross_project, memory_project, cross_output, expand, contract, gain, bias = ins
    rows, width = self_output.shape
    at = 0
    for part in (self_output, cross_project, memory_project, cross_output):
        packed[:, at : at + part.shape[1]] = part[...]
        at += part.shape[1]
    count = gain.shape[0]
    square[...] = jnp.zeros(square.shape, FULL)
    square[0:count, 0:rows] = gain[...].astype(FULL)
    square[count : 2 * count, 0:rows] = bias[...].astype(FULL)
    packed[:, at : at + LANES] = square[...].T[0:rows].astype(LOW)
    at += LANES
    packed[:, at : at + expand.shape[1]] = expand[...]
    at += expand.shape[1]
    for fold in range(contract.shape[0] // rows):
        packed[:, at : at + width] = contract[fold * rows : (fold + 1) * rows]
        at += width


def settle_kernel(part_2, part_3, other, *refs):
    output_ref, cross_ref, memory_ref, cross_out_ref, expand_ref, contract_ref, gain_ref, bias_ref, square = refs
    rows, width = output_ref.shape
    split = part_2.shape[1]
    total = add_all(part_2[...], [other[:, :split]])
    at = 0
    for ref in (output_ref, cross_ref, memory_ref, cross_out_ref):
        ref[...] = total[:, at : at + ref.shape[1]]
        at += ref.shape[1]
    square[...] = jnp.zeros(square.shape, FULL)
    square[0:rows] = total[:, at : at + LANES]
    turned = square[...].T
    count = gain_ref.shape[0]
    gain_ref[...] = turned[0:count, 0:rows]
    bias_ref[...] = turned[count : 2 * count, 0:rows]
    total = add_all(part_3[...], [other[:, split:]])
    span = expand_ref.shape[1]
    expand_ref[...] = total[:, :span]
    for fold in range(contract_ref.shape[0] // rows):
        at = span + fold * width
        contract_ref[fold * rows : (fold + 1) * rows] = total[:, at : at + width]


def attend_pair(query, flags, key_wide, value_wide, scores, kept):
    rows = query.shape[0]
    keys = key_wide.shape[0]
    left = lane_numbers((rows, LANES)) < HEAD_DIM
    zero = jnp.zeros_like(query)
    queries = [
        jnp.concatenate([jnp.where(left, query, zero), flags], axis=1),
        jnp.concatenate([jnp.where(left, zero, query), flags], axis=1),
    ]

    def score(head, start, peak):
        made = dot(queries[head], key_wide[start : start + KEY_STEP], BY_LANES)
        scores[head, :, start : start + KEY_STEP] = made
        for at in range(0, KEY_STEP, LANES):
            peak = jnp.maximum(peak, made[:, at : at + LANES])
        return peak

    def weigh(head, start, peak, total):
        span = slice(start, start + KEY_STEP)
        weights = jnp.exp(scores[head, :, span] - peak).astype(LOW)
        kept[head, :, span] = weights
        return total + dot(weights, value_wide[span])

    steps = range(0, keys, KEY_STEP)
    lowest = jnp.full((rows, LANES), -jnp.inf, FULL)
    empty = jnp.zeros((rows, 2 * LANES), FULL)
    peak = lowest
    for start in steps:
        peak = score(0, start, peak)
    first_peak = jnp.max(peak, axis=1, keepdims=True)
    peak, first = lowest, empty
    for start in steps:
        peak = score(1, start, peak)
        first = weigh(0, start, first_peak, first)
    second_peak = jnp.max(peak, axis=1, keepdims=True)
    second = empty
    for start in steps:
        second = weigh(1, start, second_peak, second)
    inverse = 1.0 / jnp.where(left, first[:, LANES:], second[:, LANES:])
    mix = jnp.where(left, first[:, :LANES], second[:, :LANES]) * inverse
    return mix, inverse


def pair_columns(first, pair):
    return pl.ds(pl.multiple_of(first + pair * LANES, LANES), LANES)


def prepare_wide(lengths, key_wide, value_wide, place):
    pairs, keys, _ = key_wide.shape
    local = keys // 4
    ones = jnp.ones((local, LANES), LOW)
    for step in range(4):
        span = slice(step * local, (step + 1) * local)
        flags = key_flags(lengths, (place ^ step) * local, local)
        for pair in range(pairs):
            key_wide[pair, span, LANES:] = flags
            value_wide[pair, span, LANES:] = ones


def project_rows(rows, weight, key_wide, value_wide):
    pairs = key_wide.shape[0]
    local = rows[0].shape[0]
    for step, part in enumerate(rows):
        span = slice(step * local, (step + 1) * local)
        for wide, first in ((key_wide, 0), (value_wide, pairs * LANES)):
            made = dot(part[...], weight[:, first : first + pairs * LANES]).astype(LOW)
            for pair in range(pairs):
                wide[pair, span, :LANES] = made[:, pair * LANES : (pair + 1) * LANES]


def project_queries(rows, weight, queries):
    made = dot(rows, weight).astype(LOW).astype(FULL) * score_scale
    for pair in range(queries.shape[0]):
        queries[pair] = made[:, pair * LANES : (pair + 1) * LANES].astype(LOW)


def self_forward_kernel(info, lengths, rows_0, rows_1, rows_2, rows_3, *refs):
    quarters = refs[:8]
    (
        mix_ref,
        query_ref,
        exact_ref,
        inverse_ref,
        key_ref,
        value_ref,
        kept,
        weight_ref,
        weight,
        saved,
        queries,
        flags_q,
        key_wide,
        value_wide,
        scores,
    ) = refs[8:]
    pair = pl.program_id(0)
    home, place = info[0], info[1]
    local, width = rows_0.shape

    @pl.when(pair == 0)
    def _():
        fill_weight(weight, quarters, home, (0, 1))
        pltpu.make_async_copy(weight, weight_ref, saved).start()
        flags_q[...] = query_flags(lengths, place * local, local)
        prepare_wide(lengths, key_wide, value_wide, place)
        project_rows((rows_0, rows_1, rows_2, rows_3), weight.at[:, width:], key_wide, value_wide)
        project_queries(rows_0[...], weight[:, :width], queries)

    query = queries[pair]
    query_ref[...] = query
    key_ref[...] = key_wide[pair, :, :LANES]
    value_ref[...] = value_wide[pair, :, :LANES]
    mix, inverse = attend_pair(
        query, flags_q[...], key_wide.at[pair], value_wide.at[pair], scores, kept
    )
    mix_ref[...] = mix.astype(LOW)
    exact_ref[...] = mix
    inverse_ref[...] = inverse

    @pl.when(pair == queries.shape[0] - 1)
    def _():
        pltpu.make_async_copy(weight, weight_ref, saved).wait()


def cross_forward_kernel(
    info, target_lengths, source_lengths, mix, states, rows_0, rows_1, rows_2, rows_3, *refs
):
    quarters = refs[:8]
    (
        mix_ref,
        query_ref,
        exact_ref,
        inverse_ref,
        key_ref,
        value_ref,
        kept,
        unit_ref,
        scale_ref,
        norms_ref,
        second_unit_ref,
        second_scale_ref,
        cross_out_ref,
        out_weight_ref,
        query_weight_ref,
        pair_weight_ref,
        out_weight,
        query_weight,
        pair_weight,
        norm_rows,
        saved,
        mixes,
        queries,
        flags_q,
        key_wide,
        value_wide,
        scores,
    ) = refs[8:]
    pair = pl.program_id(0)
    home, place = info[0], info[1]
    local, width = rows_0.shape

    copies = [
        pltpu.make_async_copy(source, target, saved.at[at])
        for at, (source, target) in enumerate(
            (
                (out_weight, out_weight_ref),
                (query_weight, query_weight_ref),
                (pair_weight, pair_weight_ref),
            )
        )
    ]

    @pl.when(pair == 0)
    def _():
        fill_weight(out_weight, quarters, home, (0, 1))
        fill_weight(query_weight, quarters, home, (width, 1))
        fill_weight(pair_weight, quarters, home, (2 * width, 1))
        for copy in copies:
            copy.start()
        fill_weight(cross_out_ref, quarters, home, (4 * width, 1))
        fill_weight(norm_rows, quarters, home, (5 * width, 1))
        norms = norm_rows[...].astype(FULL).T[0:8]
        norms_ref[...] = norms
        mixed = states[...].astype(FULL) + dot(mix[...], out_weight[...])
        unit, scale = normalise(mixed)
        unit_ref[...] = unit
        scale_ref[...] = jnp.broadcast_to(scale, (local, LANES))
        first_low = (unit * norms[0:1] + norms[3:4]).astype(LOW)
        project_queries(first_low, query_weight[...], queries)
        flags_q[...] = query_flags(target_lengths, place * local, local)
        prepare_wide(source_lengths, key_wide, value_wide, place)
        project_rows((rows_0, rows_1, rows_2, rows_3), pair_weight, key_wide, value_wide)

    query = queries[pair]
    query_ref[...] = query
    key_ref[...] = key_wide[pair, :, :LANES]
    value_ref[...] = value_wide[pair, :, :LANES]
    mixed, inverse = attend_pair(
        query, flags_q[...], key_wide.at[pair], value_wide.at[pair], scores, kept
    )
    mix_ref[...] = mixed.astype(LOW)
    exact_ref[...] = mixed
    inverse_ref[...] = inverse
    mixes[pair] = mixed.astype(LOW)

    @pl.when(pair == mixes.shape[0] - 1)
    def _():
        first_norm = unit_ref[...] * norms_ref[0:1] + norms_ref[3:4]
        whole_mix = jnp.concatenate([mixes[at] for at in range(mixes.shape[0])], axis=1)
        second_unit, second_scale = normalise(first_norm + dot(whole_mix, cross_out_ref[...]))
        second_unit_ref[...] = second_unit
        second_scale_ref[...] = jnp.broadcast_to(second_scale, (local, LANES))
        for copy in copies:
            copy.wait()


gelu_factor = 0.7978845608028654
gelu_cubic = 0.044715


def gelu_and_slope(hidden):
    square = hidden * hidden
    bend = jnp.tanh(gelu_factor * (hidden + gelu_cubic * (square * hidden)))
    half = 0.5 * (1.0 + bend)
    slope = half + (0.5 * hidden) * (1.0 - bend * bend) * (
        gelu_factor * (1.0 + (3.0 * gelu_cubic) * square)
    )
    return hidden * half, slope


def middle_kernel(info, second_unit, norms, out_grad, *refs):
    quarters = refs[:8]
    (
        output_ref,
        third_grad_ref,
        hidden_grads,
        expand,
        norm_sums_ref,
        kept,
        sent,
        contract,
        active,
        slope,
        wide_grad,
        tall_grad,
    ) = refs[8:]
    home = info[0]
    width = second_unit.shape[1]
    chunks = active.shape[0]
    span = expand.shape[1] // chunks
    fill_weight(expand, quarters, home, (0, 1))
    fill_weight(contract, quarters, home, (expand.shape[1], contract.shape[0] // width))
    second_norm = second_unit[...] * norms[1:2] + norms[4:5]
    second_low = second_norm.astype(LOW)

    def forward(at, total):
        start = pl.multiple_of(at * span, span)
        hidden = dot(second_low, expand[:, pl.ds(start, span)])
        made, bent = gelu_and_slope(hidden)
        made = made.astype(LOW)
        active[at] = made
        slope[at] = bent
        return total + dot(made, contract[pl.ds(start, span)])

    mixed = lax.fori_loop(0, chunks, forward, second_norm, unroll=True)
    third_unit, third_scale = normalise(mixed)
    output_ref[...] = third_unit * norms[2:3] + norms[5:6]
    third_grad, gain_three, bias_three = norm_backward(
        out_grad[...], third_unit, third_scale, norms[2:3]
    )
    third_grad_ref[...] = third_grad
    ffn_grad = third_grad.astype(LOW)
    second_turned = second_low.T

    def backward(at, carry):
        start = pl.multiple_of(at * span, span)
        part = contract[pl.ds(start, span)]
        hidden_grad = (dot(ffn_grad, part, BY_LANES) * slope[at]).astype(LOW)
        hidden_grads[at] = hidden_grad
        tall_grad[pl.ds(start, span)] = dot(active[at].T, ffn_grad).astype(LOW)
        wide_grad[:, pl.ds(start, span)] = dot(second_turned, hidden_grad).astype(LOW)
        return carry

    lax.fori_loop(0, chunks, backward, 0, unroll=True)
    norm_sums_ref[...] = jnp.zeros(norm_sums_ref.shape, FULL)
    norm_sums_ref[2:3] = gain_three
    norm_sums_ref[5:6] = bias_three
    pack_grad(wide_grad, kept, sent, home, (0, 1))
    pack_grad(tall_grad, kept, sent, home, (expand.shape[1], tall_grad.shape[0] // width))


def second_back_kernel(
    third_grad,
    hidden_grads,
    expand,
    second_unit,
    second_scale,
    norms,
    sums,
    mix,
    out_weight,
    second_grad_ref,
    mix_grad_ref,
    out_weight_grad,
    norm_sums_ref,
):
    cotangent = third_grad[...]
    chunks = hidden_grads.shape[0]
    span = expand.shape[1] // chunks
    for at in range(chunks):
        part = expand[:, at * span : (at + 1) * span]
        cotangent = cotangent + dot(hidden_grads[at], part, BY_LANES)
    second_grad, gain_two, bias_two = norm_backward(
        cotangent, second_unit[...], second_scale[:, 0:1], norms[1:2]
    )
    second_grad_ref[...] = second_grad
    cross_out_low = second_grad.astype(LOW)
    mix_grad_ref[...] = dot(cross_out_low, out_weight[...], BY_LANES).astype(LOW)
    out_weight_grad[...] = dot(mix[...].T, cross_out_low).astype(LOW)
    norm_sums_ref[...] = sums[...]
    norm_sums_ref[1:2] = gain_two
    norm_sums_ref[4:5] = bias_two


def attend_back_pair(query, key, value, kept, inverse, mix, grad, value_wide, made):
    rows = grad.shape[0]
    left = lane_numbers((rows, LANES)) < HEAD_DIM
    lane = lane_numbers((rows, LANES))
    value_wide[:, :LANES] = value
    low_grad = (grad.astype(FULL) * inverse).astype(LOW)
    product = low_grad.astype(FULL) * mix
    query_turned = query.T
    grad_turned = low_grad.T
    query_grads = []
    for head in range(2):
        mine = left if head == 0 else ~left
        inner = -jnp.sum(jnp.where(mine, product, 0.0), axis=1, keepdims=True)
        first, second, third = three_parts(inner)
        parts = jnp.where(lane == 0, first, jnp.where(lane == 1, second, jnp.where(lane == 2, third, 0.0)))
        wide = jnp.concatenate([jnp.where(mine, low_grad, jnp.zeros_like(low_grad)), parts.astype(LOW)], axis=1)
        weights = kept[head]
        shifted = dot(wide, value_wide[...], BY_LANES)
        score_grad = (weights.astype(FULL) * shifted).astype(LOW)
        query_grads.append(dot(score_grad, key))
        span = slice(head * HEAD_DIM, (head + 1) * HEAD_DIM)
        made[span] = dot(query_turned[span], score_grad).astype(LOW)
        made[LANES + head * HEAD_DIM : LANES + (head + 1) * HEAD_DIM] = dot(
            grad_turned[span], weights
        ).astype(LOW)
    return (jnp.where(left, query_grads[0], query_grads[1]) * score_scale).astype(LOW)


def cross_backward_kernel(
    query,
    key,
    value,
    kept,
    inverse,
    mix,
    grad,
    rows_0,
    rows_1,
    rows_2,
    rows_3,
    made,
    query_grad_ref,
    weight_grad_ref,
    value_wide,
):
    pair = pl.program_id(0)

    @pl.when(pair == 0)
    def _():
        value_wide[:, LANES:] = jnp.ones((value_wide.shape[0], LANES), LOW)

    query_grad_ref[...] = attend_back_pair(
        query[...], key[...], value[...], kept, inverse[...], mix[...], grad[...], value_wide, made.at[pair]
    )

    @pl.when(pair == made.shape[0] - 1)
    def _():
        finish_weight(made, (rows_0, rows_1, rows_2, rows_3), weight_grad_ref, 0)


def finish_rows(made, weight, first, own_ref, far_ref, core_ref):
    pairs, _, keys = made.shape
    local = keys // 4
    width = own_ref.shape[1]
    for step in range(4):
        total = None
        for pair in range(pairs):
            at = first + pair * LANES
            columns = jnp.concatenate(
                [weight[:, at : at + LANES], weight[:, width + at : width + at + LANES]], axis=1
            )
            part = made[pair, :, step * local : (step + 1) * local].T
            term = dot(part, columns, BY_LANES)
            total = term if total is None else total + term
        if step == 0:
            own_ref[...] = total
        elif step == 2:
            far_ref[...] = total.astype(LOW)
        else:
            core_ref[step // 2] = total.astype(LOW)


def finish_weight(made, row_refs, weight_grad_ref, first):
    local, width = row_refs[0].shape
    for pair in range(made.shape[0]):
        total = None
        for step in range(4):
            term = dot(made[pair, :, step * local : (step + 1) * local], row_refs[step][...])
            total = term if total is None else total + term
        total = total.T.astype(LOW)
        at = first + pair * LANES
        weight_grad_ref[:, at : at + LANES] = total[:, :LANES]
        weight_grad_ref[:, width + at : width + at + LANES] = total[:, LANES:]


def between_kernel(
    info, query_grad, second_grad, first_unit, first_scale, norms, norm_sums, self_mix, pair_grad, cross_out_grad, out_weight, query_weight, *refs
):
    (
        first_grad_ref,
        mix_grad_ref,
        kept,
        sent,
        out_grad,
        query_weight_grad,
        norm_grad,
        norm_rows,
    ) = refs
    home = info[0]
    width = self_mix.shape[1]
    unit = first_unit[...]
    first_low = (unit * norms[0:1] + norms[3:4]).astype(LOW)
    low_grad = query_grad[...]
    query_weight_grad[...] = dot(first_low.T, low_grad).astype(LOW)
    cotangent = second_grad[...] + dot(low_grad, query_weight[...], BY_LANES)
    first_grad, gain_one, bias_one = norm_backward(
        cotangent, unit, first_scale[:, 0:1], norms[0:1]
    )
    first_grad_ref[...] = first_grad
    self_out_low = first_grad.astype(LOW)
    out_grad[...] = dot(self_mix[...].T, self_out_low).astype(LOW)
    mix_grad_ref[...] = dot(self_out_low, out_weight[...], BY_LANES).astype(LOW)
    norm_rows[...] = jnp.zeros(norm_rows.shape, FULL)
    norm_rows[0:8] = norm_sums[...]
    norm_rows[0:1] = gain_one
    norm_rows[3:4] = bias_one
    norm_grad[...] = norm_rows[...].T.astype(LOW)
    pack_grad(out_grad, kept, sent, home, (0, 1))
    pack_grad(query_weight_grad, kept, sent, home, (width, 1))
    pack_grad(pair_grad, kept, sent, home, (2 * width, 1))
    pack_grad(cross_out_grad, kept, sent, home, (4 * width, 1))
    pack_grad(norm_grad, kept, sent, home, (5 * width, 1))


def self_backward_kernel(
    info,
    query,
    key,
    value,
    kept_weights,
    inverse,
    mix,
    grad,
    rows_0,
    rows_1,
    rows_2,
    rows_3,
    made,
    query_grad_ref,
    kept,
    sent,
    value_wide,
    query_grads,
    weight_grad,
):
    pair = pl.program_id(0)
    width = rows_0.shape[1]
    pairs = made.shape[0]

    @pl.when(pair == 0)
    def _():
        value_wide[:, LANES:] = jnp.ones((value_wide.shape[0], LANES), LOW)

    query_grads[pair] = attend_back_pair(
        query[...], key[...], value[...], kept_weights, inverse[...], mix[...], grad[...], value_wide, made.at[pair]
    )

    @pl.when(pair == pairs - 1)
    def _():
        finish_weight(made, (rows_0, rows_1, rows_2, rows_3), weight_grad, width)
        low_grad = jnp.concatenate([query_grads[at] for at in range(pairs)], axis=1)
        query_grad_ref[...] = low_grad
        weight_grad[:, 0:width] = dot(rows_0[...].T, low_grad).astype(LOW)
        pack_grad(weight_grad, kept, sent, info[0], (0, 1))


def memory_kernel(made, weight, own_ref, far_ref, core_ref):
    finish_rows(made, weight, 0, own_ref, far_ref, core_ref)


def states_kernel(made, query_grad, first_grad, weight, own_ref, far_ref, core_ref):
    width = own_ref.shape[1]
    finish_rows(made, weight, width, own_ref, far_ref, core_ref)
    own_ref[...] += first_grad[...] + dot(query_grad[...], weight[:, 0:width], BY_LANES)


def whole(shape):
    return pl.BlockSpec(shape, lambda *at: (0,) * len(shape))


def call(kernel, inputs, specs, outputs, out_specs, scratch, grid=(), micros=1, mib=58):
    moved = sum(math.prod(a.shape) * a.dtype.itemsize for a in list(inputs) + list(outputs))
    return pl.pallas_call(
        kernel,
        out_shape=outputs,
        grid=grid,
        in_specs=specs,
        out_specs=out_specs,
        scratch_shapes=scratch,
        compiler_params=pltpu.CompilerParams(vmem_limit_bytes=mib * 2**20),
        cost_estimate=pl.CostEstimate(flops=micros * 10**9, bytes_accessed=moved, transcendentals=0),
    )(*inputs)


SCALARS = pl.BlockSpec(memory_space=pltpu.SMEM)


def shaped(shape, kind):
    return jax.ShapeDtypeStruct(shape, kind)


def per_device(
    target_states,
    memory,
    target_lengths,
    source_lengths,
    self_project,
    self_output,
    cross_project,
    memory_project,
    cross_output,
    expand_weight,
    contract_weight,
    norm_gain,
    norm_bias,
    out_grad,
):
    _, local, width = target_states.shape
    states = target_states[0]
    own_memory = memory[0]
    rows = self_project.shape[0]
    ff = expand_weight.shape[1]
    keys = local * 4
    pairs = width // LANES
    info = jnp.stack([home_number(), lax.axis_index("narrow")]).astype(jnp.int32)

    batches = 3 * width, 5 * width + LANES, 2 * ff
    if staged():
        shards = (
            self_output,
            cross_project,
            memory_project,
            cross_output,
            expand_weight,
            contract_weight,
            norm_gain,
            norm_bias,
        )
        later = batches[1] + batches[2]
        batch_23 = call(
            pack_kernel,
            list(shards),
            [whole(shard.shape) for shard in shards],
            [shaped((rows, later), LOW)],
            [whole((rows, later))],
            [pltpu.VMEM((LANES, LANES), FULL)],
        )[0]
        far_1 = jnp.stack(gather_far(self_project))
        states_x = exchange(states, 2)
        states_c = exchange(states, 1)
        (batch_23, states_c), far_1 = after((batch_23, states_c), far_1)
        near_23 = exchange(batch_23, FAR[0])
        plane_1 = gather_plane(far_1)
        near_23, states_x = after(near_23, states_x)
        own_memory, states_c = after(own_memory, states_c)
        half_2 = jnp.stack([batch_23[:, : batches[1]], near_23[:, : batches[1]]])
        half_3 = jnp.stack([batch_23[:, batches[1] :], near_23[:, batches[1] :]])
        rest_2 = exchange(half_2, FAR[1])
        memory_x = exchange(own_memory, 2)
        half_3, rest_2 = after(half_3, rest_2)
        far_2 = jnp.concatenate([half_2, rest_2])
        rest_3 = exchange(half_3, FAR[1])
    else:
        norm_shard = jnp.concatenate([norm_gain, norm_bias], axis=0).T
        norm_shard = jnp.pad(norm_shard, ((0, 0), (0, LANES - norm_shard.shape[1])))
        folded = fold_rows(contract_weight, rows)
        plane_1 = self_project
        far_2 = jnp.concatenate(
            [self_output, cross_project, memory_project, cross_output, norm_shard], axis=1
        )
        far_3 = jnp.concatenate([expand_weight, folded], axis=1)
        states_x = exchange(states, 2)
        states_c = exchange(states, 1)
        memory_c = exchange(own_memory, 1)
        memory_x = exchange(own_memory, 2)
    states_xc = exchange(states_x, 1)
    far_2, plane_1 = after(far_2, plane_1)
    weights_1 = gather_core(plane_1)
    row_states = [states, states_c, states_x, states_xc]
    own_2 = exchange(far_2, 1) if staged() else None
    if staged():
        row_states[1], own_2 = after(row_states[1], own_2)
    plane_2 = gather_plane(far_2)

    row_spec = whole((local, width))
    pair_rows = pl.BlockSpec((local, LANES), lambda pair: (0, pair))
    pair_keys = pl.BlockSpec((keys, LANES), lambda pair: (0, pair))
    pair_kept = pl.BlockSpec((2, local, keys), lambda pair: (pair, 0, 0))
    quarter_specs_1 = [whole(q.shape) for q in weights_1]
    attend_scratch = [
        pltpu.VMEM((pairs, local, LANES), LOW),
        pltpu.VMEM((local, LANES), LOW),
        pltpu.VMEM((pairs, keys, 2 * LANES), LOW),
        pltpu.VMEM((pairs, keys, 2 * LANES), LOW),
        pltpu.VMEM((2, local, keys), FULL),
    ]
    attend_outputs = [
        shaped((local, width), LOW),
        pltpu.HBM((local, width), LOW),
        pltpu.HBM((local, width), FULL),
        pltpu.HBM((local, width), FULL),
        pltpu.HBM((keys, width), LOW),
        pltpu.HBM((keys, width), LOW),
        pltpu.HBM((2 * pairs, local, keys), LOW),
    ]
    attend_specs = [pair_rows] * 4 + [pair_keys, pair_keys, pair_kept]
    in_place = pl.BlockSpec(memory_space=pl.ANY)
    self_mix, self_query, self_exact, self_inverse, self_key, self_value, self_kept, self_weight = call(
        self_forward_kernel,
        [info, target_lengths, *row_states, *weights_1],
        [SCALARS, SCALARS] + [row_spec] * 4 + quarter_specs_1,
        attend_outputs + [pltpu.HBM((width, 3 * width), LOW)],
        attend_specs + [in_place],
        [pltpu.VMEM((width, 3 * width), LOW), pltpu.SemaphoreType.DMA] + attend_scratch,
        grid=(pairs,),
        micros=25, mib=38,
    )

    if staged():
        (memory_x, own_memory, rest_3), self_mix = after((memory_x, own_memory, rest_3), self_mix)
        memory_c = exchange(own_memory, 1)
        far_3 = jnp.concatenate([half_3, rest_3])
    plane_2, self_mix = after(plane_2, self_mix)
    own_3 = exchange(far_3, 1) if staged() else None
    memory_xc = exchange(memory_x, 1)
    weights_2 = gather_core(plane_2, own_2)
    row_memory = [own_memory, memory_c, memory_x, memory_xc]
    plane_3 = gather_plane(far_3)
    quarter_specs_2 = [whole(q.shape) for q in weights_2]
    wide_scale = whole((local, LANES))
    norm_spec = whole((8, width))
    square = whole((width, width))
    (
        cross_mix,
        cross_query,
        cross_exact,
        cross_inverse,
        cross_key,
        cross_value,
        cross_kept,
        first_unit,
        first_scale,
        norms,
        second_unit,
        second_scale,
        cross_out_weight,
        out_weight,
        query_weight,
        pair_weight,
    ) = call(
        cross_forward_kernel,
        [info, target_lengths, source_lengths, self_mix, states, *row_memory, *weights_2],
        [SCALARS] * 3 + [row_spec] * 6 + quarter_specs_2,
        attend_outputs
        + [
            pltpu.HBM((local, width), FULL),
            pltpu.HBM((local, LANES), FULL),
            shaped((8, width), FULL),
            shaped((local, width), FULL),
            shaped((local, LANES), FULL),
            shaped((width, width), LOW),
            pltpu.HBM((width, width), LOW),
            pltpu.HBM((width, width), LOW),
            pltpu.HBM((width, 2 * width), LOW),
        ],
        attend_specs + [row_spec, wide_scale, norm_spec, row_spec, wide_scale, square] + [in_place] * 3,
        [
            pltpu.VMEM((width, width), LOW),
            pltpu.VMEM((width, width), LOW),
            pltpu.VMEM((width, 2 * width), LOW),
            pltpu.VMEM((width, LANES), LOW),
            pltpu.SemaphoreType.DMA((3,)),
            pltpu.VMEM((pairs, local, LANES), LOW),
        ]
        + attend_scratch,
        grid=(pairs,),
        micros=25, mib=46,
    )

    plane_3, second_unit = after(plane_3, second_unit)
    weights_3 = gather_core(plane_3, own_3, ff // width)
    quarter_specs_3 = [whole(q.shape) for q in weights_3]
    chunk_count = ff // width
    packed_3 = (4, 4, TILE_ROWS, 2 * ff)
    hidden_shape = (chunk_count, local, width)
    output, third_grad, hidden_grads, expand_whole, norm_sums, kept_3, sent_3 = call(
        middle_kernel,
        [info, second_unit, norms, out_grad[0], *weights_3],
        [SCALARS, row_spec, norm_spec, row_spec] + quarter_specs_3,
        [
            shaped((local, width), FULL),
            shaped((local, width), FULL),
            shaped(hidden_shape, LOW),
            shaped((width, ff), LOW),
            shaped((8, width), FULL),
            shaped(packed_3, LOW),
            shaped(packed_3, LOW),
        ],
        [row_spec, row_spec, whole(hidden_shape), whole((width, ff)), norm_spec]
        + [whole(packed_3), whole(packed_3)],
        [
            pltpu.VMEM((ff, width), LOW),
            pltpu.VMEM(hidden_shape, LOW),
            pltpu.VMEM(hidden_shape, FULL),
            pltpu.VMEM((width, ff), LOW),
            pltpu.VMEM((ff, width), LOW),
        ],
        micros=14, mib=34,
    )
    other_3 = exchange_core(sent_3)
    second_grad, cross_mix_grad, cross_out_grad, norm_sums = call(
        second_back_kernel,
        [
            third_grad,
            hidden_grads,
            expand_whole,
            second_unit,
            second_scale,
            norms,
            norm_sums,
            cross_mix,
            cross_out_weight,
        ],
        [row_spec, whole(hidden_shape), whole((width, ff))]
        + [row_spec, wide_scale, norm_spec, norm_spec, row_spec, square],
        [
            shaped((local, width), FULL),
            shaped((local, width), LOW),
            shaped((width, width), LOW),
            shaped((8, width), FULL),
        ],
        [row_spec, row_spec, square, norm_spec],
        [],
        micros=4, mib=12,
    )
    other_3, cross_mix_grad = after(other_3, cross_mix_grad)
    core_3 = reduce_core(kept_3, other_3)
    core_3, cross_mix_grad = after(core_3, cross_mix_grad)
    planes_3 = exchange_plane(core_3)

    back_specs = [pair_rows, pair_keys, pair_keys, pair_kept, pair_rows, pair_rows, pair_rows]
    made_shape = (pairs, 2 * LANES, keys)
    cross_made, cross_query_grad, pair_weight_grad = call(
        cross_backward_kernel,
        [
            cross_query,
            cross_key,
            cross_value,
            cross_kept,
            cross_inverse,
            cross_exact,
            cross_mix_grad,
            *row_memory,
        ],
        back_specs + [row_spec] * 4,
        [
            shaped(made_shape, LOW),
            shaped((local, width), LOW),
            shaped((width, 2 * width), LOW),
        ],
        [whole(made_shape), pair_rows, whole((width, 2 * width))],
        [pltpu.VMEM((keys, 2 * LANES), LOW)],
        grid=(pairs,),
        micros=33, mib=36,
    )
    planes_3, cross_query_grad = after(planes_3, cross_query_grad)
    plane_sum_3 = reduce_plane(planes_3)
    plane_sum_3, cross_query_grad = after(plane_sum_3, cross_query_grad)
    half_sum_3 = exchange_half(plane_sum_3)

    packed_2 = (4, 4, TILE_ROWS, 5 * width + LANES)
    first_grad, self_mix_grad, kept_2, sent_2 = call(
        between_kernel,
        [
            info,
            cross_query_grad,
            second_grad,
            first_unit,
            first_scale,
            norms,
            norm_sums,
            self_mix,
            pair_weight_grad,
            cross_out_grad,
            out_weight,
            query_weight,
        ],
        [SCALARS, row_spec, row_spec, row_spec, whole((local, LANES))]
        + [whole((8, width))] * 2
        + [row_spec, whole((width, 2 * width)), whole((width, width))]
        + [square] * 2,
        [
            shaped((local, width), FULL),
            shaped((local, width), LOW),
            shaped(packed_2, LOW),
            shaped(packed_2, LOW),
        ],
        [row_spec, row_spec, whole(packed_2), whole(packed_2)],
        [
            pltpu.VMEM((width, width), LOW),
            pltpu.VMEM((width, width), LOW),
            pltpu.VMEM((width, LANES), LOW),
            pltpu.VMEM((LANES, width), FULL),
        ],
        micros=6, mib=14,
    )
    other_2 = exchange_core(sent_2)
    cross_made, sent_2 = after(cross_made, sent_2)
    rows_shapes = [
        shaped((local, width), FULL),
        shaped((local, width), LOW),
        shaped((2, local, width), LOW),
    ]
    rows_specs = [row_spec, row_spec, whole((2, local, width))]
    memory_own, memory_far_part, memory_parts = call(
        memory_kernel,
        [cross_made, pair_weight],
        [whole(made_shape), whole((width, 2 * width))],
        rows_shapes,
        rows_specs,
        [],
        micros=3, mib=20,
    )
    other_2, memory_parts = after(other_2, memory_parts)
    memory_sent = exchange(memory_parts, 1)
    core_2 = reduce_core(kept_2, other_2)
    memory_other = reduce_row_core(memory_far_part, memory_sent)
    (core_2, memory_other), self_mix_grad = after((core_2, memory_other), self_mix_grad)
    planes_2 = exchange_plane(core_2)
    memory_far = exchange(memory_other, 2)

    packed_1 = (4, 4, TILE_ROWS, 3 * width)
    made, self_query_grad, kept_1, sent_1 = call(
        self_backward_kernel,
        [
            info,
            self_query,
            self_key,
            self_value,
            self_kept,
            self_inverse,
            self_exact,
            self_mix_grad,
            *row_states,
        ],
        [SCALARS] + back_specs + [row_spec] * 4,
        [
            shaped(made_shape, LOW),
            shaped((local, width), LOW),
            shaped(packed_1, LOW),
            shaped(packed_1, LOW),
        ],
        [whole(made_shape), row_spec, whole(packed_1), whole(packed_1)],
        [
            pltpu.VMEM((keys, 2 * LANES), LOW),
            pltpu.VMEM((pairs, local, LANES), LOW),
            pltpu.VMEM((width, 3 * width), LOW),
        ],
        grid=(pairs,),
        micros=33, mib=36,
    )
    (planes_2, memory_far, half_sum_3), (sent_1, kept_1) = after(
        (planes_2, memory_far, half_sum_3), (sent_1, kept_1)
    )
    other_1 = exchange_core(sent_1)
    states_own, states_far_part, states_parts = call(
        states_kernel,
        [made, self_query_grad, first_grad, self_weight],
        [whole(made_shape), row_spec, row_spec, whole((width, 3 * width))],
        rows_shapes,
        rows_specs,
        [],
        micros=4, mib=20,
    )
    other_1, states_parts = after(other_1, states_parts)
    core_1 = reduce_core(kept_1, other_1)
    planes_1 = exchange_plane(core_1)
    states_sent = exchange(states_parts, 1)
    (planes_2, half_sum_3, memory_far), core_1 = after((planes_2, half_sum_3, memory_far), core_1)
    plane_sum_2 = reduce_plane(planes_2)
    half_sum_2 = exchange_half(plane_sum_2)
    states_other = reduce_row_core(states_far_part, states_sent)
    (half_sum_2, half_sum_3), states_other = after((half_sum_2, half_sum_3), states_other)
    states_far = exchange(states_other, 2)
    total_3 = reduce_half(plane_sum_3, half_sum_3)
    total_2 = reduce_half(plane_sum_2, half_sum_2)
    planes_1, (total_2, total_3, states_other) = after(planes_1, (total_2, total_3, states_other))
    plane_sum_1 = reduce_plane(planes_1)
    fars_1 = exchange_far(plane_sum_1)
    memory_grad = reduce_row(memory_own, memory_sent, memory_far)
    states_grad = reduce_row(states_own, states_sent, states_far)
    count = norm_gain.shape[0]
    if staged():
        near = exchange(jnp.concatenate([total_2[1], total_3[1]], axis=1), FAR[0])
        settled = [
            shaped((rows, width), FULL),
            shaped((rows, width), FULL),
            shaped((rows, 2 * width), FULL),
            shaped((rows, width), FULL),
            shaped((rows, ff), FULL),
            shaped((rows * ff // width, width), FULL),
            shaped(norm_gain.shape, FULL),
            shaped(norm_gain.shape, FULL),
        ]
        out, cross, pairs_grad, cross_out, expand_grad, contract_grad, gain, bias = call(
            settle_kernel,
            [total_2[0], total_3[0], near],
            [whole((rows, batches[1])), whole((rows, batches[2])), whole((rows, later))],
            settled,
            [whole(each.shape) for each in settled],
            [pltpu.VMEM((LANES, LANES), FULL)],
        )
        fars_1, out = after(fars_1, out)
        project = reduce_far(fars_1)
    else:
        grad_3 = reduce_far(total_3, ff // width)
        grad_2 = reduce_far(total_2)
        project = reduce_far(fars_1)
        expand_grad, contract_grad = grad_3[:, :ff], unfold_rows(grad_3[:, ff:], width)
        out, cross = grad_2[:, :width], grad_2[:, width : 2 * width]
        pairs_grad, cross_out = grad_2[:, 2 * width : 4 * width], grad_2[:, 4 * width : 5 * width]
        norm_grads = grad_2[:, 5 * width :].T
        gain, bias = norm_grads[:count], norm_grads[count : 2 * count]
    return (
        output[None],
        states_grad[None],
        memory_grad[None],
        project,
        out,
        cross,
        pairs_grad,
        cross_out,
        expand_grad,
        contract_grad,
        gain,
        bias,
    )


def reduce_row_core(part, sent):
    return add_all(part, [sent[1]]).astype(LOW)


def reduce_row(own, sent, far):
    return add_all(own, [sent[0], far])


def solution(mesh):
    in_specs = (
        P("wide", "narrow", None),
        P("wide", "narrow", None),
        P("wide", None),
        P("wide", None),
        P(("wide", "narrow"), None),
        P(("wide", "narrow"), None),
        P(("wide", "narrow"), None),
        P(("wide", "narrow"), None),
        P(("wide", "narrow"), None),
        P(("wide", "narrow"), None),
        P(("wide", "narrow"), None),
        P(None, ("wide", "narrow")),
        P(None, ("wide", "narrow")),
        P("wide", "narrow", None),
    )
    out_specs = (
        P("wide", "narrow", None),
        P("wide", "narrow", None),
        P("wide", "narrow", None),
        P(("wide", "narrow"), None),
        P(("wide", "narrow"), None),
        P(("wide", "narrow"), None),
        P(("wide", "narrow"), None),
        P(("wide", "narrow"), None),
        P(("wide", "narrow"), None),
        P(("wide", "narrow"), None),
        P(None, ("wide", "narrow")),
        P(None, ("wide", "narrow")),
    )
    return jax.shard_map(
        per_device, mesh=mesh, in_specs=in_specs, out_specs=out_specs, check_vma=False
    )
```

```python
import functools
import math

import jax
import jax.numpy as jnp
from jax import lax
from jax.experimental import pallas as pl
from jax.experimental.pallas import tpu as pltpu
from jax.sharding import PartitionSpec as P

HEAD_DIM = 64
LANES = 128
TILE_ROWS = 16
BLOCKS = 32
AXES = ("wide", "narrow")
LOW = jnp.bfloat16
FULL = jnp.float32

ln_eps = 1e-05
score_scale = HEAD_DIM ** (-0.5)
mask_step = -(2.0**30)

BY_LANES = (((1,), (1,)), ((), ()))
PLAIN = (((1,), (0,)), ((), ()))


def dot(left, right, dims=PLAIN):
    return lax.dot_general(left, right, dims, preferred_element_type=FULL)


def exchange(block, mask):
    device_count = lax.axis_size("wide") * lax.axis_size("narrow")
    pairs = [(device, device ^ mask) for device in range(device_count)]
    return lax.ppermute(block, AXES, pairs)


def device_number():
    return lax.axis_index("wide") * lax.axis_size("narrow") + lax.axis_index("narrow")


def staged():
    return lax.axis_size("wide") * lax.axis_size("narrow") == BLOCKS


FAR = (8, 16, 24)
PLANE = (2, 4, 6)


def gather_far(shard):
    if not staged():
        return shard
    return [shard] + [exchange(shard, mask) for mask in FAR]


def gather_plane(held):
    if not staged():
        return held
    return [held] + [exchange(held, mask) for mask in PLANE]


def gather_core(held, own=None, folds=0):
    if staged():
        first = exchange(held[0], 1) if own is None else own
        return held + [first] + [exchange(quarter, 1) for quarter in held[1:]]
    whole = lax.all_gather(held, AXES, axis=0, tiled=True)
    if folds:
        rows, columns = held.shape
        split = columns - folds * whole.shape[0]
        tall = unfold_rows(held[:, split:], whole.shape[0])
        tall = lax.all_gather(tall, AXES, axis=0, tiled=True)
        tall = tall.reshape(BLOCKS, folds, TILE_ROWS, -1).transpose(0, 2, 1, 3)
        whole = jnp.concatenate([whole[:, :split], tall.reshape(whole.shape[0], -1)], axis=1)
    whole = whole.reshape(4, 4, 2, TILE_ROWS, held.shape[1]).transpose(2, 1, 0, 3, 4)
    return [whole[core, plane] for core in range(2) for plane in range(4)]


def home_number():
    return device_number() if staged() else jnp.zeros((), jnp.int32)


def block_number(home, core, plane, far):
    return home ^ (far * 8 + plane * 2 + core)


def add_all(first, others):
    total = first.astype(FULL)
    for other in others:
        total = total + other.astype(FULL)
    return total


def exchange_core(sent):
    return exchange(sent, 1) if staged() else sent


def reduce_core(kept, other):
    return add_all(kept, [other]).astype(LOW) if staged() else (kept, other)


def exchange_plane(held):
    if not staged():
        return held
    return [held[0]] + [exchange(held[plane + 1], mask) for plane, mask in enumerate(PLANE)]


def reduce_plane(planes):
    return add_all(planes[0], planes[1:]).astype(LOW) if staged() else planes


def exchange_far(held):
    if not staged():
        return held
    return [held[0]] + [exchange(held[far + 1], mask) for far, mask in enumerate(FAR)]


def exchange_half(held):
    return exchange(held[2:], FAR[1]) if staged() else held


def reduce_half(held, other):
    return add_all(held[:2], [other]).astype(LOW) if staged() else held


def reduce_far(held, folds=0):
    if staged():
        return add_all(held[0], held[1:])
    whole = jnp.stack(held).transpose(2, 1, 0, 3, 4)
    whole = whole.reshape(BLOCKS * TILE_ROWS, -1).astype(FULL)
    if folds:
        split = whole.shape[1] - folds * whole.shape[0]
        tall = whole[:, split:].reshape(BLOCKS, TILE_ROWS, folds, -1).transpose(0, 2, 1, 3)
        tall = tall.reshape(folds * whole.shape[0], -1)
        tall = lax.psum_scatter(tall, AXES, scatter_dimension=0, tiled=True)
        whole = lax.psum_scatter(whole[:, :split], AXES, scatter_dimension=0, tiled=True)
        return jnp.concatenate([whole, fold_rows(tall, whole.shape[0])], axis=1)
    return lax.psum_scatter(whole, AXES, scatter_dimension=0, tiled=True)


def after(values, token):
    return lax.optimization_barrier((values, token))


def fold_rows(block, rows):
    return jnp.concatenate(
        [block[at : at + rows] for at in range(0, block.shape[0], rows)], axis=1
    )


def unfold_rows(block, width):
    return jnp.concatenate(
        [block[:, at : at + width] for at in range(0, block.shape[1], width)], axis=0
    )


def lane_numbers(shape):
    return lax.broadcasted_iota(jnp.int32, shape, 1)


def segment_bounds(lengths_ref):
    lane = lane_numbers((1, LANES))
    first = jnp.full((1, LANES), 2**30, jnp.int32)
    last = jnp.zeros((1, LANES), jnp.int32)
    start = jnp.int32(0)
    count = lengths_ref.shape[1]
    for segment in range(count + 1):
        end = start + lengths_ref[0, segment] if segment < count else jnp.int32(2**30)
        first = jnp.where(lane == segment, start, first)
        last = jnp.where(lane == segment, end, last)
        start = end
    return first, last


def segment_flags(start, rows, bounds):
    position = start + lax.broadcasted_iota(jnp.int32, (rows, LANES), 0)
    return (position >= bounds[0]) & (position < bounds[1])


def three_parts(value):
    first = value.astype(LOW)
    rest = value - first.astype(FULL)
    second = rest.astype(LOW)
    third = (rest - second.astype(FULL)).astype(LOW)
    return first.astype(FULL), second.astype(FULL), third.astype(FULL)


def query_flags(lengths_ref, start, rows):
    segments = lengths_ref.shape[1] + 1
    own = segment_flags(start, rows, segment_bounds(lengths_ref))
    return jnp.where(own | (lane_numbers((rows, LANES)) >= segments), 0.0, mask_step).astype(LOW)


def key_flags(lengths_ref, start, rows):
    own = segment_flags(start, rows, segment_bounds(lengths_ref))
    return jnp.where(own, 1.0, 0.0).astype(LOW)


def fill_weight(target, quarters, home, columns):
    first, folds = columns
    width = target.shape[1]
    for core in range(2):
        for plane in range(4):
            for far in range(4):
                block = block_number(home, core, plane, far)
                piece = quarters[core * 4 + plane]
                for fold in range(folds):
                    row = pl.multiple_of(block * (TILE_ROWS * folds) + fold * TILE_ROWS, TILE_ROWS)
                    start = first + fold * width
                    target[pl.ds(row, TILE_ROWS), :] = piece[far, :, start : start + width]


def pack_grad(source, kept, sent, home, columns):
    first, folds = columns
    width = source.shape[1]
    for core, target in ((0, kept), (1, sent)):
        for plane in range(4):
            for far in range(4):
                block = block_number(home, core, plane, far)
                for fold in range(folds):
                    row = pl.multiple_of(block * (TILE_ROWS * folds) + fold * TILE_ROWS, TILE_ROWS)
                    start = first + fold * width
                    target[plane, far, :, start : start + width] = source[pl.ds(row, TILE_ROWS), :]


def normalise(states):
    centred = states - jnp.mean(states, axis=1, keepdims=True)
    spread = jnp.mean(centred * centred, axis=1, keepdims=True)
    scale = lax.rsqrt(spread + ln_eps)
    return centred * scale, scale


def norm_backward(cotangent, unit, scale, gain):
    scaled = cotangent * gain
    grad = scale * (
        scaled
        - jnp.mean(scaled, axis=1, keepdims=True)
        - unit * jnp.mean(scaled * unit, axis=1, keepdims=True)
    )
    return (
        grad,
        jnp.sum(cotangent * unit, axis=0, keepdims=True),
        jnp.sum(cotangent, axis=0, keepdims=True),
    )


KEY_STEP = 256


def pack_kernel(*refs):
    ins, (packed, square) = refs[:8], refs[8:]
    self_output, cross_project, memory_project, cross_output, expand, contract, gain, bias = ins
    rows, width = self_output.shape
    at = 0
    for part in (self_output, cross_project, memory_project, cross_output):
        packed[:, at : at + part.shape[1]] = part[...]
        at += part.shape[1]
    count = gain.shape[0]
    square[...] = jnp.zeros(square.shape, FULL)
    square[0:count, 0:rows] = gain[...].astype(FULL)
    square[count : 2 * count, 0:rows] = bias[...].astype(FULL)
    packed[:, at : at + LANES] = square[...].T[0:rows].astype(LOW)
    at += LANES
    packed[:, at : at + expand.shape[1]] = expand[...]
    at += expand.shape[1]
    for fold in range(contract.shape[0] // rows):
        packed[:, at : at + width] = contract[fold * rows : (fold + 1) * rows]
        at += width


def settle_kernel(part_2, part_3, other, *refs):
    output_ref, cross_ref, memory_ref, cross_out_ref, expand_ref, contract_ref, gain_ref, bias_ref, square = refs
    rows, width = output_ref.shape
    split = part_2.shape[1]
    total = add_all(part_2[...], [other[:, :split]])
    at = 0
    for ref in (output_ref, cross_ref, memory_ref, cross_out_ref):
        ref[...] = total[:, at : at + ref.shape[1]]
        at += ref.shape[1]
    square[...] = jnp.zeros(square.shape, FULL)
    square[0:rows] = total[:, at : at + LANES]
    turned = square[...].T
    count = gain_ref.shape[0]
    gain_ref[...] = turned[0:count, 0:rows]
    bias_ref[...] = turned[count : 2 * count, 0:rows]
    total = add_all(part_3[...], [other[:, split:]])
    span = expand_ref.shape[1]
    expand_ref[...] = total[:, :span]
    for fold in range(contract_ref.shape[0] // rows):
        at = span + fold * width
        contract_ref[fold * rows : (fold + 1) * rows] = total[:, at : at + width]


def attend_pair(query, flags, key_wide, values, scores, kept):
    rows = query.shape[0]
    keys = key_wide.shape[0]
    left = lane_numbers((rows, LANES)) < HEAD_DIM
    zero = jnp.zeros_like(query)
    queries = [
        jnp.concatenate([jnp.where(left, query, zero), flags], axis=1),
        jnp.concatenate([jnp.where(left, zero, query), flags], axis=1),
    ]

    def score(head, start, peak):
        made = dot(queries[head], key_wide[start : start + KEY_STEP], BY_LANES)
        scores[head, :, start : start + KEY_STEP] = made
        for at in range(0, KEY_STEP, LANES):
            peak = jnp.maximum(peak, made[:, at : at + LANES])
        return peak

    def raise_scores(head, start, peak, total):
        span = slice(start, start + KEY_STEP)
        weights = jnp.exp(scores[head, :, span] - peak)
        for at in range(0, KEY_STEP, LANES):
            total = total + weights[:, at : at + LANES]
        return total

    def weigh(head, start, shift, total):
        span = slice(start, start + KEY_STEP)
        probs = jnp.exp(scores[head, :, span] - shift).astype(LOW)
        kept[head, :, span] = probs
        return total + dot(probs, values[span])

    steps = range(0, keys, KEY_STEP)
    lowest = jnp.full((rows, LANES), -jnp.inf, FULL)
    empty = jnp.zeros((rows, LANES), FULL)
    peak = lowest
    for start in steps:
        peak = score(0, start, peak)
    first_peak = jnp.max(peak, axis=1, keepdims=True)
    peak, first_total = lowest, empty
    for start in steps:
        peak = score(1, start, peak)
        first_total = raise_scores(0, start, first_peak, first_total)
    second_peak = jnp.max(peak, axis=1, keepdims=True)
    first_shift = first_peak + jnp.log(jnp.sum(first_total, axis=1, keepdims=True))
    first, second_total = empty, empty
    for start in steps:
        second_total = raise_scores(1, start, second_peak, second_total)
        first = weigh(0, start, first_shift, first)
    second_shift = second_peak + jnp.log(jnp.sum(second_total, axis=1, keepdims=True))
    second = empty
    for start in steps:
        second = weigh(1, start, second_shift, second)
    return jnp.where(left, first, second)


def pair_columns(first, pair):
    return pl.ds(pl.multiple_of(first + pair * LANES, LANES), LANES)


def prepare_wide(lengths, key_wide, place):
    pairs, keys, _ = key_wide.shape
    local = keys // 4
    for step in range(4):
        span = slice(step * local, (step + 1) * local)
        flags = key_flags(lengths, (place ^ step) * local, local)
        for pair in range(pairs):
            key_wide[pair, span, LANES:] = flags


def project_rows(rows, weight, key_wide, values):
    pairs = key_wide.shape[0]
    local = rows[0].shape[0]
    for step, part in enumerate(rows):
        span = slice(step * local, (step + 1) * local)
        for target, first in ((key_wide, 0), (values, pairs * LANES)):
            made = dot(part[...], weight[:, first : first + pairs * LANES]).astype(LOW)
            for pair in range(pairs):
                target[pair, span, :LANES] = made[:, pair * LANES : (pair + 1) * LANES]


def project_queries(rows, weight, queries):
    made = dot(rows, weight).astype(LOW).astype(FULL) * score_scale
    for pair in range(queries.shape[0]):
        queries[pair] = made[:, pair * LANES : (pair + 1) * LANES].astype(LOW)


def self_forward_kernel(info, lengths, rows_0, rows_1, rows_2, rows_3, *refs):
    quarters = refs[:8]
    (
        mix_ref,
        query_ref,
        exact_ref,
        key_ref,
        value_ref,
        kept,
        weight_ref,
        weight,
        saved,
        queries,
        flags_q,
        key_wide,
        values,
        scores,
    ) = refs[8:]
    pair = pl.program_id(0)
    home, place = info[0], info[1]
    local, width = rows_0.shape

    @pl.when(pair == 0)
    def _():
        fill_weight(weight, quarters, home, (0, 1))
        pltpu.make_async_copy(weight, weight_ref, saved).start()
        flags_q[...] = query_flags(lengths, place * local, local)
        prepare_wide(lengths, key_wide, place)
        project_rows((rows_0, rows_1, rows_2, rows_3), weight.at[:, width:], key_wide, values)
        project_queries(rows_0[...], weight[:, :width], queries)

    query = queries[pair]
    query_ref[...] = query
    key_ref[...] = key_wide[pair, :, :LANES]
    value_ref[...] = values[pair]
    mix = attend_pair(
        query, flags_q[...], key_wide.at[pair], values.at[pair], scores, kept
    )
    mix_ref[...] = mix.astype(LOW)
    exact_ref[...] = mix

    @pl.when(pair == queries.shape[0] - 1)
    def _():
        pltpu.make_async_copy(weight, weight_ref, saved).wait()


def cross_forward_kernel(
    info, target_lengths, source_lengths, mix, states, rows_0, rows_1, rows_2, rows_3, *refs
):
    quarters = refs[:8]
    (
        mix_ref,
        query_ref,
        exact_ref,
        key_ref,
        value_ref,
        kept,
        unit_ref,
        scale_ref,
        norms_ref,
        second_unit_ref,
        second_scale_ref,
        cross_out_ref,
        out_weight_ref,
        query_weight_ref,
        pair_weight_ref,
        out_weight,
        query_weight,
        pair_weight,
        norm_rows,
        saved,
        mixes,
        queries,
        flags_q,
        key_wide,
        values,
        scores,
    ) = refs[8:]
    pair = pl.program_id(0)
    home, place = info[0], info[1]
    local, width = rows_0.shape

    copies = [
        pltpu.make_async_copy(source, target, saved.at[at])
        for at, (source, target) in enumerate(
            (
                (out_weight, out_weight_ref),
                (query_weight, query_weight_ref),
                (pair_weight, pair_weight_ref),
            )
        )
    ]

    @pl.when(pair == 0)
    def _():
        fill_weight(out_weight, quarters, home, (0, 1))
        fill_weight(query_weight, quarters, home, (width, 1))
        fill_weight(pair_weight, quarters, home, (2 * width, 1))
        for copy in copies:
            copy.start()
        fill_weight(cross_out_ref, quarters, home, (4 * width, 1))
        fill_weight(norm_rows, quarters, home, (5 * width, 1))
        norms = norm_rows[...].astype(FULL).T[0:8]
        norms_ref[...] = norms
        mixed = states[...].astype(FULL) + dot(mix[...], out_weight[...])
        unit, scale = normalise(mixed)
        unit_ref[...] = unit
        scale_ref[...] = jnp.broadcast_to(scale, (local, LANES))
        first_low = (unit * norms[0:1] + norms[3:4]).astype(LOW)
        project_queries(first_low, query_weight[...], queries)
        flags_q[...] = query_flags(target_lengths, place * local, local)
        prepare_wide(source_lengths, key_wide, place)
        project_rows((rows_0, rows_1, rows_2, rows_3), pair_weight, key_wide, values)

    query = queries[pair]
    query_ref[...] = query
    key_ref[...] = key_wide[pair, :, :LANES]
    value_ref[...] = values[pair]
    mixed = attend_pair(
        query, flags_q[...], key_wide.at[pair], values.at[pair], scores, kept
    )
    mix_ref[...] = mixed.astype(LOW)
    exact_ref[...] = mixed
    mixes[pair] = mixed.astype(LOW)

    @pl.when(pair == mixes.shape[0] - 1)
    def _():
        first_norm = unit_ref[...] * norms_ref[0:1] + norms_ref[3:4]
        whole_mix = jnp.concatenate([mixes[at] for at in range(mixes.shape[0])], axis=1)
        second_unit, second_scale = normalise(first_norm + dot(whole_mix, cross_out_ref[...]))
        second_unit_ref[...] = second_unit
        second_scale_ref[...] = jnp.broadcast_to(second_scale, (local, LANES))
        for copy in copies:
            copy.wait()


gelu_factor = 0.7978845608028654
gelu_cubic = 0.044715


def gelu_and_slope(hidden):
    square = hidden * hidden
    bend = jnp.tanh(gelu_factor * (hidden + gelu_cubic * (square * hidden)))
    half = 0.5 * (1.0 + bend)
    slope = half + (0.5 * hidden) * (1.0 - bend * bend) * (
        gelu_factor * (1.0 + (3.0 * gelu_cubic) * square)
    )
    return hidden * half, slope


def middle_kernel(info, second_unit, norms, out_grad, *refs):
    quarters = refs[:8]
    (
        output_ref,
        third_grad_ref,
        hidden_grads,
        expand,
        norm_sums_ref,
        kept,
        sent,
        contract,
        active,
        slope,
        wide_grad,
        tall_grad,
    ) = refs[8:]
    home = info[0]
    width = second_unit.shape[1]
    chunks = active.shape[0]
    span = expand.shape[1] // chunks
    fill_weight(expand, quarters, home, (0, 1))
    fill_weight(contract, quarters, home, (expand.shape[1], contract.shape[0] // width))
    second_norm = second_unit[...] * norms[1:2] + norms[4:5]
    second_low = second_norm.astype(LOW)

    def forward(at, total):
        start = pl.multiple_of(at * span, span)
        hidden = dot(second_low, expand[:, pl.ds(start, span)])
        made, bent = gelu_and_slope(hidden)
        made = made.astype(LOW)
        active[at] = made
        slope[at] = bent
        return total + dot(made, contract[pl.ds(start, span)])

    mixed = lax.fori_loop(0, chunks, forward, second_norm, unroll=True)
    third_unit, third_scale = normalise(mixed)
    output_ref[...] = third_unit * norms[2:3] + norms[5:6]
    third_grad, gain_three, bias_three = norm_backward(
        out_grad[...], third_unit, third_scale, norms[2:3]
    )
    third_grad_ref[...] = third_grad
    ffn_grad = third_grad.astype(LOW)
    second_turned = second_low.T

    def backward(at, carry):
        start = pl.multiple_of(at * span, span)
        part = contract[pl.ds(start, span)]
        hidden_grad = (dot(ffn_grad, part, BY_LANES) * slope[at]).astype(LOW)
        hidden_grads[at] = hidden_grad
        tall_grad[pl.ds(start, span)] = dot(active[at].T, ffn_grad).astype(LOW)
        wide_grad[:, pl.ds(start, span)] = dot(second_turned, hidden_grad).astype(LOW)
        return carry

    lax.fori_loop(0, chunks, backward, 0, unroll=True)
    norm_sums_ref[...] = jnp.zeros(norm_sums_ref.shape, FULL)
    norm_sums_ref[2:3] = gain_three
    norm_sums_ref[5:6] = bias_three
    pack_grad(wide_grad, kept, sent, home, (0, 1))
    pack_grad(tall_grad, kept, sent, home, (expand.shape[1], tall_grad.shape[0] // width))


def second_back_kernel(
    third_grad,
    hidden_grads,
    expand,
    second_unit,
    second_scale,
    norms,
    sums,
    mix,
    out_weight,
    second_grad_ref,
    mix_grad_ref,
    out_weight_grad,
    norm_sums_ref,
):
    cotangent = third_grad[...]
    chunks = hidden_grads.shape[0]
    span = expand.shape[1] // chunks
    for at in range(chunks):
        part = expand[:, at * span : (at + 1) * span]
        cotangent = cotangent + dot(hidden_grads[at], part, BY_LANES)
    second_grad, gain_two, bias_two = norm_backward(
        cotangent, second_unit[...], second_scale[:, 0:1], norms[1:2]
    )
    second_grad_ref[...] = second_grad
    cross_out_low = second_grad.astype(LOW)
    mix_grad_ref[...] = dot(cross_out_low, out_weight[...], BY_LANES).astype(LOW)
    out_weight_grad[...] = dot(mix[...].T, cross_out_low).astype(LOW)
    norm_sums_ref[...] = sums[...]
    norm_sums_ref[1:2] = gain_two
    norm_sums_ref[4:5] = bias_two


def attend_back_pair(query, key, value, kept, mix, low_grad, value_wide, made):
    rows = low_grad.shape[0]
    left = lane_numbers((rows, LANES)) < HEAD_DIM
    lane = lane_numbers((rows, LANES))
    value_wide[:, :LANES] = value
    product = low_grad.astype(FULL) * mix
    query_turned = query.T
    grad_turned = low_grad.T
    query_grads = []
    for head in range(2):
        mine = left if head == 0 else ~left
        inner = -jnp.sum(jnp.where(mine, product, 0.0), axis=1, keepdims=True)
        first, second, third = three_parts(inner)
        parts = jnp.where(lane == 0, first, jnp.where(lane == 1, second, jnp.where(lane == 2, third, 0.0)))
        wide = jnp.concatenate([jnp.where(mine, low_grad, jnp.zeros_like(low_grad)), parts.astype(LOW)], axis=1)
        weights = kept[head]
        shifted = dot(wide, value_wide[...], BY_LANES)
        score_grad = (weights.astype(FULL) * shifted).astype(LOW)
        query_grads.append(dot(score_grad, key))
        span = slice(head * HEAD_DIM, (head + 1) * HEAD_DIM)
        made[span] = dot(query_turned[span], score_grad).astype(LOW)
        made[LANES + head * HEAD_DIM : LANES + (head + 1) * HEAD_DIM] = dot(
            grad_turned[span], weights
        ).astype(LOW)
    return (jnp.where(left, query_grads[0], query_grads[1]) * score_scale).astype(LOW)


def cross_backward_kernel(
    query,
    key,
    value,
    kept,
    mix,
    grad,
    rows_0,
    rows_1,
    rows_2,
    rows_3,
    made,
    query_grad_ref,
    weight_grad_ref,
    value_wide,
):
    pair = pl.program_id(0)

    @pl.when(pair == 0)
    def _():
        value_wide[:, LANES:] = jnp.ones((value_wide.shape[0], LANES), LOW)

    query_grad_ref[...] = attend_back_pair(
        query[...], key[...], value[...], kept, mix[...], grad[...], value_wide, made.at[pair]
    )

    @pl.when(pair == made.shape[0] - 1)
    def _():
        finish_weight(made, (rows_0, rows_1, rows_2, rows_3), weight_grad_ref, 0)


def finish_rows(made, weight, first, own_ref, far_ref, core_ref):
    pairs, _, keys = made.shape
    local = keys // 4
    width = own_ref.shape[1]
    for step in range(4):
        total = None
        for pair in range(pairs):
            at = first + pair * LANES
            columns = jnp.concatenate(
                [weight[:, at : at + LANES], weight[:, width + at : width + at + LANES]], axis=1
            )
            part = made[pair, :, step * local : (step + 1) * local].T
            term = dot(part, columns, BY_LANES)
            total = term if total is None else total + term
        if step == 0:
            own_ref[...] = total
        elif step == 2:
            far_ref[...] = total.astype(LOW)
        else:
            core_ref[step // 2] = total.astype(LOW)


def finish_weight(made, row_refs, weight_grad_ref, first):
    local, width = row_refs[0].shape
    for pair in range(made.shape[0]):
        total = None
        for step in range(4):
            term = dot(made[pair, :, step * local : (step + 1) * local], row_refs[step][...])
            total = term if total is None else total + term
        total = total.T.astype(LOW)
        at = first + pair * LANES
        weight_grad_ref[:, at : at + LANES] = total[:, :LANES]
        weight_grad_ref[:, width + at : width + at + LANES] = total[:, LANES:]


def between_kernel(
    info, query_grad, second_grad, first_unit, first_scale, norms, norm_sums, self_mix, pair_grad, cross_out_grad, out_weight, query_weight, *refs
):
    (
        first_grad_ref,
        mix_grad_ref,
        kept,
        sent,
        out_grad,
        query_weight_grad,
        norm_grad,
        norm_rows,
    ) = refs
    home = info[0]
    width = self_mix.shape[1]
    unit = first_unit[...]
    first_low = (unit * norms[0:1] + norms[3:4]).astype(LOW)
    low_grad = query_grad[...]
    query_weight_grad[...] = dot(first_low.T, low_grad).astype(LOW)
    cotangent = second_grad[...] + dot(low_grad, query_weight[...], BY_LANES)
    first_grad, gain_one, bias_one = norm_backward(
        cotangent, unit, first_scale[:, 0:1], norms[0:1]
    )
    first_grad_ref[...] = first_grad
    self_out_low = first_grad.astype(LOW)
    out_grad[...] = dot(self_mix[...].T, self_out_low).astype(LOW)
    mix_grad_ref[...] = dot(self_out_low, out_weight[...], BY_LANES).astype(LOW)
    norm_rows[...] = jnp.zeros(norm_rows.shape, FULL)
    norm_rows[0:8] = norm_sums[...]
    norm_rows[0:1] = gain_one
    norm_rows[3:4] = bias_one
    norm_grad[...] = norm_rows[...].T.astype(LOW)
    pack_grad(out_grad, kept, sent, home, (0, 1))
    pack_grad(query_weight_grad, kept, sent, home, (width, 1))
    pack_grad(pair_grad, kept, sent, home, (2 * width, 1))
    pack_grad(cross_out_grad, kept, sent, home, (4 * width, 1))
    pack_grad(norm_grad, kept, sent, home, (5 * width, 1))


def self_backward_kernel(
    info,
    query,
    key,
    value,
    kept_weights,
    mix,
    grad,
    rows_0,
    rows_1,
    rows_2,
    rows_3,
    made,
    query_grad_ref,
    kept,
    sent,
    value_wide,
    query_grads,
    weight_grad,
):
    pair = pl.program_id(0)
    width = rows_0.shape[1]
    pairs = made.shape[0]

    @pl.when(pair == 0)
    def _():
        value_wide[:, LANES:] = jnp.ones((value_wide.shape[0], LANES), LOW)

    query_grads[pair] = attend_back_pair(
        query[...], key[...], value[...], kept_weights, mix[...], grad[...], value_wide, made.at[pair]
    )

    @pl.when(pair == pairs - 1)
    def _():
        finish_weight(made, (rows_0, rows_1, rows_2, rows_3), weight_grad, width)
        low_grad = jnp.concatenate([query_grads[at] for at in range(pairs)], axis=1)
        query_grad_ref[...] = low_grad
        weight_grad[:, 0:width] = dot(rows_0[...].T, low_grad).astype(LOW)
        pack_grad(weight_grad, kept, sent, info[0], (0, 1))


def memory_kernel(made, weight, own_ref, far_ref, core_ref):
    finish_rows(made, weight, 0, own_ref, far_ref, core_ref)


def states_kernel(made, query_grad, first_grad, weight, own_ref, far_ref, core_ref):
    width = own_ref.shape[1]
    finish_rows(made, weight, width, own_ref, far_ref, core_ref)
    own_ref[...] += first_grad[...] + dot(query_grad[...], weight[:, 0:width], BY_LANES)


def whole(shape):
    return pl.BlockSpec(shape, lambda *at: (0,) * len(shape))


def call(kernel, inputs, specs, outputs, out_specs, scratch, grid=(), micros=1, mib=58):
    moved = sum(math.prod(a.shape) * a.dtype.itemsize for a in list(inputs) + list(outputs))
    return pl.pallas_call(
        kernel,
        out_shape=outputs,
        grid=grid,
        in_specs=specs,
        out_specs=out_specs,
        scratch_shapes=scratch,
        compiler_params=pltpu.CompilerParams(vmem_limit_bytes=mib * 2**20),
        cost_estimate=pl.CostEstimate(flops=micros * 10**9, bytes_accessed=moved, transcendentals=0),
    )(*inputs)


SCALARS = pl.BlockSpec(memory_space=pltpu.SMEM)


def shaped(shape, kind):
    return jax.ShapeDtypeStruct(shape, kind)


def per_device(
    target_states,
    memory,
    target_lengths,
    source_lengths,
    self_project,
    self_output,
    cross_project,
    memory_project,
    cross_output,
    expand_weight,
    contract_weight,
    norm_gain,
    norm_bias,
    out_grad,
):
    _, local, width = target_states.shape
    states = target_states[0]
    own_memory = memory[0]
    rows = self_project.shape[0]
    ff = expand_weight.shape[1]
    keys = local * 4
    pairs = width // LANES
    info = jnp.stack([home_number(), lax.axis_index("narrow")]).astype(jnp.int32)

    batches = 3 * width, 5 * width + LANES, 2 * ff
    if staged():
        shards = (
            self_output,
            cross_project,
            memory_project,
            cross_output,
            expand_weight,
            contract_weight,
            norm_gain,
            norm_bias,
        )
        later = batches[1] + batches[2]
        batch_23 = call(
            pack_kernel,
            list(shards),
            [whole(shard.shape) for shard in shards],
            [shaped((rows, later), LOW)],
            [whole((rows, later))],
            [pltpu.VMEM((LANES, LANES), FULL)],
        )[0]
        far_1 = jnp.stack(gather_far(self_project))
        states_x = exchange(states, 2)
        states_c = exchange(states, 1)
        (batch_23, states_c), far_1 = after((batch_23, states_c), far_1)
        near_23 = exchange(batch_23, FAR[0])
        plane_1 = gather_plane(far_1)
        near_23, states_x = after(near_23, states_x)
        own_memory, states_c = after(own_memory, states_c)
        half_2 = jnp.stack([batch_23[:, : batches[1]], near_23[:, : batches[1]]])
        half_3 = jnp.stack([batch_23[:, batches[1] :], near_23[:, batches[1] :]])
        rest_2 = exchange(half_2, FAR[1])
        memory_x = exchange(own_memory, 2)
        half_3, rest_2 = after(half_3, rest_2)
        far_2 = jnp.concatenate([half_2, rest_2])
        rest_3 = exchange(half_3, FAR[1])
    else:
        norm_shard = jnp.concatenate([norm_gain, norm_bias], axis=0).T
        norm_shard = jnp.pad(norm_shard, ((0, 0), (0, LANES - norm_shard.shape[1])))
        folded = fold_rows(contract_weight, rows)
        plane_1 = self_project
        far_2 = jnp.concatenate(
            [self_output, cross_project, memory_project, cross_output, norm_shard], axis=1
        )
        far_3 = jnp.concatenate([expand_weight, folded], axis=1)
        states_x = exchange(states, 2)
        states_c = exchange(states, 1)
        memory_c = exchange(own_memory, 1)
        memory_x = exchange(own_memory, 2)
    states_xc = exchange(states_x, 1)
    far_2, plane_1 = after(far_2, plane_1)
    weights_1 = gather_core(plane_1)
    row_states = [states, states_c, states_x, states_xc]
    own_2 = exchange(far_2, 1) if staged() else None
    if staged():
        row_states[1], own_2 = after(row_states[1], own_2)
    plane_2 = gather_plane(far_2)

    row_spec = whole((local, width))
    pair_rows = pl.BlockSpec((local, LANES), lambda pair: (0, pair))
    pair_keys = pl.BlockSpec((keys, LANES), lambda pair: (0, pair))
    pair_kept = pl.BlockSpec((2, local, keys), lambda pair: (pair, 0, 0))
    quarter_specs_1 = [whole(q.shape) for q in weights_1]
    attend_scratch = [
        pltpu.VMEM((pairs, local, LANES), LOW),
        pltpu.VMEM((local, LANES), LOW),
        pltpu.VMEM((pairs, keys, 2 * LANES), LOW),
        pltpu.VMEM((pairs, keys, LANES), LOW),
        pltpu.VMEM((2, local, keys), FULL),
    ]
    attend_outputs = [
        shaped((local, width), LOW),
        pltpu.HBM((local, width), LOW),
        pltpu.HBM((local, width), FULL),
        pltpu.HBM((keys, width), LOW),
        pltpu.HBM((keys, width), LOW),
        pltpu.HBM((2 * pairs, local, keys), LOW),
    ]
    attend_specs = [pair_rows] * 3 + [pair_keys, pair_keys, pair_kept]
    in_place = pl.BlockSpec(memory_space=pl.ANY)
    self_mix, self_query, self_exact, self_key, self_value, self_kept, self_weight = call(
        self_forward_kernel,
        [info, target_lengths, *row_states, *weights_1],
        [SCALARS, SCALARS] + [row_spec] * 4 + quarter_specs_1,
        attend_outputs + [pltpu.HBM((width, 3 * width), LOW)],
        attend_specs + [in_place],
        [pltpu.VMEM((width, 3 * width), LOW), pltpu.SemaphoreType.DMA] + attend_scratch,
        grid=(pairs,),
        micros=25, mib=38,
    )

    if staged():
        (memory_x, own_memory, rest_3), self_mix = after((memory_x, own_memory, rest_3), self_mix)
        memory_c = exchange(own_memory, 1)
        far_3 = jnp.concatenate([half_3, rest_3])
    plane_2, self_mix = after(plane_2, self_mix)
    own_3 = exchange(far_3, 1) if staged() else None
    memory_xc = exchange(memory_x, 1)
    weights_2 = gather_core(plane_2, own_2)
    row_memory = [own_memory, memory_c, memory_x, memory_xc]
    plane_3 = gather_plane(far_3)
    quarter_specs_2 = [whole(q.shape) for q in weights_2]
    wide_scale = whole((local, LANES))
    norm_spec = whole((8, width))
    square = whole((width, width))
    (
        cross_mix,
        cross_query,
        cross_exact,
        cross_key,
        cross_value,
        cross_kept,
        first_unit,
        first_scale,
        norms,
        second_unit,
        second_scale,
        cross_out_weight,
        out_weight,
        query_weight,
        pair_weight,
    ) = call(
        cross_forward_kernel,
        [info, target_lengths, source_lengths, self_mix, states, *row_memory, *weights_2],
        [SCALARS] * 3 + [row_spec] * 6 + quarter_specs_2,
        attend_outputs
        + [
            pltpu.HBM((local, width), FULL),
            pltpu.HBM((local, LANES), FULL),
            shaped((8, width), FULL),
            shaped((local, width), FULL),
            shaped((local, LANES), FULL),
            shaped((width, width), LOW),
            pltpu.HBM((width, width), LOW),
            pltpu.HBM((width, width), LOW),
            pltpu.HBM((width, 2 * width), LOW),
        ],
        attend_specs + [row_spec, wide_scale, norm_spec, row_spec, wide_scale, square] + [in_place] * 3,
        [
            pltpu.VMEM((width, width), LOW),
            pltpu.VMEM((width, width), LOW),
            pltpu.VMEM((width, 2 * width), LOW),
            pltpu.VMEM((width, LANES), LOW),
            pltpu.SemaphoreType.DMA((3,)),
            pltpu.VMEM((pairs, local, LANES), LOW),
        ]
        + attend_scratch,
        grid=(pairs,),
        micros=25, mib=46,
    )

    plane_3, second_unit = after(plane_3, second_unit)
    weights_3 = gather_core(plane_3, own_3, ff // width)
    quarter_specs_3 = [whole(q.shape) for q in weights_3]
    chunk_count = ff // width
    packed_3 = (4, 4, TILE_ROWS, 2 * ff)
    hidden_shape = (chunk_count, local, width)
    output, third_grad, hidden_grads, expand_whole, norm_sums, kept_3, sent_3 = call(
        middle_kernel,
        [info, second_unit, norms, out_grad[0], *weights_3],
        [SCALARS, row_spec, norm_spec, row_spec] + quarter_specs_3,
        [
            shaped((local, width), FULL),
            shaped((local, width), FULL),
            shaped(hidden_shape, LOW),
            shaped((width, ff), LOW),
            shaped((8, width), FULL),
            shaped(packed_3, LOW),
            shaped(packed_3, LOW),
        ],
        [row_spec, row_spec, whole(hidden_shape), whole((width, ff)), norm_spec]
        + [whole(packed_3), whole(packed_3)],
        [
            pltpu.VMEM((ff, width), LOW),
            pltpu.VMEM(hidden_shape, LOW),
            pltpu.VMEM(hidden_shape, FULL),
            pltpu.VMEM((width, ff), LOW),
            pltpu.VMEM((ff, width), LOW),
        ],
        micros=14, mib=34,
    )
    other_3 = exchange_core(sent_3)
    second_grad, cross_mix_grad, cross_out_grad, norm_sums = call(
        second_back_kernel,
        [
            third_grad,
            hidden_grads,
            expand_whole,
            second_unit,
            second_scale,
            norms,
            norm_sums,
            cross_mix,
            cross_out_weight,
        ],
        [row_spec, whole(hidden_shape), whole((width, ff))]
        + [row_spec, wide_scale, norm_spec, norm_spec, row_spec, square],
        [
            shaped((local, width), FULL),
            shaped((local, width), LOW),
            shaped((width, width), LOW),
            shaped((8, width), FULL),
        ],
        [row_spec, row_spec, square, norm_spec],
        [],
        micros=4, mib=12,
    )
    other_3, cross_mix_grad = after(other_3, cross_mix_grad)
    core_3 = reduce_core(kept_3, other_3)
    core_3, cross_mix_grad = after(core_3, cross_mix_grad)
    planes_3 = exchange_plane(core_3)

    back_specs = [pair_rows, pair_keys, pair_keys, pair_kept, pair_rows, pair_rows]
    made_shape = (pairs, 2 * LANES, keys)
    cross_made, cross_query_grad, pair_weight_grad = call(
        cross_backward_kernel,
        [
            cross_query,
            cross_key,
            cross_value,
            cross_kept,
            cross_exact,
            cross_mix_grad,
            *row_memory,
        ],
        back_specs + [row_spec] * 4,
        [
            shaped(made_shape, LOW),
            shaped((local, width), LOW),
            shaped((width, 2 * width), LOW),
        ],
        [whole(made_shape), pair_rows, whole((width, 2 * width))],
        [pltpu.VMEM((keys, 2 * LANES), LOW)],
        grid=(pairs,),
        micros=33, mib=36,
    )
    planes_3, cross_query_grad = after(planes_3, cross_query_grad)
    plane_sum_3 = reduce_plane(planes_3)
    plane_sum_3, cross_query_grad = after(plane_sum_3, cross_query_grad)
    half_sum_3 = exchange_half(plane_sum_3)

    packed_2 = (4, 4, TILE_ROWS, 5 * width + LANES)
    first_grad, self_mix_grad, kept_2, sent_2 = call(
        between_kernel,
        [
            info,
            cross_query_grad,
            second_grad,
            first_unit,
            first_scale,
            norms,
            norm_sums,
            self_mix,
            pair_weight_grad,
            cross_out_grad,
            out_weight,
            query_weight,
        ],
        [SCALARS, row_spec, row_spec, row_spec, whole((local, LANES))]
        + [whole((8, width))] * 2
        + [row_spec, whole((width, 2 * width)), whole((width, width))]
        + [square] * 2,
        [
            shaped((local, width), FULL),
            shaped((local, width), LOW),
            shaped(packed_2, LOW),
            shaped(packed_2, LOW),
        ],
        [row_spec, row_spec, whole(packed_2), whole(packed_2)],
        [
            pltpu.VMEM((width, width), LOW),
            pltpu.VMEM((width, width), LOW),
            pltpu.VMEM((width, LANES), LOW),
            pltpu.VMEM((LANES, width), FULL),
        ],
        micros=6, mib=14,
    )
    other_2 = exchange_core(sent_2)
    cross_made, sent_2 = after(cross_made, sent_2)
    rows_shapes = [
        shaped((local, width), FULL),
        shaped((local, width), LOW),
        shaped((2, local, width), LOW),
    ]
    rows_specs = [row_spec, row_spec, whole((2, local, width))]
    memory_own, memory_far_part, memory_parts = call(
        memory_kernel,
        [cross_made, pair_weight],
        [whole(made_shape), whole((width, 2 * width))],
        rows_shapes,
        rows_specs,
        [],
        micros=3, mib=20,
    )
    other_2, memory_parts = after(other_2, memory_parts)
    memory_sent = exchange(memory_parts, 1)
    core_2 = reduce_core(kept_2, other_2)
    memory_other = reduce_row_core(memory_far_part, memory_sent)
    (core_2, memory_other), self_mix_grad = after((core_2, memory_other), self_mix_grad)
    planes_2 = exchange_plane(core_2)
    memory_far = exchange(memory_other, 2)

    packed_1 = (4, 4, TILE_ROWS, 3 * width)
    made, self_query_grad, kept_1, sent_1 = call(
        self_backward_kernel,
        [
            info,
            self_query,
            self_key,
            self_value,
            self_kept,
            self_exact,
            self_mix_grad,
            *row_states,
        ],
        [SCALARS] + back_specs + [row_spec] * 4,
        [
            shaped(made_shape, LOW),
            shaped((local, width), LOW),
            shaped(packed_1, LOW),
            shaped(packed_1, LOW),
        ],
        [whole(made_shape), row_spec, whole(packed_1), whole(packed_1)],
        [
            pltpu.VMEM((keys, 2 * LANES), LOW),
            pltpu.VMEM((pairs, local, LANES), LOW),
            pltpu.VMEM((width, 3 * width), LOW),
        ],
        grid=(pairs,),
        micros=33, mib=36,
    )
    (planes_2, memory_far, half_sum_3), (sent_1, kept_1) = after(
        (planes_2, memory_far, half_sum_3), (sent_1, kept_1)
    )
    other_1 = exchange_core(sent_1)
    states_own, states_far_part, states_parts = call(
        states_kernel,
        [made, self_query_grad, first_grad, self_weight],
        [whole(made_shape), row_spec, row_spec, whole((width, 3 * width))],
        rows_shapes,
        rows_specs,
        [],
        micros=4, mib=20,
    )
    other_1, states_parts = after(other_1, states_parts)
    core_1 = reduce_core(kept_1, other_1)
    planes_1 = exchange_plane(core_1)
    states_sent = exchange(states_parts, 1)
    (planes_2, half_sum_3, memory_far), core_1 = after((planes_2, half_sum_3, memory_far), core_1)
    plane_sum_2 = reduce_plane(planes_2)
    half_sum_2 = exchange_half(plane_sum_2)
    states_other = reduce_row_core(states_far_part, states_sent)
    (half_sum_2, half_sum_3), states_other = after((half_sum_2, half_sum_3), states_other)
    states_far = exchange(states_other, 2)
    total_3 = reduce_half(plane_sum_3, half_sum_3)
    total_2 = reduce_half(plane_sum_2, half_sum_2)
    planes_1, (total_2, total_3, states_other) = after(planes_1, (total_2, total_3, states_other))
    plane_sum_1 = reduce_plane(planes_1)
    fars_1 = exchange_far(plane_sum_1)
    memory_grad = reduce_row(memory_own, memory_sent, memory_far)
    states_grad = reduce_row(states_own, states_sent, states_far)
    count = norm_gain.shape[0]
    if staged():
        near = exchange(jnp.concatenate([total_2[1], total_3[1]], axis=1), FAR[0])
        settled = [
            shaped((rows, width), FULL),
            shaped((rows, width), FULL),
            shaped((rows, 2 * width), FULL),
            shaped((rows, width), FULL),
            shaped((rows, ff), FULL),
            shaped((rows * ff // width, width), FULL),
            shaped(norm_gain.shape, FULL),
            shaped(norm_gain.shape, FULL),
        ]
        out, cross, pairs_grad, cross_out, expand_grad, contract_grad, gain, bias = call(
            settle_kernel,
            [total_2[0], total_3[0], near],
            [whole((rows, batches[1])), whole((rows, batches[2])), whole((rows, later))],
            settled,
            [whole(each.shape) for each in settled],
            [pltpu.VMEM((LANES, LANES), FULL)],
            mib=8,
        )
        fars_1, out = after(fars_1, out)
        project = reduce_far(fars_1)
    else:
        grad_3 = reduce_far(total_3, ff // width)
        grad_2 = reduce_far(total_2)
        project = reduce_far(fars_1)
        expand_grad, contract_grad = grad_3[:, :ff], unfold_rows(grad_3[:, ff:], width)
        out, cross = grad_2[:, :width], grad_2[:, width : 2 * width]
        pairs_grad, cross_out = grad_2[:, 2 * width : 4 * width], grad_2[:, 4 * width : 5 * width]
        norm_grads = grad_2[:, 5 * width :].T
        gain, bias = norm_grads[:count], norm_grads[count : 2 * count]
    return (
        output[None],
        states_grad[None],
        memory_grad[None],
        project,
        out,
        cross,
        pairs_grad,
        cross_out,
        expand_grad,
        contract_grad,
        gain,
        bias,
    )


def reduce_row_core(part, sent):
    return add_all(part, [sent[1]]).astype(LOW)


def reduce_row(own, sent, far):
    return add_all(own, [sent[0], far])


def solution(mesh):
    in_specs = (
        P("wide", "narrow", None),
        P("wide", "narrow", None),
        P("wide", None),
        P("wide", None),
        P(("wide", "narrow"), None),
        P(("wide", "narrow"), None),
        P(("wide", "narrow"), None),
        P(("wide", "narrow"), None),
        P(("wide", "narrow"), None),
        P(("wide", "narrow"), None),
        P(("wide", "narrow"), None),
        P(None, ("wide", "narrow")),
        P(None, ("wide", "narrow")),
        P("wide", "narrow", None),
    )
    out_specs = (
        P("wide", "narrow", None),
        P("wide", "narrow", None),
        P("wide", "narrow", None),
        P(("wide", "narrow"), None),
        P(("wide", "narrow"), None),
        P(("wide", "narrow"), None),
        P(("wide", "narrow"), None),
        P(("wide", "narrow"), None),
        P(("wide", "narrow"), None),
        P(("wide", "narrow"), None),
        P(None, ("wide", "narrow")),
        P(None, ("wide", "narrow")),
    )
    return jax.shard_map(
        per_device, mesh=mesh, in_specs=in_specs, out_specs=out_specs, check_vma=False
    )
```

```python
import functools
import math

import jax
import jax.numpy as jnp
from jax import lax
from jax.experimental import pallas as pl
from jax.experimental.pallas import tpu as pltpu
from jax.sharding import PartitionSpec as P

HEAD_DIM = 64
LANES = 128
TILE_ROWS = 16
BLOCKS = 32
AXES = ("wide", "narrow")
LOW = jnp.bfloat16
FULL = jnp.float32

ln_eps = 1e-05
score_scale = HEAD_DIM ** (-0.5)
mask_step = -(2.0**30)

BY_LANES = (((1,), (1,)), ((), ()))
PLAIN = (((1,), (0,)), ((), ()))


def dot(left, right, dims=PLAIN):
    return lax.dot_general(left, right, dims, preferred_element_type=FULL)


def exchange(block, mask):
    device_count = lax.axis_size("wide") * lax.axis_size("narrow")
    pairs = [(device, device ^ mask) for device in range(device_count)]
    return lax.ppermute(block, AXES, pairs)


def device_number():
    return lax.axis_index("wide") * lax.axis_size("narrow") + lax.axis_index("narrow")


def staged():
    return lax.axis_size("wide") * lax.axis_size("narrow") == BLOCKS


FAR = (8, 16, 24)
PLANE = (2, 4, 6)


def gather_far(shard):
    if not staged():
        return shard
    return [shard] + [exchange(shard, mask) for mask in FAR]


def gather_plane(held):
    if not staged():
        return held
    return [held] + [exchange(held, mask) for mask in PLANE]


def gather_core(held, own=None, folds=0):
    if staged():
        first = exchange(held[0], 1) if own is None else own
        return held + [first] + [exchange(quarter, 1) for quarter in held[1:]]
    whole = lax.all_gather(held, AXES, axis=0, tiled=True)
    if folds:
        rows, columns = held.shape
        split = columns - folds * whole.shape[0]
        tall = unfold_rows(held[:, split:], whole.shape[0])
        tall = lax.all_gather(tall, AXES, axis=0, tiled=True)
        tall = tall.reshape(BLOCKS, folds, TILE_ROWS, -1).transpose(0, 2, 1, 3)
        whole = jnp.concatenate([whole[:, :split], tall.reshape(whole.shape[0], -1)], axis=1)
    whole = whole.reshape(4, 4, 2, TILE_ROWS, held.shape[1]).transpose(2, 1, 0, 3, 4)
    return [whole[core, plane] for core in range(2) for plane in range(4)]


def home_number():
    return device_number() if staged() else jnp.zeros((), jnp.int32)


def block_number(home, core, plane, far):
    return home ^ (far * 8 + plane * 2 + core)


def add_all(first, others):
    total = first.astype(FULL)
    for other in others:
        total = total + other.astype(FULL)
    return total


def exchange_core(sent):
    return exchange(sent, 1) if staged() else sent


def reduce_core(kept, other):
    return add_all(kept, [other]).astype(LOW) if staged() else (kept, other)


def exchange_plane(held):
    if not staged():
        return held
    return [held[0]] + [exchange(held[plane + 1], mask) for plane, mask in enumerate(PLANE)]


def reduce_plane(planes):
    return add_all(planes[0], planes[1:]).astype(LOW) if staged() else planes


def exchange_far(held):
    if not staged():
        return held
    return [held[0]] + [exchange(held[far + 1], mask) for far, mask in enumerate(FAR)]


def exchange_half(held):
    return exchange(held[2:], FAR[1]) if staged() else held


def reduce_half(held, other):
    return add_all(held[:2], [other]).astype(LOW) if staged() else held


def reduce_far(held, folds=0):
    if staged():
        return add_all(held[0], held[1:])
    whole = jnp.stack(held).transpose(2, 1, 0, 3, 4)
    whole = whole.reshape(BLOCKS * TILE_ROWS, -1).astype(FULL)
    if folds:
        split = whole.shape[1] - folds * whole.shape[0]
        tall = whole[:, split:].reshape(BLOCKS, TILE_ROWS, folds, -1).transpose(0, 2, 1, 3)
        tall = tall.reshape(folds * whole.shape[0], -1)
        tall = lax.psum_scatter(tall, AXES, scatter_dimension=0, tiled=True)
        whole = lax.psum_scatter(whole[:, :split], AXES, scatter_dimension=0, tiled=True)
        return jnp.concatenate([whole, fold_rows(tall, whole.shape[0])], axis=1)
    return lax.psum_scatter(whole, AXES, scatter_dimension=0, tiled=True)


def after(values, token):
    return lax.optimization_barrier((values, token))


def fold_rows(block, rows):
    return jnp.concatenate(
        [block[at : at + rows] for at in range(0, block.shape[0], rows)], axis=1
    )


def unfold_rows(block, width):
    return jnp.concatenate(
        [block[:, at : at + width] for at in range(0, block.shape[1], width)], axis=0
    )


def lane_numbers(shape):
    return lax.broadcasted_iota(jnp.int32, shape, 1)


def segment_bounds(lengths_ref):
    lane = lane_numbers((1, LANES))
    first = jnp.full((1, LANES), 2**30, jnp.int32)
    last = jnp.zeros((1, LANES), jnp.int32)
    start = jnp.int32(0)
    count = lengths_ref.shape[1]
    for segment in range(count + 1):
        end = start + lengths_ref[0, segment] if segment < count else jnp.int32(2**30)
        first = jnp.where(lane == segment, start, first)
        last = jnp.where(lane == segment, end, last)
        start = end
    return first, last


def segment_flags(start, rows, bounds):
    position = start + lax.broadcasted_iota(jnp.int32, (rows, LANES), 0)
    return (position >= bounds[0]) & (position < bounds[1])


def three_parts(value):
    first = value.astype(LOW)
    rest = value - first.astype(FULL)
    second = rest.astype(LOW)
    third = (rest - second.astype(FULL)).astype(LOW)
    return first.astype(FULL), second.astype(FULL), third.astype(FULL)


def query_flags(lengths_ref, start, rows):
    segments = lengths_ref.shape[1] + 1
    own = segment_flags(start, rows, segment_bounds(lengths_ref))
    return jnp.where(own | (lane_numbers((rows, LANES)) >= segments), 0.0, mask_step).astype(LOW)


def key_flags(lengths_ref, start, rows):
    own = segment_flags(start, rows, segment_bounds(lengths_ref))
    return jnp.where(own, 1.0, 0.0).astype(LOW)


def fill_weight(target, quarters, home, columns):
    first, folds = columns
    width = target.shape[1]
    for core in range(2):
        for plane in range(4):
            for far in range(4):
                block = block_number(home, core, plane, far)
                piece = quarters[core * 4 + plane]
                for fold in range(folds):
                    row = pl.multiple_of(block * (TILE_ROWS * folds) + fold * TILE_ROWS, TILE_ROWS)
                    start = first + fold * width
                    target[pl.ds(row, TILE_ROWS), :] = piece[far, :, start : start + width]


def pack_grad(source, kept, sent, home, columns):
    first, folds = columns
    width = source.shape[1]
    for core, target in ((0, kept), (1, sent)):
        for plane in range(4):
            for far in range(4):
                block = block_number(home, core, plane, far)
                for fold in range(folds):
                    row = pl.multiple_of(block * (TILE_ROWS * folds) + fold * TILE_ROWS, TILE_ROWS)
                    start = first + fold * width
                    target[plane, far, :, start : start + width] = source[pl.ds(row, TILE_ROWS), :]


def normalise(states):
    centred = states - jnp.mean(states, axis=1, keepdims=True)
    spread = jnp.mean(centred * centred, axis=1, keepdims=True)
    scale = lax.rsqrt(spread + ln_eps)
    return centred * scale, scale


def norm_backward(cotangent, unit, scale, gain):
    scaled = cotangent * gain
    grad = scale * (
        scaled
        - jnp.mean(scaled, axis=1, keepdims=True)
        - unit * jnp.mean(scaled * unit, axis=1, keepdims=True)
    )
    return (
        grad,
        jnp.sum(cotangent * unit, axis=0, keepdims=True),
        jnp.sum(cotangent, axis=0, keepdims=True),
    )


KEY_STEP = 256


def pack_kernel(*refs):
    ins, (packed, square) = refs[:8], refs[8:]
    self_output, cross_project, memory_project, cross_output, expand, contract, gain, bias = ins
    rows, width = self_output.shape
    at = 0
    for part in (self_output, cross_project, memory_project, cross_output):
        packed[:, at : at + part.shape[1]] = part[...]
        at += part.shape[1]
    count = gain.shape[0]
    square[...] = jnp.zeros(square.shape, FULL)
    square[0:count, 0:rows] = gain[...].astype(FULL)
    square[count : 2 * count, 0:rows] = bias[...].astype(FULL)
    packed[:, at : at + LANES] = square[...].T[0:rows].astype(LOW)
    at += LANES
    packed[:, at : at + expand.shape[1]] = expand[...]
    at += expand.shape[1]
    for fold in range(contract.shape[0] // rows):
        packed[:, at : at + width] = contract[fold * rows : (fold + 1) * rows]
        at += width


def settle_kernel(part_2, part_3, other, *refs):
    output_ref, cross_ref, memory_ref, cross_out_ref, expand_ref, contract_ref, gain_ref, bias_ref, square = refs
    rows, width = output_ref.shape
    split = part_2.shape[1]
    total = add_all(part_2[...], [other[:, :split]])
    at = 0
    for ref in (output_ref, cross_ref, memory_ref, cross_out_ref):
        ref[...] = total[:, at : at + ref.shape[1]]
        at += ref.shape[1]
    square[...] = jnp.zeros(square.shape, FULL)
    square[0:rows] = total[:, at : at + LANES]
    turned = square[...].T
    count = gain_ref.shape[0]
    gain_ref[...] = turned[0:count, 0:rows]
    bias_ref[...] = turned[count : 2 * count, 0:rows]
    total = add_all(part_3[...], [other[:, split:]])
    span = expand_ref.shape[1]
    expand_ref[...] = total[:, :span]
    for fold in range(contract_ref.shape[0] // rows):
        at = span + fold * width
        contract_ref[fold * rows : (fold + 1) * rows] = total[:, at : at + width]


def attend_pair(query, flags, key_wide, values, scores, kept):
    rows = query.shape[0]
    keys = key_wide.shape[0]
    left = lane_numbers((rows, LANES)) < HEAD_DIM
    zero = jnp.zeros_like(query)
    queries = [
        jnp.concatenate([jnp.where(left, query, zero), flags], axis=1),
        jnp.concatenate([jnp.where(left, zero, query), flags], axis=1),
    ]

    def score(head, start, peak):
        made = dot(queries[head], key_wide[start : start + KEY_STEP], BY_LANES)
        scores[head, :, start : start + KEY_STEP] = made
        for at in range(0, KEY_STEP, LANES):
            peak = jnp.maximum(peak, made[:, at : at + LANES])
        return peak

    def raise_scores(head, start, peak, total):
        span = slice(start, start + KEY_STEP)
        weights = jnp.exp(scores[head, :, span] - peak)
        for at in range(0, KEY_STEP, LANES):
            total = total + weights[:, at : at + LANES]
        return total

    def weigh(head, start, shift, total):
        span = slice(start, start + KEY_STEP)
        probs = jnp.exp(scores[head, :, span] - shift).astype(LOW)
        kept[head, :, span] = probs
        return total + dot(probs, values[span])

    steps = range(0, keys, KEY_STEP)
    lowest = jnp.full((rows, LANES), -jnp.inf, FULL)
    empty = jnp.zeros((rows, LANES), FULL)
    peak = lowest
    for start in steps:
        peak = score(0, start, peak)
    first_peak = jnp.max(peak, axis=1, keepdims=True)
    peak, first_total = lowest, empty
    for start in steps:
        peak = score(1, start, peak)
        first_total = raise_scores(0, start, first_peak, first_total)
    second_peak = jnp.max(peak, axis=1, keepdims=True)
    first_shift = first_peak + jnp.log(jnp.sum(first_total, axis=1, keepdims=True))
    first, second_total = empty, empty
    for start in steps:
        second_total = raise_scores(1, start, second_peak, second_total)
        first = weigh(0, start, first_shift, first)
    second_shift = second_peak + jnp.log(jnp.sum(second_total, axis=1, keepdims=True))
    second = empty
    for start in steps:
        second = weigh(1, start, second_shift, second)
    return jnp.where(left, first, second)


def pair_columns(first, pair):
    return pl.ds(pl.multiple_of(first + pair * LANES, LANES), LANES)


def prepare_wide(lengths, key_wide, place):
    pairs, keys, _ = key_wide.shape
    local = keys // 4
    for step in range(4):
        span = slice(step * local, (step + 1) * local)
        flags = key_flags(lengths, (place ^ step) * local, local)
        for pair in range(pairs):
            key_wide[pair, span, LANES:] = flags


def project_rows(rows, weight, key_wide, values):
    pairs = key_wide.shape[0]
    local = rows[0].shape[0]
    for step, part in enumerate(rows):
        span = slice(step * local, (step + 1) * local)
        for target, first in ((key_wide, 0), (values, pairs * LANES)):
            made = dot(part[...], weight[:, first : first + pairs * LANES]).astype(LOW)
            for pair in range(pairs):
                target[pair, span, :LANES] = made[:, pair * LANES : (pair + 1) * LANES]


def project_queries(rows, weight, queries):
    made = dot(rows, weight).astype(LOW).astype(FULL) * score_scale
    for pair in range(queries.shape[0]):
        queries[pair] = made[:, pair * LANES : (pair + 1) * LANES].astype(LOW)


def self_forward_kernel(info, lengths, rows_0, rows_1, rows_2, rows_3, *refs):
    quarters = refs[:8]
    (
        mix_ref,
        query_ref,
        exact_ref,
        key_ref,
        value_ref,
        kept,
        weight_ref,
        weight,
        saved,
        queries,
        flags_q,
        key_wide,
        values,
        scores,
    ) = refs[8:]
    pair = pl.program_id(0)
    home, place = info[0], info[1]
    local, width = rows_0.shape

    @pl.when(pair == 0)
    def _():
        fill_weight(weight, quarters, home, (0, 1))
        pltpu.make_async_copy(weight, weight_ref, saved).start()
        flags_q[...] = query_flags(lengths, place * local, local)
        prepare_wide(lengths, key_wide, place)
        project_rows((rows_0, rows_1, rows_2, rows_3), weight.at[:, width:], key_wide, values)
        project_queries(rows_0[...], weight[:, :width], queries)

    query = queries[pair]
    query_ref[...] = query
    key_ref[...] = key_wide[pair, :, :LANES]
    value_ref[...] = values[pair]
    mix = attend_pair(
        query, flags_q[...], key_wide.at[pair], values.at[pair], scores, kept
    )
    mix_ref[...] = mix.astype(LOW)
    exact_ref[...] = mix

    @pl.when(pair == queries.shape[0] - 1)
    def _():
        pltpu.make_async_copy(weight, weight_ref, saved).wait()


def cross_forward_kernel(
    info, target_lengths, source_lengths, mix, states, rows_0, rows_1, rows_2, rows_3, *refs
):
    quarters = refs[:8]
    (
        mix_ref,
        query_ref,
        exact_ref,
        key_ref,
        value_ref,
        kept,
        unit_ref,
        scale_ref,
        norms_ref,
        second_unit_ref,
        second_scale_ref,
        cross_out_ref,
        out_weight_ref,
        query_weight_ref,
        pair_weight_ref,
        out_weight,
        query_weight,
        pair_weight,
        norm_rows,
        saved,
        mixes,
        queries,
        flags_q,
        key_wide,
        values,
        scores,
    ) = refs[8:]
    pair = pl.program_id(0)
    home, place = info[0], info[1]
    local, width = rows_0.shape

    copies = [
        pltpu.make_async_copy(source, target, saved.at[at])
        for at, (source, target) in enumerate(
            (
                (out_weight, out_weight_ref),
                (query_weight, query_weight_ref),
                (pair_weight, pair_weight_ref),
            )
        )
    ]

    @pl.when(pair == 0)
    def _():
        fill_weight(out_weight, quarters, home, (0, 1))
        fill_weight(query_weight, quarters, home, (width, 1))
        fill_weight(pair_weight, quarters, home, (2 * width, 1))
        for copy in copies:
            copy.start()
        fill_weight(cross_out_ref, quarters, home, (4 * width, 1))
        fill_weight(norm_rows, quarters, home, (5 * width, 1))
        norms = norm_rows[...].astype(FULL).T[0:8]
        norms_ref[...] = norms
        mixed = states[...].astype(FULL) + dot(mix[...], out_weight[...])
        unit, scale = normalise(mixed)
        unit_ref[...] = unit
        scale_ref[...] = jnp.broadcast_to(scale, (local, LANES))
        first_low = (unit * norms[0:1] + norms[3:4]).astype(LOW)
        project_queries(first_low, query_weight[...], queries)
        flags_q[...] = query_flags(target_lengths, place * local, local)
        prepare_wide(source_lengths, key_wide, place)
        project_rows((rows_0, rows_1, rows_2, rows_3), pair_weight, key_wide, values)

    query = queries[pair]
    query_ref[...] = query
    key_ref[...] = key_wide[pair, :, :LANES]
    value_ref[...] = values[pair]
    mixed = attend_pair(
        query, flags_q[...], key_wide.at[pair], values.at[pair], scores, kept
    )
    mix_ref[...] = mixed.astype(LOW)
    exact_ref[...] = mixed
    mixes[pair] = mixed.astype(LOW)

    @pl.when(pair == mixes.shape[0] - 1)
    def _():
        first_norm = unit_ref[...] * norms_ref[0:1] + norms_ref[3:4]
        whole_mix = jnp.concatenate([mixes[at] for at in range(mixes.shape[0])], axis=1)
        second_unit, second_scale = normalise(first_norm + dot(whole_mix, cross_out_ref[...]))
        second_unit_ref[...] = second_unit
        second_scale_ref[...] = jnp.broadcast_to(second_scale, (local, LANES))
        for copy in copies:
            copy.wait()


gelu_factor = 0.7978845608028654
gelu_cubic = 0.044715


def gelu_and_slope(hidden):
    square = hidden * hidden
    bend = jnp.tanh(gelu_factor * (hidden + gelu_cubic * (square * hidden)))
    half = 0.5 * (1.0 + bend)
    slope = half + (0.5 * hidden) * (1.0 - bend * bend) * (
        gelu_factor * (1.0 + (3.0 * gelu_cubic) * square)
    )
    return hidden * half, slope


def middle_kernel(info, second_unit, norms, out_grad, *refs):
    quarters = refs[:8]
    (
        output_ref,
        third_grad_ref,
        hidden_grads,
        expand,
        norm_sums_ref,
        kept,
        sent,
        contract,
        active,
        slope,
        wide_grad,
        tall_grad,
    ) = refs[8:]
    home = info[0]
    width = second_unit.shape[1]
    chunks = active.shape[0]
    span = expand.shape[1] // chunks
    fill_weight(expand, quarters, home, (0, 1))
    fill_weight(contract, quarters, home, (expand.shape[1], contract.shape[0] // width))
    second_norm = second_unit[...] * norms[1:2] + norms[4:5]
    second_low = second_norm.astype(LOW)

    def forward(at, total):
        start = pl.multiple_of(at * span, span)
        hidden = dot(second_low, expand[:, pl.ds(start, span)])
        made, bent = gelu_and_slope(hidden)
        made = made.astype(LOW)
        active[at] = made
        slope[at] = bent
        return total + dot(made, contract[pl.ds(start, span)])

    mixed = lax.fori_loop(0, chunks, forward, second_norm, unroll=True)
    third_unit, third_scale = normalise(mixed)
    output_ref[...] = third_unit * norms[2:3] + norms[5:6]
    third_grad, gain_three, bias_three = norm_backward(
        out_grad[...], third_unit, third_scale, norms[2:3]
    )
    third_grad_ref[...] = third_grad
    ffn_grad = third_grad.astype(LOW)
    second_turned = second_low.T

    def backward(at, carry):
        start = pl.multiple_of(at * span, span)
        part = contract[pl.ds(start, span)]
        hidden_grad = (dot(ffn_grad, part, BY_LANES) * slope[at]).astype(LOW)
        hidden_grads[at] = hidden_grad
        tall_grad[pl.ds(start, span)] = dot(active[at].T, ffn_grad).astype(LOW)
        wide_grad[:, pl.ds(start, span)] = dot(second_turned, hidden_grad).astype(LOW)
        return carry

    lax.fori_loop(0, chunks, backward, 0, unroll=True)
    norm_sums_ref[...] = jnp.zeros(norm_sums_ref.shape, FULL)
    norm_sums_ref[2:3] = gain_three
    norm_sums_ref[5:6] = bias_three
    pack_grad(wide_grad, kept, sent, home, (0, 1))
    pack_grad(tall_grad, kept, sent, home, (expand.shape[1], tall_grad.shape[0] // width))


def second_back_kernel(
    third_grad,
    hidden_grads,
    expand,
    second_unit,
    second_scale,
    norms,
    sums,
    mix,
    out_weight,
    second_grad_ref,
    mix_grad_ref,
    out_weight_grad,
    norm_sums_ref,
):
    cotangent = third_grad[...]
    chunks = hidden_grads.shape[0]
    span = expand.shape[1] // chunks
    for at in range(chunks):
        part = expand[:, at * span : (at + 1) * span]
        cotangent = cotangent + dot(hidden_grads[at], part, BY_LANES)
    second_grad, gain_two, bias_two = norm_backward(
        cotangent, second_unit[...], second_scale[:, 0:1], norms[1:2]
    )
    second_grad_ref[...] = second_grad
    cross_out_low = second_grad.astype(LOW)
    mix_grad_ref[...] = dot(cross_out_low, out_weight[...], BY_LANES).astype(LOW)
    out_weight_grad[...] = dot(mix[...].T, cross_out_low).astype(LOW)
    norm_sums_ref[...] = sums[...]
    norm_sums_ref[1:2] = gain_two
    norm_sums_ref[4:5] = bias_two


def attend_back_pair(query, key, value, kept, mix, low_grad, value_wide, made):
    rows = low_grad.shape[0]
    left = lane_numbers((rows, LANES)) < HEAD_DIM
    lane = lane_numbers((rows, LANES))
    value_wide[:, :LANES] = value
    product = low_grad.astype(FULL) * mix
    query_turned = query.T
    grad_turned = low_grad.T
    query_grads = []
    for head in range(2):
        mine = left if head == 0 else ~left
        inner = -jnp.sum(jnp.where(mine, product, 0.0), axis=1, keepdims=True)
        first, second, third = three_parts(inner)
        parts = jnp.where(lane == 0, first, jnp.where(lane == 1, second, jnp.where(lane == 2, third, 0.0)))
        wide = jnp.concatenate([jnp.where(mine, low_grad, jnp.zeros_like(low_grad)), parts.astype(LOW)], axis=1)
        weights = kept[head]
        shifted = dot(wide, value_wide[...], BY_LANES)
        score_grad = (weights.astype(FULL) * shifted).astype(LOW)
        query_grads.append(dot(score_grad, key))
        span = slice(head * HEAD_DIM, (head + 1) * HEAD_DIM)
        made[span] = dot(query_turned[span], score_grad).astype(LOW)
        made[LANES + head * HEAD_DIM : LANES + (head + 1) * HEAD_DIM] = dot(
            grad_turned[span], weights
        ).astype(LOW)
    return (jnp.where(left, query_grads[0], query_grads[1]) * score_scale).astype(LOW)


def cross_backward_kernel(
    query,
    key,
    value,
    kept,
    mix,
    grad,
    rows_0,
    rows_1,
    rows_2,
    rows_3,
    made,
    query_grad_ref,
    weight_grad_ref,
    value_wide,
):
    pair = pl.program_id(0)

    @pl.when(pair == 0)
    def _():
        value_wide[:, LANES:] = jnp.ones((value_wide.shape[0], LANES), LOW)

    query_grad_ref[...] = attend_back_pair(
        query[...], key[...], value[...], kept, mix[...], grad[...], value_wide, made.at[pair]
    )

    @pl.when(pair == made.shape[0] - 1)
    def _():
        finish_weight(made, (rows_0, rows_1, rows_2, rows_3), weight_grad_ref, 0)


def finish_rows(made, weight, first, own_ref, far_ref, core_ref):
    pairs, _, keys = made.shape
    local = keys // 4
    width = own_ref.shape[1]
    for step in range(4):
        total = None
        for pair in range(pairs):
            at = first + pair * LANES
            columns = jnp.concatenate(
                [weight[:, at : at + LANES], weight[:, width + at : width + at + LANES]], axis=1
            )
            part = made[pair, :, step * local : (step + 1) * local].T
            term = dot(part, columns, BY_LANES)
            total = term if total is None else total + term
        if step == 0:
            own_ref[...] = total
        elif step == 2:
            far_ref[...] = total.astype(LOW)
        else:
            core_ref[step // 2] = total.astype(LOW)


def finish_weight(made, row_refs, weight_grad_ref, first):
    local, width = row_refs[0].shape
    for pair in range(made.shape[0]):
        total = None
        for step in range(4):
            term = dot(made[pair, :, step * local : (step + 1) * local], row_refs[step][...])
            total = term if total is None else total + term
        total = total.T.astype(LOW)
        at = first + pair * LANES
        weight_grad_ref[:, at : at + LANES] = total[:, :LANES]
        weight_grad_ref[:, width + at : width + at + LANES] = total[:, LANES:]


def between_kernel(
    info, query_grad, second_grad, first_unit, first_scale, norms, norm_sums, self_mix, pair_grad, cross_out_grad, out_weight, query_weight, *refs
):
    (
        first_grad_ref,
        mix_grad_ref,
        kept,
        sent,
        out_grad,
        query_weight_grad,
        norm_grad,
        norm_rows,
    ) = refs
    home = info[0]
    width = self_mix.shape[1]
    unit = first_unit[...]
    first_low = (unit * norms[0:1] + norms[3:4]).astype(LOW)
    low_grad = query_grad[...]
    query_weight_grad[...] = dot(first_low.T, low_grad).astype(LOW)
    cotangent = second_grad[...] + dot(low_grad, query_weight[...], BY_LANES)
    first_grad, gain_one, bias_one = norm_backward(
        cotangent, unit, first_scale[:, 0:1], norms[0:1]
    )
    first_grad_ref[...] = first_grad
    self_out_low = first_grad.astype(LOW)
    out_grad[...] = dot(self_mix[...].T, self_out_low).astype(LOW)
    mix_grad_ref[...] = dot(self_out_low, out_weight[...], BY_LANES).astype(LOW)
    norm_rows[...] = jnp.zeros(norm_rows.shape, FULL)
    norm_rows[0:8] = norm_sums[...]
    norm_rows[0:1] = gain_one
    norm_rows[3:4] = bias_one
    norm_grad[...] = norm_rows[...].T.astype(LOW)
    pack_grad(out_grad, kept, sent, home, (0, 1))
    pack_grad(query_weight_grad, kept, sent, home, (width, 1))
    pack_grad(pair_grad, kept, sent, home, (2 * width, 1))
    pack_grad(cross_out_grad, kept, sent, home, (4 * width, 1))
    pack_grad(norm_grad, kept, sent, home, (5 * width, 1))


def self_backward_kernel(
    info,
    query,
    key,
    value,
    kept_weights,
    mix,
    grad,
    rows_0,
    rows_1,
    rows_2,
    rows_3,
    made,
    query_grad_ref,
    kept,
    sent,
    value_wide,
    query_grads,
    weight_grad,
):
    pair = pl.program_id(0)
    width = rows_0.shape[1]
    pairs = made.shape[0]

    @pl.when(pair == 0)
    def _():
        value_wide[:, LANES:] = jnp.ones((value_wide.shape[0], LANES), LOW)

    query_grads[pair] = attend_back_pair(
        query[...], key[...], value[...], kept_weights, mix[...], grad[...], value_wide, made.at[pair]
    )

    @pl.when(pair == pairs - 1)
    def _():
        finish_weight(made, (rows_0, rows_1, rows_2, rows_3), weight_grad, width)
        low_grad = jnp.concatenate([query_grads[at] for at in range(pairs)], axis=1)
        query_grad_ref[...] = low_grad
        weight_grad[:, 0:width] = dot(rows_0[...].T, low_grad).astype(LOW)
        pack_grad(weight_grad, kept, sent, info[0], (0, 1))


def memory_kernel(made, weight, own_ref, far_ref, core_ref):
    finish_rows(made, weight, 0, own_ref, far_ref, core_ref)


def states_kernel(made, query_grad, first_grad, weight, own_ref, far_ref, core_ref):
    width = own_ref.shape[1]
    finish_rows(made, weight, width, own_ref, far_ref, core_ref)
    own_ref[...] += first_grad[...] + dot(query_grad[...], weight[:, 0:width], BY_LANES)


def whole(shape):
    return pl.BlockSpec(shape, lambda *at: (0,) * len(shape))


def call(kernel, inputs, specs, outputs, out_specs, scratch, grid=(), micros=1, mib=58):
    moved = sum(math.prod(a.shape) * a.dtype.itemsize for a in list(inputs) + list(outputs))
    return pl.pallas_call(
        kernel,
        out_shape=outputs,
        grid=grid,
        in_specs=specs,
        out_specs=out_specs,
        scratch_shapes=scratch,
        compiler_params=pltpu.CompilerParams(vmem_limit_bytes=mib * 2**20),
        cost_estimate=pl.CostEstimate(flops=micros * 10**9, bytes_accessed=moved, transcendentals=0),
    )(*inputs)


SCALARS = pl.BlockSpec(memory_space=pltpu.SMEM)


def shaped(shape, kind):
    return jax.ShapeDtypeStruct(shape, kind)


def per_device(
    target_states,
    memory,
    target_lengths,
    source_lengths,
    self_project,
    self_output,
    cross_project,
    memory_project,
    cross_output,
    expand_weight,
    contract_weight,
    norm_gain,
    norm_bias,
    out_grad,
):
    _, local, width = target_states.shape
    states = target_states[0]
    own_memory = memory[0]
    rows = self_project.shape[0]
    ff = expand_weight.shape[1]
    keys = local * 4
    pairs = width // LANES
    info = jnp.stack([home_number(), lax.axis_index("narrow")]).astype(jnp.int32)

    batches = 3 * width, 5 * width + LANES, 2 * ff
    if staged():
        shards = (
            self_output,
            cross_project,
            memory_project,
            cross_output,
            expand_weight,
            contract_weight,
            norm_gain,
            norm_bias,
        )
        later = batches[1] + batches[2]
        batch_23 = call(
            pack_kernel,
            list(shards),
            [whole(shard.shape) for shard in shards],
            [shaped((rows, later), LOW)],
            [whole((rows, later))],
            [pltpu.VMEM((LANES, LANES), FULL)],
        )[0]
        far_1 = jnp.stack(gather_far(self_project))
        states_x = exchange(states, 2)
        states_c = exchange(states, 1)
        (batch_23, states_c), far_1 = after((batch_23, states_c), far_1)
        near_23 = exchange(batch_23, FAR[0])
        plane_1 = gather_plane(far_1)
        near_23, states_x = after(near_23, states_x)
        own_memory, states_c = after(own_memory, states_c)
        half_2 = jnp.stack([batch_23[:, : batches[1]], near_23[:, : batches[1]]])
        half_3 = jnp.stack([batch_23[:, batches[1] :], near_23[:, batches[1] :]])
        rest_2 = exchange(half_2, FAR[1])
        memory_x = exchange(own_memory, 2)
        half_3, rest_2 = after(half_3, rest_2)
        far_2 = jnp.concatenate([half_2, rest_2])
        rest_3 = exchange(half_3, FAR[1])
    else:
        norm_shard = jnp.concatenate([norm_gain, norm_bias], axis=0).T
        norm_shard = jnp.pad(norm_shard, ((0, 0), (0, LANES - norm_shard.shape[1])))
        folded = fold_rows(contract_weight, rows)
        plane_1 = self_project
        far_2 = jnp.concatenate(
            [self_output, cross_project, memory_project, cross_output, norm_shard], axis=1
        )
        far_3 = jnp.concatenate([expand_weight, folded], axis=1)
        states_x = exchange(states, 2)
        states_c = exchange(states, 1)
        memory_c = exchange(own_memory, 1)
        memory_x = exchange(own_memory, 2)
    states_xc = exchange(states_x, 1)
    far_2, plane_1 = after(far_2, plane_1)
    weights_1 = gather_core(plane_1)
    row_states = [states, states_c, states_x, states_xc]
    own_2 = exchange(far_2, 1) if staged() else None
    if staged():
        row_states[1], own_2 = after(row_states[1], own_2)
    plane_2 = gather_plane(far_2)

    row_spec = whole((local, width))
    pair_rows = pl.BlockSpec((local, LANES), lambda pair: (0, pair))
    pair_keys = pl.BlockSpec((keys, LANES), lambda pair: (0, pair))
    pair_kept = pl.BlockSpec((2, local, keys), lambda pair: (pair, 0, 0))
    quarter_specs_1 = [whole(q.shape) for q in weights_1]
    attend_scratch = [
        pltpu.VMEM((pairs, local, LANES), LOW),
        pltpu.VMEM((local, LANES), LOW),
        pltpu.VMEM((pairs, keys, 2 * LANES), LOW),
        pltpu.VMEM((pairs, keys, LANES), LOW),
        pltpu.VMEM((2, local, keys), FULL),
    ]
    attend_outputs = [
        shaped((local, width), LOW),
        pltpu.HBM((local, width), LOW),
        pltpu.HBM((local, width), FULL),
        pltpu.HBM((keys, width), LOW),
        pltpu.HBM((keys, width), LOW),
        pltpu.HBM((2 * pairs, local, keys), LOW),
    ]
    attend_specs = [pair_rows] * 3 + [pair_keys, pair_keys, pair_kept]
    in_place = pl.BlockSpec(memory_space=pl.ANY)
    self_mix, self_query, self_exact, self_key, self_value, self_kept, self_weight = call(
        self_forward_kernel,
        [info, target_lengths, *row_states, *weights_1],
        [SCALARS, SCALARS] + [row_spec] * 4 + quarter_specs_1,
        attend_outputs + [pltpu.HBM((width, 3 * width), LOW)],
        attend_specs + [in_place],
        [pltpu.VMEM((width, 3 * width), LOW), pltpu.SemaphoreType.DMA] + attend_scratch,
        grid=(pairs,),
        micros=25, mib=38,
    )

    if staged():
        (memory_x, own_memory, rest_3), self_mix = after((memory_x, own_memory, rest_3), self_mix)
        memory_c = exchange(own_memory, 1)
        far_3 = jnp.concatenate([half_3, rest_3])
    plane_2, self_mix = after(plane_2, self_mix)
    own_3 = exchange(far_3, 1) if staged() else None
    memory_xc = exchange(memory_x, 1)
    weights_2 = gather_core(plane_2, own_2)
    row_memory = [own_memory, memory_c, memory_x, memory_xc]
    plane_3 = gather_plane(far_3)
    quarter_specs_2 = [whole(q.shape) for q in weights_2]
    wide_scale = whole((local, LANES))
    norm_spec = whole((8, width))
    square = whole((width, width))
    (
        cross_mix,
        cross_query,
        cross_exact,
        cross_key,
        cross_value,
        cross_kept,
        first_unit,
        first_scale,
        norms,
        second_unit,
        second_scale,
        cross_out_weight,
        out_weight,
        query_weight,
        pair_weight,
    ) = call(
        cross_forward_kernel,
        [info, target_lengths, source_lengths, self_mix, states, *row_memory, *weights_2],
        [SCALARS] * 3 + [row_spec] * 6 + quarter_specs_2,
        attend_outputs
        + [
            pltpu.HBM((local, width), FULL),
            pltpu.HBM((local, LANES), FULL),
            shaped((8, width), FULL),
            shaped((local, width), FULL),
            shaped((local, LANES), FULL),
            shaped((width, width), LOW),
            pltpu.HBM((width, width), LOW),
            pltpu.HBM((width, width), LOW),
            pltpu.HBM((width, 2 * width), LOW),
        ],
        attend_specs + [row_spec, wide_scale, norm_spec, row_spec, wide_scale, square] + [in_place] * 3,
        [
            pltpu.VMEM((width, width), LOW),
            pltpu.VMEM((width, width), LOW),
            pltpu.VMEM((width, 2 * width), LOW),
            pltpu.VMEM((width, LANES), LOW),
            pltpu.SemaphoreType.DMA((3,)),
            pltpu.VMEM((pairs, local, LANES), LOW),
        ]
        + attend_scratch,
        grid=(pairs,),
        micros=25, mib=46,
    )

    plane_3, second_unit = after(plane_3, second_unit)
    weights_3 = gather_core(plane_3, own_3, ff // width)
    quarter_specs_3 = [whole(q.shape) for q in weights_3]
    chunk_count = ff // width
    packed_3 = (4, 4, TILE_ROWS, 2 * ff)
    hidden_shape = (chunk_count, local, width)
    output, third_grad, hidden_grads, expand_whole, norm_sums, kept_3, sent_3 = call(
        middle_kernel,
        [info, second_unit, norms, out_grad[0], *weights_3],
        [SCALARS, row_spec, norm_spec, row_spec] + quarter_specs_3,
        [
            shaped((local, width), FULL),
            shaped((local, width), FULL),
            shaped(hidden_shape, LOW),
            shaped((width, ff), LOW),
            shaped((8, width), FULL),
            shaped(packed_3, LOW),
            shaped(packed_3, LOW),
        ],
        [row_spec, row_spec, whole(hidden_shape), whole((width, ff)), norm_spec]
        + [whole(packed_3), whole(packed_3)],
        [
            pltpu.VMEM((ff, width), LOW),
            pltpu.VMEM(hidden_shape, LOW),
            pltpu.VMEM(hidden_shape, FULL),
            pltpu.VMEM((width, ff), LOW),
            pltpu.VMEM((ff, width), LOW),
        ],
        micros=14, mib=34,
    )
    other_3 = exchange_core(sent_3)
    second_grad, cross_mix_grad, cross_out_grad, norm_sums = call(
        second_back_kernel,
        [
            third_grad,
            hidden_grads,
            expand_whole,
            second_unit,
            second_scale,
            norms,
            norm_sums,
            cross_mix,
            cross_out_weight,
        ],
        [row_spec, whole(hidden_shape), whole((width, ff))]
        + [row_spec, wide_scale, norm_spec, norm_spec, row_spec, square],
        [
            shaped((local, width), FULL),
            shaped((local, width), LOW),
            shaped((width, width), LOW),
            shaped((8, width), FULL),
        ],
        [row_spec, row_spec, square, norm_spec],
        [],
        micros=4, mib=12,
    )
    other_3, cross_mix_grad = after(other_3, cross_mix_grad)
    core_3 = reduce_core(kept_3, other_3)
    core_3, cross_mix_grad = after(core_3, cross_mix_grad)
    planes_3 = exchange_plane(core_3)

    back_specs = [pair_rows, pair_keys, pair_keys, pair_kept, pair_rows, pair_rows]
    made_shape = (pairs, 2 * LANES, keys)
    cross_made, cross_query_grad, pair_weight_grad = call(
        cross_backward_kernel,
        [
            cross_query,
            cross_key,
            cross_value,
            cross_kept,
            cross_exact,
            cross_mix_grad,
            *row_memory,
        ],
        back_specs + [row_spec] * 4,
        [
            shaped(made_shape, LOW),
            shaped((local, width), LOW),
            shaped((width, 2 * width), LOW),
        ],
        [whole(made_shape), pair_rows, whole((width, 2 * width))],
        [pltpu.VMEM((keys, 2 * LANES), LOW)],
        grid=(pairs,),
        micros=33, mib=36,
    )
    planes_3, cross_query_grad = after(planes_3, cross_query_grad)
    plane_sum_3 = reduce_plane(planes_3)
    plane_sum_3, cross_query_grad = after(plane_sum_3, cross_query_grad)
    half_sum_3 = exchange_half(plane_sum_3)

    packed_2 = (4, 4, TILE_ROWS, 5 * width + LANES)
    first_grad, self_mix_grad, kept_2, sent_2 = call(
        between_kernel,
        [
            info,
            cross_query_grad,
            second_grad,
            first_unit,
            first_scale,
            norms,
            norm_sums,
            self_mix,
            pair_weight_grad,
            cross_out_grad,
            out_weight,
            query_weight,
        ],
        [SCALARS, row_spec, row_spec, row_spec, whole((local, LANES))]
        + [whole((8, width))] * 2
        + [row_spec, whole((width, 2 * width)), whole((width, width))]
        + [square] * 2,
        [
            shaped((local, width), FULL),
            shaped((local, width), LOW),
            shaped(packed_2, LOW),
            shaped(packed_2, LOW),
        ],
        [row_spec, row_spec, whole(packed_2), whole(packed_2)],
        [
            pltpu.VMEM((width, width), LOW),
            pltpu.VMEM((width, width), LOW),
            pltpu.VMEM((width, LANES), LOW),
            pltpu.VMEM((LANES, width), FULL),
        ],
        micros=6, mib=14,
    )
    other_2 = exchange_core(sent_2)
    cross_made, sent_2 = after(cross_made, sent_2)
    rows_shapes = [
        shaped((local, width), FULL),
        shaped((local, width), LOW),
        shaped((2, local, width), LOW),
    ]
    rows_specs = [row_spec, row_spec, whole((2, local, width))]
    memory_own, memory_far_part, memory_parts = call(
        memory_kernel,
        [cross_made, pair_weight],
        [whole(made_shape), whole((width, 2 * width))],
        rows_shapes,
        rows_specs,
        [],
        micros=3, mib=20,
    )
    other_2, memory_parts = after(other_2, memory_parts)
    memory_sent = exchange(memory_parts, 1)
    core_2 = reduce_core(kept_2, other_2)
    memory_other = reduce_row_core(memory_far_part, memory_sent)
    (core_2, memory_other), self_mix_grad = after((core_2, memory_other), self_mix_grad)
    planes_2 = exchange_plane(core_2)
    memory_far = exchange(memory_other, 2)

    packed_1 = (4, 4, TILE_ROWS, 3 * width)
    made, self_query_grad, kept_1, sent_1 = call(
        self_backward_kernel,
        [
            info,
            self_query,
            self_key,
            self_value,
            self_kept,
            self_exact,
            self_mix_grad,
            *row_states,
        ],
        [SCALARS] + back_specs + [row_spec] * 4,
        [
            shaped(made_shape, LOW),
            shaped((local, width), LOW),
            shaped(packed_1, LOW),
            shaped(packed_1, LOW),
        ],
        [whole(made_shape), row_spec, whole(packed_1), whole(packed_1)],
        [
            pltpu.VMEM((keys, 2 * LANES), LOW),
            pltpu.VMEM((pairs, local, LANES), LOW),
            pltpu.VMEM((width, 3 * width), LOW),
        ],
        grid=(pairs,),
        micros=33, mib=36,
    )
    (planes_2, memory_far, half_sum_3), (sent_1, kept_1) = after(
        (planes_2, memory_far, half_sum_3), (sent_1, kept_1)
    )
    other_1 = exchange_core(sent_1)
    states_own, states_far_part, states_parts = call(
        states_kernel,
        [made, self_query_grad, first_grad, self_weight],
        [whole(made_shape), row_spec, row_spec, whole((width, 3 * width))],
        rows_shapes,
        rows_specs,
        [],
        micros=4, mib=20,
    )
    other_1, states_parts = after(other_1, states_parts)
    core_1 = reduce_core(kept_1, other_1)
    planes_1 = exchange_plane(core_1)
    states_sent = exchange(states_parts, 1)
    states_other = reduce_row_core(states_far_part, states_sent)
    (planes_2, half_sum_3, memory_far), states_other = after(
        (planes_2, half_sum_3, memory_far), states_other
    )
    plane_sum_2 = reduce_plane(planes_2)
    half_sum_2 = exchange_half(plane_sum_2)
    states_far = exchange(states_other, 2)
    total_3 = reduce_half(plane_sum_3, half_sum_3)
    total_2 = reduce_half(plane_sum_2, half_sum_2)
    planes_1, (total_2, total_3, states_other) = after(planes_1, (total_2, total_3, states_other))
    plane_sum_1 = reduce_plane(planes_1)
    fars_1 = exchange_far(plane_sum_1)
    memory_grad = reduce_row(memory_own, memory_sent, memory_far)
    states_grad = reduce_row(states_own, states_sent, states_far)
    count = norm_gain.shape[0]
    if staged():
        near = exchange(jnp.concatenate([total_2[1], total_3[1]], axis=1), FAR[0])
        settled = [
            shaped((rows, width), FULL),
            shaped((rows, width), FULL),
            shaped((rows, 2 * width), FULL),
            shaped((rows, width), FULL),
            shaped((rows, ff), FULL),
            shaped((rows * ff // width, width), FULL),
            shaped(norm_gain.shape, FULL),
            shaped(norm_gain.shape, FULL),
        ]
        out, cross, pairs_grad, cross_out, expand_grad, contract_grad, gain, bias = call(
            settle_kernel,
            [total_2[0], total_3[0], near],
            [whole((rows, batches[1])), whole((rows, batches[2])), whole((rows, later))],
            settled,
            [whole(each.shape) for each in settled],
            [pltpu.VMEM((LANES, LANES), FULL)],
            mib=8,
        )
        fars_1, out = after(fars_1, out)
        project = reduce_far(fars_1)
    else:
        grad_3 = reduce_far(total_3, ff // width)
        grad_2 = reduce_far(total_2)
        project = reduce_far(fars_1)
        expand_grad, contract_grad = grad_3[:, :ff], unfold_rows(grad_3[:, ff:], width)
        out, cross = grad_2[:, :width], grad_2[:, width : 2 * width]
        pairs_grad, cross_out = grad_2[:, 2 * width : 4 * width], grad_2[:, 4 * width : 5 * width]
        norm_grads = grad_2[:, 5 * width :].T
        gain, bias = norm_grads[:count], norm_grads[count : 2 * count]
    return (
        output[None],
        states_grad[None],
        memory_grad[None],
        project,
        out,
        cross,
        pairs_grad,
        cross_out,
        expand_grad,
        contract_grad,
        gain,
        bias,
    )


def reduce_row_core(part, sent):
    return add_all(part, [sent[1]]).astype(LOW)


def reduce_row(own, sent, far):
    return add_all(own, [sent[0], far])


def solution(mesh):
    in_specs = (
        P("wide", "narrow", None),
        P("wide", "narrow", None),
        P("wide", None),
        P("wide", None),
        P(("wide", "narrow"), None),
        P(("wide", "narrow"), None),
        P(("wide", "narrow"), None),
        P(("wide", "narrow"), None),
        P(("wide", "narrow"), None),
        P(("wide", "narrow"), None),
        P(("wide", "narrow"), None),
        P(None, ("wide", "narrow")),
        P(None, ("wide", "narrow")),
        P("wide", "narrow", None),
    )
    out_specs = (
        P("wide", "narrow", None),
        P("wide", "narrow", None),
        P("wide", "narrow", None),
        P(("wide", "narrow"), None),
        P(("wide", "narrow"), None),
        P(("wide", "narrow"), None),
        P(("wide", "narrow"), None),
        P(("wide", "narrow"), None),
        P(("wide", "narrow"), None),
        P(("wide", "narrow"), None),
        P(None, ("wide", "narrow")),
        P(None, ("wide", "narrow")),
    )
    return jax.shard_map(
        per_device, mesh=mesh, in_specs=in_specs, out_specs=out_specs, check_vma=False
    )
```

```python
import functools
import math

import jax
import jax.numpy as jnp
from jax import lax
from jax.experimental import pallas as pl
from jax.experimental.pallas import tpu as pltpu
from jax.sharding import PartitionSpec as P

HEAD_DIM = 64
LANES = 128
TILE_ROWS = 16
BLOCKS = 32
AXES = ("wide", "narrow")
LOW = jnp.bfloat16
FULL = jnp.float32

ln_eps = 1e-05
score_scale = HEAD_DIM ** (-0.5)
mask_step = -(2.0**30)

BY_LANES = (((1,), (1,)), ((), ()))
PLAIN = (((1,), (0,)), ((), ()))


def dot(left, right, dims=PLAIN):
    return lax.dot_general(left, right, dims, preferred_element_type=FULL)


def exchange(block, mask):
    device_count = lax.axis_size("wide") * lax.axis_size("narrow")
    pairs = [(device, device ^ mask) for device in range(device_count)]
    return lax.ppermute(block, AXES, pairs)


def device_number():
    return lax.axis_index("wide") * lax.axis_size("narrow") + lax.axis_index("narrow")


def staged():
    return lax.axis_size("wide") * lax.axis_size("narrow") == BLOCKS


FAR = (8, 16, 24)
PLANE = (2, 4, 6)


def gather_far(shard):
    if not staged():
        return shard
    return [shard] + [exchange(shard, mask) for mask in FAR]


def gather_plane(held):
    if not staged():
        return held
    return [held] + [exchange(held, mask) for mask in PLANE]


def gather_core(held, own=None, folds=0):
    if staged():
        first = exchange(held[0], 1) if own is None else own
        return held + [first] + [exchange(quarter, 1) for quarter in held[1:]]
    whole = lax.all_gather(held, AXES, axis=0, tiled=True)
    if folds:
        rows, columns = held.shape
        split = columns - folds * whole.shape[0]
        tall = unfold_rows(held[:, split:], whole.shape[0])
        tall = lax.all_gather(tall, AXES, axis=0, tiled=True)
        tall = tall.reshape(BLOCKS, folds, TILE_ROWS, -1).transpose(0, 2, 1, 3)
        whole = jnp.concatenate([whole[:, :split], tall.reshape(whole.shape[0], -1)], axis=1)
    whole = whole.reshape(4, 4, 2, TILE_ROWS, held.shape[1]).transpose(2, 1, 0, 3, 4)
    return [whole[core, plane] for core in range(2) for plane in range(4)]


def home_number():
    return device_number() if staged() else jnp.zeros((), jnp.int32)


def block_number(home, core, plane, far):
    return home ^ (far * 8 + plane * 2 + core)


def add_all(first, others):
    total = first.astype(FULL)
    for other in others:
        total = total + other.astype(FULL)
    return total


def exchange_core(sent):
    return exchange(sent, 1) if staged() else sent


def reduce_core(kept, other):
    return add_all(kept, [other]).astype(LOW) if staged() else (kept, other)


def exchange_plane(held):
    if not staged():
        return held
    return [held[0]] + [exchange(held[plane + 1], mask) for plane, mask in enumerate(PLANE)]


def reduce_plane(planes):
    return add_all(planes[0], planes[1:]).astype(LOW) if staged() else planes


def exchange_far(held):
    if not staged():
        return held
    return [held[0]] + [exchange(held[far + 1], mask) for far, mask in enumerate(FAR)]


def exchange_half(held):
    return exchange(held[2:], FAR[1]) if staged() else held


def reduce_half(held, other):
    return add_all(held[:2], [other]).astype(LOW) if staged() else held


def reduce_far(held, folds=0):
    if staged():
        return add_all(held[0], held[1:])
    whole = jnp.stack(held).transpose(2, 1, 0, 3, 4)
    whole = whole.reshape(BLOCKS * TILE_ROWS, -1).astype(FULL)
    if folds:
        split = whole.shape[1] - folds * whole.shape[0]
        tall = whole[:, split:].reshape(BLOCKS, TILE_ROWS, folds, -1).transpose(0, 2, 1, 3)
        tall = tall.reshape(folds * whole.shape[0], -1)
        tall = lax.psum_scatter(tall, AXES, scatter_dimension=0, tiled=True)
        whole = lax.psum_scatter(whole[:, :split], AXES, scatter_dimension=0, tiled=True)
        return jnp.concatenate([whole, fold_rows(tall, whole.shape[0])], axis=1)
    return lax.psum_scatter(whole, AXES, scatter_dimension=0, tiled=True)


def after(values, token):
    return lax.optimization_barrier((values, token))


def fold_rows(block, rows):
    return jnp.concatenate(
        [block[at : at + rows] for at in range(0, block.shape[0], rows)], axis=1
    )


def unfold_rows(block, width):
    return jnp.concatenate(
        [block[:, at : at + width] for at in range(0, block.shape[1], width)], axis=0
    )


def lane_numbers(shape):
    return lax.broadcasted_iota(jnp.int32, shape, 1)


def segment_bounds(lengths_ref):
    lane = lane_numbers((1, LANES))
    first = jnp.full((1, LANES), 2**30, jnp.int32)
    last = jnp.zeros((1, LANES), jnp.int32)
    start = jnp.int32(0)
    count = lengths_ref.shape[1]
    for segment in range(count + 1):
        end = start + lengths_ref[0, segment] if segment < count else jnp.int32(2**30)
        first = jnp.where(lane == segment, start, first)
        last = jnp.where(lane == segment, end, last)
        start = end
    return first, last


def segment_flags(start, rows, bounds):
    position = start + lax.broadcasted_iota(jnp.int32, (rows, LANES), 0)
    return (position >= bounds[0]) & (position < bounds[1])


def three_parts(value):
    first = value.astype(LOW)
    rest = value - first.astype(FULL)
    second = rest.astype(LOW)
    third = (rest - second.astype(FULL)).astype(LOW)
    return first.astype(FULL), second.astype(FULL), third.astype(FULL)


def query_flags(lengths_ref, start, rows):
    segments = lengths_ref.shape[1] + 1
    own = segment_flags(start, rows, segment_bounds(lengths_ref))
    return jnp.where(own | (lane_numbers((rows, LANES)) >= segments), 0.0, mask_step).astype(LOW)


def key_flags(lengths_ref, start, rows):
    own = segment_flags(start, rows, segment_bounds(lengths_ref))
    return jnp.where(own, 1.0, 0.0).astype(LOW)


def fill_weight(target, quarters, home, columns):
    first, folds = columns
    width = target.shape[1]
    for core in range(2):
        for plane in range(4):
            for far in range(4):
                block = block_number(home, core, plane, far)
                piece = quarters[core * 4 + plane]
                for fold in range(folds):
                    row = pl.multiple_of(block * (TILE_ROWS * folds) + fold * TILE_ROWS, TILE_ROWS)
                    start = first + fold * width
                    target[pl.ds(row, TILE_ROWS), :] = piece[far, :, start : start + width]


def pack_grad(source, kept, sent, home, columns):
    first, folds = columns
    width = source.shape[1]
    for core, target in ((0, kept), (1, sent)):
        for plane in range(4):
            for far in range(4):
                block = block_number(home, core, plane, far)
                for fold in range(folds):
                    row = pl.multiple_of(block * (TILE_ROWS * folds) + fold * TILE_ROWS, TILE_ROWS)
                    start = first + fold * width
                    target[plane, far, :, start : start + width] = source[pl.ds(row, TILE_ROWS), :]


def normalise(states):
    centred = states - jnp.mean(states, axis=1, keepdims=True)
    spread = jnp.mean(centred * centred, axis=1, keepdims=True)
    scale = lax.rsqrt(spread + ln_eps)
    return centred * scale, scale


def norm_backward(cotangent, unit, scale, gain):
    scaled = cotangent * gain
    grad = scale * (
        scaled
        - jnp.mean(scaled, axis=1, keepdims=True)
        - unit * jnp.mean(scaled * unit, axis=1, keepdims=True)
    )
    return (
        grad,
        jnp.sum(cotangent * unit, axis=0, keepdims=True),
        jnp.sum(cotangent, axis=0, keepdims=True),
    )


KEY_STEP = 512


def pack_kernel(*refs):
    ins, (packed, square) = refs[:8], refs[8:]
    self_output, cross_project, memory_project, cross_output, expand, contract, gain, bias = ins
    rows, width = self_output.shape
    at = 0
    for part in (self_output, cross_project, memory_project, cross_output):
        packed[:, at : at + part.shape[1]] = part[...]
        at += part.shape[1]
    count = gain.shape[0]
    square[...] = jnp.zeros(square.shape, FULL)
    square[0:count, 0:rows] = gain[...].astype(FULL)
    square[count : 2 * count, 0:rows] = bias[...].astype(FULL)
    packed[:, at : at + LANES] = square[...].T[0:rows].astype(LOW)
    at += LANES
    packed[:, at : at + expand.shape[1]] = expand[...]
    at += expand.shape[1]
    for fold in range(contract.shape[0] // rows):
        packed[:, at : at + width] = contract[fold * rows : (fold + 1) * rows]
        at += width


def settle_kernel(part_2, part_3, other, *refs):
    output_ref, cross_ref, memory_ref, cross_out_ref, expand_ref, contract_ref, gain_ref, bias_ref, square = refs
    rows, width = output_ref.shape
    split = part_2.shape[1]
    total = add_all(part_2[...], [other[:, :split]])
    at = 0
    for ref in (output_ref, cross_ref, memory_ref, cross_out_ref):
        ref[...] = total[:, at : at + ref.shape[1]]
        at += ref.shape[1]
    square[...] = jnp.zeros(square.shape, FULL)
    square[0:rows] = total[:, at : at + LANES]
    turned = square[...].T
    count = gain_ref.shape[0]
    gain_ref[...] = turned[0:count, 0:rows]
    bias_ref[...] = turned[count : 2 * count, 0:rows]
    total = add_all(part_3[...], [other[:, split:]])
    span = expand_ref.shape[1]
    expand_ref[...] = total[:, :span]
    for fold in range(contract_ref.shape[0] // rows):
        at = span + fold * width
        contract_ref[fold * rows : (fold + 1) * rows] = total[:, at : at + width]


def attend_pair(query, flags, key_wide, values, scores, kept):
    rows = query.shape[0]
    keys = key_wide.shape[0]
    left = lane_numbers((rows, LANES)) < HEAD_DIM
    zero = jnp.zeros_like(query)
    queries = [
        jnp.concatenate([jnp.where(left, query, zero), flags], axis=1),
        jnp.concatenate([jnp.where(left, zero, query), flags], axis=1),
    ]

    def score(head, start, peak):
        made = dot(queries[head], key_wide[start : start + KEY_STEP], BY_LANES)
        scores[head, :, start : start + KEY_STEP] = made
        for at in range(0, KEY_STEP, LANES):
            peak = jnp.maximum(peak, made[:, at : at + LANES])
        return peak

    def raise_scores(head, start, peak, total):
        span = slice(start, start + KEY_STEP)
        weights = jnp.exp(scores[head, :, span] - peak)
        for at in range(0, KEY_STEP, LANES):
            total = total + weights[:, at : at + LANES]
        return total

    def weigh(head, start, shift, total):
        span = slice(start, start + KEY_STEP)
        probs = jnp.exp(scores[head, :, span] - shift).astype(LOW)
        kept[head, :, span] = probs
        return total + dot(probs, values[span])

    steps = range(0, keys, KEY_STEP)
    lowest = jnp.full((rows, LANES), -jnp.inf, FULL)
    empty = jnp.zeros((rows, LANES), FULL)
    peak = lowest
    for start in steps:
        peak = score(0, start, peak)
    first_peak = jnp.max(peak, axis=1, keepdims=True)
    peak, first_total = lowest, empty
    for start in steps:
        peak = score(1, start, peak)
        first_total = raise_scores(0, start, first_peak, first_total)
    second_peak = jnp.max(peak, axis=1, keepdims=True)
    first_shift = first_peak + jnp.log(jnp.sum(first_total, axis=1, keepdims=True))
    first, second_total = empty, empty
    for start in steps:
        second_total = raise_scores(1, start, second_peak, second_total)
        first = weigh(0, start, first_shift, first)
    second_shift = second_peak + jnp.log(jnp.sum(second_total, axis=1, keepdims=True))
    second = empty
    for start in steps:
        second = weigh(1, start, second_shift, second)
    return jnp.where(left, first, second)


def pair_columns(first, pair):
    return pl.ds(pl.multiple_of(first + pair * LANES, LANES), LANES)


def prepare_wide(lengths, key_wide, place):
    pairs, keys, _ = key_wide.shape
    local = keys // 4
    for step in range(4):
        span = slice(step * local, (step + 1) * local)
        flags = key_flags(lengths, (place ^ step) * local, local)
        for pair in range(pairs):
            key_wide[pair, span, LANES:] = flags


def project_rows(rows, weight, key_wide, values):
    pairs = key_wide.shape[0]
    local = rows[0].shape[0]
    for step, part in enumerate(rows):
        span = slice(step * local, (step + 1) * local)
        for target, first in ((key_wide, 0), (values, pairs * LANES)):
            made = dot(part[...], weight[:, first : first + pairs * LANES]).astype(LOW)
            for pair in range(pairs):
                target[pair, span, :LANES] = made[:, pair * LANES : (pair + 1) * LANES]


def project_queries(rows, weight, queries):
    made = dot(rows, weight).astype(LOW).astype(FULL) * score_scale
    for pair in range(queries.shape[0]):
        queries[pair] = made[:, pair * LANES : (pair + 1) * LANES].astype(LOW)


def self_forward_kernel(info, lengths, rows_0, rows_1, rows_2, rows_3, *refs):
    quarters = refs[:8]
    (
        mix_ref,
        query_ref,
        exact_ref,
        key_ref,
        value_ref,
        kept,
        weight_ref,
        weight,
        saved,
        queries,
        flags_q,
        key_wide,
        values,
        scores,
    ) = refs[8:]
    pair = pl.program_id(0)
    home, place = info[0], info[1]
    local, width = rows_0.shape

    @pl.when(pair == 0)
    def _():
        fill_weight(weight, quarters, home, (0, 1))
        pltpu.make_async_copy(weight, weight_ref, saved).start()
        flags_q[...] = query_flags(lengths, place * local, local)
        prepare_wide(lengths, key_wide, place)
        project_rows((rows_0, rows_1, rows_2, rows_3), weight.at[:, width:], key_wide, values)
        project_queries(rows_0[...], weight[:, :width], queries)

    query = queries[pair]
    query_ref[...] = query
    key_ref[...] = key_wide[pair, :, :LANES]
    value_ref[...] = values[pair]
    mix = attend_pair(
        query, flags_q[...], key_wide.at[pair], values.at[pair], scores, kept
    )
    mix_ref[...] = mix.astype(LOW)
    exact_ref[...] = mix

    @pl.when(pair == queries.shape[0] - 1)
    def _():
        pltpu.make_async_copy(weight, weight_ref, saved).wait()


def cross_forward_kernel(
    info, target_lengths, source_lengths, mix, states, rows_0, rows_1, rows_2, rows_3, *refs
):
    quarters = refs[:8]
    (
        mix_ref,
        query_ref,
        exact_ref,
        key_ref,
        value_ref,
        kept,
        unit_ref,
        scale_ref,
        norms_ref,
        second_unit_ref,
        second_scale_ref,
        cross_out_ref,
        out_weight_ref,
        query_weight_ref,
        pair_weight_ref,
        out_weight,
        query_weight,
        pair_weight,
        norm_rows,
        saved,
        mixes,
        queries,
        flags_q,
        key_wide,
        values,
        scores,
    ) = refs[8:]
    pair = pl.program_id(0)
    home, place = info[0], info[1]
    local, width = rows_0.shape

    copies = [
        pltpu.make_async_copy(source, target, saved.at[at])
        for at, (source, target) in enumerate(
            (
                (out_weight, out_weight_ref),
                (query_weight, query_weight_ref),
                (pair_weight, pair_weight_ref),
            )
        )
    ]

    @pl.when(pair == 0)
    def _():
        fill_weight(out_weight, quarters, home, (0, 1))
        fill_weight(query_weight, quarters, home, (width, 1))
        fill_weight(pair_weight, quarters, home, (2 * width, 1))
        for copy in copies:
            copy.start()
        fill_weight(cross_out_ref, quarters, home, (4 * width, 1))
        fill_weight(norm_rows, quarters, home, (5 * width, 1))
        norms = norm_rows[...].astype(FULL).T[0:8]
        norms_ref[...] = norms
        mixed = states[...].astype(FULL) + dot(mix[...], out_weight[...])
        unit, scale = normalise(mixed)
        unit_ref[...] = unit
        scale_ref[...] = jnp.broadcast_to(scale, (local, LANES))
        first_low = (unit * norms[0:1] + norms[3:4]).astype(LOW)
        project_queries(first_low, query_weight[...], queries)
        flags_q[...] = query_flags(target_lengths, place * local, local)
        prepare_wide(source_lengths, key_wide, place)
        project_rows((rows_0, rows_1, rows_2, rows_3), pair_weight, key_wide, values)

    query = queries[pair]
    query_ref[...] = query
    key_ref[...] = key_wide[pair, :, :LANES]
    value_ref[...] = values[pair]
    mixed = attend_pair(
        query, flags_q[...], key_wide.at[pair], values.at[pair], scores, kept
    )
    mix_ref[...] = mixed.astype(LOW)
    exact_ref[...] = mixed
    mixes[pair] = mixed.astype(LOW)

    @pl.when(pair == mixes.shape[0] - 1)
    def _():
        first_norm = unit_ref[...] * norms_ref[0:1] + norms_ref[3:4]
        whole_mix = jnp.concatenate([mixes[at] for at in range(mixes.shape[0])], axis=1)
        second_unit, second_scale = normalise(first_norm + dot(whole_mix, cross_out_ref[...]))
        second_unit_ref[...] = second_unit
        second_scale_ref[...] = jnp.broadcast_to(second_scale, (local, LANES))
        for copy in copies:
            copy.wait()


gelu_factor = 0.7978845608028654
gelu_cubic = 0.044715


def gelu_and_slope(hidden):
    square = hidden * hidden
    bend = jnp.tanh(gelu_factor * (hidden + gelu_cubic * (square * hidden)))
    half = 0.5 * (1.0 + bend)
    slope = half + (0.5 * hidden) * (1.0 - bend * bend) * (
        gelu_factor * (1.0 + (3.0 * gelu_cubic) * square)
    )
    return hidden * half, slope


def middle_kernel(info, second_unit, norms, out_grad, *refs):
    quarters = refs[:8]
    (
        output_ref,
        third_grad_ref,
        hidden_grads,
        expand,
        norm_sums_ref,
        kept,
        sent,
        contract,
        active,
        slope,
        wide_grad,
        tall_grad,
    ) = refs[8:]
    home = info[0]
    width = second_unit.shape[1]
    chunks = active.shape[0]
    span = expand.shape[1] // chunks
    fill_weight(expand, quarters, home, (0, 1))
    fill_weight(contract, quarters, home, (expand.shape[1], contract.shape[0] // width))
    second_norm = second_unit[...] * norms[1:2] + norms[4:5]
    second_low = second_norm.astype(LOW)

    def forward(at, total):
        start = pl.multiple_of(at * span, span)
        hidden = dot(second_low, expand[:, pl.ds(start, span)])
        made, bent = gelu_and_slope(hidden)
        made = made.astype(LOW)
        active[at] = made
        slope[at] = bent
        return total + dot(made, contract[pl.ds(start, span)])

    mixed = lax.fori_loop(0, chunks, forward, second_norm, unroll=True)
    third_unit, third_scale = normalise(mixed)
    output_ref[...] = third_unit * norms[2:3] + norms[5:6]
    third_grad, gain_three, bias_three = norm_backward(
        out_grad[...], third_unit, third_scale, norms[2:3]
    )
    third_grad_ref[...] = third_grad
    ffn_grad = third_grad.astype(LOW)
    second_turned = second_low.T

    def backward(at, carry):
        start = pl.multiple_of(at * span, span)
        part = contract[pl.ds(start, span)]
        hidden_grad = (dot(ffn_grad, part, BY_LANES) * slope[at]).astype(LOW)
        hidden_grads[at] = hidden_grad
        tall_grad[pl.ds(start, span)] = dot(active[at].T, ffn_grad).astype(LOW)
        wide_grad[:, pl.ds(start, span)] = dot(second_turned, hidden_grad).astype(LOW)
        return carry

    lax.fori_loop(0, chunks, backward, 0, unroll=True)
    norm_sums_ref[...] = jnp.zeros(norm_sums_ref.shape, FULL)
    norm_sums_ref[2:3] = gain_three
    norm_sums_ref[5:6] = bias_three
    pack_grad(wide_grad, kept, sent, home, (0, 1))
    pack_grad(tall_grad, kept, sent, home, (expand.shape[1], tall_grad.shape[0] // width))


def second_back_kernel(
    third_grad,
    hidden_grads,
    expand,
    second_unit,
    second_scale,
    norms,
    sums,
    mix,
    out_weight,
    second_grad_ref,
    mix_grad_ref,
    out_weight_grad,
    norm_sums_ref,
):
    cotangent = third_grad[...]
    chunks = hidden_grads.shape[0]
    span = expand.shape[1] // chunks
    for at in range(chunks):
        part = expand[:, at * span : (at + 1) * span]
        cotangent = cotangent + dot(hidden_grads[at], part, BY_LANES)
    second_grad, gain_two, bias_two = norm_backward(
        cotangent, second_unit[...], second_scale[:, 0:1], norms[1:2]
    )
    second_grad_ref[...] = second_grad
    cross_out_low = second_grad.astype(LOW)
    mix_grad_ref[...] = dot(cross_out_low, out_weight[...], BY_LANES).astype(LOW)
    out_weight_grad[...] = dot(mix[...].T, cross_out_low).astype(LOW)
    norm_sums_ref[...] = sums[...]
    norm_sums_ref[1:2] = gain_two
    norm_sums_ref[4:5] = bias_two


def attend_back_pair(query, key, value, kept, mix, low_grad, value_wide, made):
    rows = low_grad.shape[0]
    left = lane_numbers((rows, LANES)) < HEAD_DIM
    lane = lane_numbers((rows, LANES))
    value_wide[:, :LANES] = value
    product = low_grad.astype(FULL) * mix
    query_turned = query.T
    grad_turned = low_grad.T
    query_grads = []
    for head in range(2):
        mine = left if head == 0 else ~left
        inner = -jnp.sum(jnp.where(mine, product, 0.0), axis=1, keepdims=True)
        first, second, third = three_parts(inner)
        parts = jnp.where(lane == 0, first, jnp.where(lane == 1, second, jnp.where(lane == 2, third, 0.0)))
        wide = jnp.concatenate([jnp.where(mine, low_grad, jnp.zeros_like(low_grad)), parts.astype(LOW)], axis=1)
        weights = kept[head]
        shifted = dot(wide, value_wide[...], BY_LANES)
        score_grad = (weights.astype(FULL) * shifted).astype(LOW)
        query_grads.append(dot(score_grad, key))
        span = slice(head * HEAD_DIM, (head + 1) * HEAD_DIM)
        made[span] = dot(query_turned[span], score_grad).astype(LOW)
        made[LANES + head * HEAD_DIM : LANES + (head + 1) * HEAD_DIM] = dot(
            grad_turned[span], weights
        ).astype(LOW)
    return (jnp.where(left, query_grads[0], query_grads[1]) * score_scale).astype(LOW)


def cross_backward_kernel(
    query,
    key,
    value,
    kept,
    mix,
    grad,
    rows_0,
    rows_1,
    rows_2,
    rows_3,
    made,
    query_grad_ref,
    weight_grad_ref,
    value_wide,
):
    pair = pl.program_id(0)

    @pl.when(pair == 0)
    def _():
        value_wide[:, LANES:] = jnp.ones((value_wide.shape[0], LANES), LOW)

    query_grad_ref[...] = attend_back_pair(
        query[...], key[...], value[...], kept, mix[...], grad[...], value_wide, made.at[pair]
    )

    @pl.when(pair == made.shape[0] - 1)
    def _():
        finish_weight(made, (rows_0, rows_1, rows_2, rows_3), weight_grad_ref, 0)


def finish_rows(made, weight, first, own_ref, far_ref, core_ref):
    pairs, _, keys = made.shape
    local = keys // 4
    width = own_ref.shape[1]
    for step in range(4):
        total = None
        for pair in range(pairs):
            at = first + pair * LANES
            columns = jnp.concatenate(
                [weight[:, at : at + LANES], weight[:, width + at : width + at + LANES]], axis=1
            )
            part = made[pair, :, step * local : (step + 1) * local].T
            term = dot(part, columns, BY_LANES)
            total = term if total is None else total + term
        if step == 0:
            own_ref[...] = total
        elif step == 2:
            far_ref[...] = total.astype(LOW)
        else:
            core_ref[step // 2] = total.astype(LOW)


def finish_weight(made, row_refs, weight_grad_ref, first):
    local, width = row_refs[0].shape
    for pair in range(made.shape[0]):
        total = None
        for step in range(4):
            term = dot(made[pair, :, step * local : (step + 1) * local], row_refs[step][...])
            total = term if total is None else total + term
        total = total.T.astype(LOW)
        at = first + pair * LANES
        weight_grad_ref[:, at : at + LANES] = total[:, :LANES]
        weight_grad_ref[:, width + at : width + at + LANES] = total[:, LANES:]


def between_kernel(
    info, query_grad, second_grad, first_unit, first_scale, norms, norm_sums, self_mix, pair_grad, cross_out_grad, out_weight, query_weight, *refs
):
    (
        first_grad_ref,
        mix_grad_ref,
        kept,
        sent,
        out_grad,
        query_weight_grad,
        norm_grad,
        norm_rows,
    ) = refs
    home = info[0]
    width = self_mix.shape[1]
    unit = first_unit[...]
    first_low = (unit * norms[0:1] + norms[3:4]).astype(LOW)
    low_grad = query_grad[...]
    query_weight_grad[...] = dot(first_low.T, low_grad).astype(LOW)
    cotangent = second_grad[...] + dot(low_grad, query_weight[...], BY_LANES)
    first_grad, gain_one, bias_one = norm_backward(
        cotangent, unit, first_scale[:, 0:1], norms[0:1]
    )
    first_grad_ref[...] = first_grad
    self_out_low = first_grad.astype(LOW)
    out_grad[...] = dot(self_mix[...].T, self_out_low).astype(LOW)
    mix_grad_ref[...] = dot(self_out_low, out_weight[...], BY_LANES).astype(LOW)
    norm_rows[...] = jnp.zeros(norm_rows.shape, FULL)
    norm_rows[0:8] = norm_sums[...]
    norm_rows[0:1] = gain_one
    norm_rows[3:4] = bias_one
    norm_grad[...] = norm_rows[...].T.astype(LOW)
    pack_grad(out_grad, kept, sent, home, (0, 1))
    pack_grad(query_weight_grad, kept, sent, home, (width, 1))
    pack_grad(pair_grad, kept, sent, home, (2 * width, 1))
    pack_grad(cross_out_grad, kept, sent, home, (4 * width, 1))
    pack_grad(norm_grad, kept, sent, home, (5 * width, 1))


def self_backward_kernel(
    info,
    query,
    key,
    value,
    kept_weights,
    mix,
    grad,
    rows_0,
    rows_1,
    rows_2,
    rows_3,
    made,
    query_grad_ref,
    kept,
    sent,
    value_wide,
    query_grads,
    weight_grad,
):
    pair = pl.program_id(0)
    width = rows_0.shape[1]
    pairs = made.shape[0]

    @pl.when(pair == 0)
    def _():
        value_wide[:, LANES:] = jnp.ones((value_wide.shape[0], LANES), LOW)

    query_grads[pair] = attend_back_pair(
        query[...], key[...], value[...], kept_weights, mix[...], grad[...], value_wide, made.at[pair]
    )

    @pl.when(pair == pairs - 1)
    def _():
        finish_weight(made, (rows_0, rows_1, rows_2, rows_3), weight_grad, width)
        low_grad = jnp.concatenate([query_grads[at] for at in range(pairs)], axis=1)
        query_grad_ref[...] = low_grad
        weight_grad[:, 0:width] = dot(rows_0[...].T, low_grad).astype(LOW)
        pack_grad(weight_grad, kept, sent, info[0], (0, 1))


def memory_kernel(made, weight, own_ref, far_ref, core_ref):
    finish_rows(made, weight, 0, own_ref, far_ref, core_ref)


def states_kernel(made, query_grad, first_grad, weight, own_ref, far_ref, core_ref):
    width = own_ref.shape[1]
    finish_rows(made, weight, width, own_ref, far_ref, core_ref)
    own_ref[...] += first_grad[...] + dot(query_grad[...], weight[:, 0:width], BY_LANES)


def whole(shape):
    return pl.BlockSpec(shape, lambda *at: (0,) * len(shape))


def call(kernel, inputs, specs, outputs, out_specs, scratch, grid=(), micros=1, mib=58):
    moved = sum(math.prod(a.shape) * a.dtype.itemsize for a in list(inputs) + list(outputs))
    return pl.pallas_call(
        kernel,
        out_shape=outputs,
        grid=grid,
        in_specs=specs,
        out_specs=out_specs,
        scratch_shapes=scratch,
        compiler_params=pltpu.CompilerParams(vmem_limit_bytes=mib * 2**20),
        cost_estimate=pl.CostEstimate(flops=micros * 10**9, bytes_accessed=moved, transcendentals=0),
    )(*inputs)


SCALARS = pl.BlockSpec(memory_space=pltpu.SMEM)


def shaped(shape, kind):
    return jax.ShapeDtypeStruct(shape, kind)


def per_device(
    target_states,
    memory,
    target_lengths,
    source_lengths,
    self_project,
    self_output,
    cross_project,
    memory_project,
    cross_output,
    expand_weight,
    contract_weight,
    norm_gain,
    norm_bias,
    out_grad,
):
    _, local, width = target_states.shape
    states = target_states[0]
    own_memory = memory[0]
    rows = self_project.shape[0]
    ff = expand_weight.shape[1]
    keys = local * 4
    pairs = width // LANES
    info = jnp.stack([home_number(), lax.axis_index("narrow")]).astype(jnp.int32)

    batches = 3 * width, 5 * width + LANES, 2 * ff
    if staged():
        shards = (
            self_output,
            cross_project,
            memory_project,
            cross_output,
            expand_weight,
            contract_weight,
            norm_gain,
            norm_bias,
        )
        later = batches[1] + batches[2]
        batch_23 = call(
            pack_kernel,
            list(shards),
            [whole(shard.shape) for shard in shards],
            [shaped((rows, later), LOW)],
            [whole((rows, later))],
            [pltpu.VMEM((LANES, LANES), FULL)],
        )[0]
        far_1 = jnp.stack(gather_far(self_project))
        states_x = exchange(states, 2)
        states_c = exchange(states, 1)
        (batch_23, states_c), far_1 = after((batch_23, states_c), far_1)
        near_23 = exchange(batch_23, FAR[0])
        plane_1 = gather_plane(far_1)
        near_23, states_x = after(near_23, states_x)
        own_memory, states_c = after(own_memory, states_c)
        half_2 = jnp.stack([batch_23[:, : batches[1]], near_23[:, : batches[1]]])
        half_3 = jnp.stack([batch_23[:, batches[1] :], near_23[:, batches[1] :]])
        rest_2 = exchange(half_2, FAR[1])
        memory_x = exchange(own_memory, 2)
        half_3, rest_2 = after(half_3, rest_2)
        far_2 = jnp.concatenate([half_2, rest_2])
        rest_3 = exchange(half_3, FAR[1])
    else:
        norm_shard = jnp.concatenate([norm_gain, norm_bias], axis=0).T
        norm_shard = jnp.pad(norm_shard, ((0, 0), (0, LANES - norm_shard.shape[1])))
        folded = fold_rows(contract_weight, rows)
        plane_1 = self_project
        far_2 = jnp.concatenate(
            [self_output, cross_project, memory_project, cross_output, norm_shard], axis=1
        )
        far_3 = jnp.concatenate([expand_weight, folded], axis=1)
        states_x = exchange(states, 2)
        states_c = exchange(states, 1)
        memory_c = exchange(own_memory, 1)
        memory_x = exchange(own_memory, 2)
    states_xc = exchange(states_x, 1)
    far_2, plane_1 = after(far_2, plane_1)
    weights_1 = gather_core(plane_1)
    row_states = [states, states_c, states_x, states_xc]
    own_2 = exchange(far_2, 1) if staged() else None
    if staged():
        row_states[1], own_2 = after(row_states[1], own_2)
    plane_2 = gather_plane(far_2)

    row_spec = whole((local, width))
    pair_rows = pl.BlockSpec((local, LANES), lambda pair: (0, pair))
    pair_keys = pl.BlockSpec((keys, LANES), lambda pair: (0, pair))
    pair_kept = pl.BlockSpec((2, local, keys), lambda pair: (pair, 0, 0))
    quarter_specs_1 = [whole(q.shape) for q in weights_1]
    attend_scratch = [
        pltpu.VMEM((pairs, local, LANES), LOW),
        pltpu.VMEM((local, LANES), LOW),
        pltpu.VMEM((pairs, keys, 2 * LANES), LOW),
        pltpu.VMEM((pairs, keys, LANES), LOW),
        pltpu.VMEM((2, local, keys), FULL),
    ]
    attend_outputs = [
        shaped((local, width), LOW),
        pltpu.HBM((local, width), LOW),
        pltpu.HBM((local, width), FULL),
        pltpu.HBM((keys, width), LOW),
        pltpu.HBM((keys, width), LOW),
        pltpu.HBM((2 * pairs, local, keys), LOW),
    ]
    attend_specs = [pair_rows] * 3 + [pair_keys, pair_keys, pair_kept]
    in_place = pl.BlockSpec(memory_space=pl.ANY)
    self_mix, self_query, self_exact, self_key, self_value, self_kept, self_weight = call(
        self_forward_kernel,
        [info, target_lengths, *row_states, *weights_1],
        [SCALARS, SCALARS] + [row_spec] * 4 + quarter_specs_1,
        attend_outputs + [pltpu.HBM((width, 3 * width), LOW)],
        attend_specs + [in_place],
        [pltpu.VMEM((width, 3 * width), LOW), pltpu.SemaphoreType.DMA] + attend_scratch,
        grid=(pairs,),
        micros=25, mib=38,
    )

    if staged():
        (memory_x, own_memory, rest_3), self_mix = after((memory_x, own_memory, rest_3), self_mix)
        memory_c = exchange(own_memory, 1)
        far_3 = jnp.concatenate([half_3, rest_3])
    plane_2, self_mix = after(plane_2, self_mix)
    own_3 = exchange(far_3, 1) if staged() else None
    memory_xc = exchange(memory_x, 1)
    weights_2 = gather_core(plane_2, own_2)
    row_memory = [own_memory, memory_c, memory_x, memory_xc]
    plane_3 = gather_plane(far_3)
    quarter_specs_2 = [whole(q.shape) for q in weights_2]
    wide_scale = whole((local, LANES))
    norm_spec = whole((8, width))
    square = whole((width, width))
    (
        cross_mix,
        cross_query,
        cross_exact,
        cross_key,
        cross_value,
        cross_kept,
        first_unit,
        first_scale,
        norms,
        second_unit,
        second_scale,
        cross_out_weight,
        out_weight,
        query_weight,
        pair_weight,
    ) = call(
        cross_forward_kernel,
        [info, target_lengths, source_lengths, self_mix, states, *row_memory, *weights_2],
        [SCALARS] * 3 + [row_spec] * 6 + quarter_specs_2,
        attend_outputs
        + [
            pltpu.HBM((local, width), FULL),
            pltpu.HBM((local, LANES), FULL),
            shaped((8, width), FULL),
            shaped((local, width), FULL),
            shaped((local, LANES), FULL),
            shaped((width, width), LOW),
            pltpu.HBM((width, width), LOW),
            pltpu.HBM((width, width), LOW),
            pltpu.HBM((width, 2 * width), LOW),
        ],
        attend_specs + [row_spec, wide_scale, norm_spec, row_spec, wide_scale, square] + [in_place] * 3,
        [
            pltpu.VMEM((width, width), LOW),
            pltpu.VMEM((width, width), LOW),
            pltpu.VMEM((width, 2 * width), LOW),
            pltpu.VMEM((width, LANES), LOW),
            pltpu.SemaphoreType.DMA((3,)),
            pltpu.VMEM((pairs, local, LANES), LOW),
        ]
        + attend_scratch,
        grid=(pairs,),
        micros=25, mib=46,
    )

    plane_3, second_unit = after(plane_3, second_unit)
    weights_3 = gather_core(plane_3, own_3, ff // width)
    quarter_specs_3 = [whole(q.shape) for q in weights_3]
    chunk_count = ff // width
    packed_3 = (4, 4, TILE_ROWS, 2 * ff)
    hidden_shape = (chunk_count, local, width)
    output, third_grad, hidden_grads, expand_whole, norm_sums, kept_3, sent_3 = call(
        middle_kernel,
        [info, second_unit, norms, out_grad[0], *weights_3],
        [SCALARS, row_spec, norm_spec, row_spec] + quarter_specs_3,
        [
            shaped((local, width), FULL),
            shaped((local, width), FULL),
            shaped(hidden_shape, LOW),
            shaped((width, ff), LOW),
            shaped((8, width), FULL),
            shaped(packed_3, LOW),
            shaped(packed_3, LOW),
        ],
        [row_spec, row_spec, whole(hidden_shape), whole((width, ff)), norm_spec]
        + [whole(packed_3), whole(packed_3)],
        [
            pltpu.VMEM((ff, width), LOW),
            pltpu.VMEM(hidden_shape, LOW),
            pltpu.VMEM(hidden_shape, FULL),
            pltpu.VMEM((width, ff), LOW),
            pltpu.VMEM((ff, width), LOW),
        ],
        micros=14, mib=34,
    )
    other_3 = exchange_core(sent_3)
    second_grad, cross_mix_grad, cross_out_grad, norm_sums = call(
        second_back_kernel,
        [
            third_grad,
            hidden_grads,
            expand_whole,
            second_unit,
            second_scale,
            norms,
            norm_sums,
            cross_mix,
            cross_out_weight,
        ],
        [row_spec, whole(hidden_shape), whole((width, ff))]
        + [row_spec, wide_scale, norm_spec, norm_spec, row_spec, square],
        [
            shaped((local, width), FULL),
            shaped((local, width), LOW),
            shaped((width, width), LOW),
            shaped((8, width), FULL),
        ],
        [row_spec, row_spec, square, norm_spec],
        [],
        micros=4, mib=12,
    )
    other_3, cross_mix_grad = after(other_3, cross_mix_grad)
    core_3 = reduce_core(kept_3, other_3)
    core_3, cross_mix_grad = after(core_3, cross_mix_grad)
    planes_3 = exchange_plane(core_3)

    back_specs = [pair_rows, pair_keys, pair_keys, pair_kept, pair_rows, pair_rows]
    made_shape = (pairs, 2 * LANES, keys)
    cross_made, cross_query_grad, pair_weight_grad = call(
        cross_backward_kernel,
        [
            cross_query,
            cross_key,
            cross_value,
            cross_kept,
            cross_exact,
            cross_mix_grad,
            *row_memory,
        ],
        back_specs + [row_spec] * 4,
        [
            shaped(made_shape, LOW),
            shaped((local, width), LOW),
            shaped((width, 2 * width), LOW),
        ],
        [whole(made_shape), pair_rows, whole((width, 2 * width))],
        [pltpu.VMEM((keys, 2 * LANES), LOW)],
        grid=(pairs,),
        micros=33, mib=36,
    )
    planes_3, cross_query_grad = after(planes_3, cross_query_grad)
    plane_sum_3 = reduce_plane(planes_3)
    plane_sum_3, cross_query_grad = after(plane_sum_3, cross_query_grad)
    half_sum_3 = exchange_half(plane_sum_3)

    packed_2 = (4, 4, TILE_ROWS, 5 * width + LANES)
    first_grad, self_mix_grad, kept_2, sent_2 = call(
        between_kernel,
        [
            info,
            cross_query_grad,
            second_grad,
            first_unit,
            first_scale,
            norms,
            norm_sums,
            self_mix,
            pair_weight_grad,
            cross_out_grad,
            out_weight,
            query_weight,
        ],
        [SCALARS, row_spec, row_spec, row_spec, whole((local, LANES))]
        + [whole((8, width))] * 2
        + [row_spec, whole((width, 2 * width)), whole((width, width))]
        + [square] * 2,
        [
            shaped((local, width), FULL),
            shaped((local, width), LOW),
            shaped(packed_2, LOW),
            shaped(packed_2, LOW),
        ],
        [row_spec, row_spec, whole(packed_2), whole(packed_2)],
        [
            pltpu.VMEM((width, width), LOW),
            pltpu.VMEM((width, width), LOW),
            pltpu.VMEM((width, LANES), LOW),
            pltpu.VMEM((LANES, width), FULL),
        ],
        micros=6, mib=14,
    )
    other_2 = exchange_core(sent_2)
    cross_made, sent_2 = after(cross_made, sent_2)
    rows_shapes = [
        shaped((local, width), FULL),
        shaped((local, width), LOW),
        shaped((2, local, width), LOW),
    ]
    rows_specs = [row_spec, row_spec, whole((2, local, width))]
    memory_own, memory_far_part, memory_parts = call(
        memory_kernel,
        [cross_made, pair_weight],
        [whole(made_shape), whole((width, 2 * width))],
        rows_shapes,
        rows_specs,
        [],
        micros=3, mib=20,
    )
    other_2, memory_parts = after(other_2, memory_parts)
    memory_sent = exchange(memory_parts, 1)
    core_2 = reduce_core(kept_2, other_2)
    memory_other = reduce_row_core(memory_far_part, memory_sent)
    (core_2, memory_other), self_mix_grad = after((core_2, memory_other), self_mix_grad)
    planes_2 = exchange_plane(core_2)
    memory_far = exchange(memory_other, 2)

    packed_1 = (4, 4, TILE_ROWS, 3 * width)
    made, self_query_grad, kept_1, sent_1 = call(
        self_backward_kernel,
        [
            info,
            self_query,
            self_key,
            self_value,
            self_kept,
            self_exact,
            self_mix_grad,
            *row_states,
        ],
        [SCALARS] + back_specs + [row_spec] * 4,
        [
            shaped(made_shape, LOW),
            shaped((local, width), LOW),
            shaped(packed_1, LOW),
            shaped(packed_1, LOW),
        ],
        [whole(made_shape), row_spec, whole(packed_1), whole(packed_1)],
        [
            pltpu.VMEM((keys, 2 * LANES), LOW),
            pltpu.VMEM((pairs, local, LANES), LOW),
            pltpu.VMEM((width, 3 * width), LOW),
        ],
        grid=(pairs,),
        micros=33, mib=36,
    )
    (planes_2, memory_far, half_sum_3), (sent_1, kept_1) = after(
        (planes_2, memory_far, half_sum_3), (sent_1, kept_1)
    )
    other_1 = exchange_core(sent_1)
    states_own, states_far_part, states_parts = call(
        states_kernel,
        [made, self_query_grad, first_grad, self_weight],
        [whole(made_shape), row_spec, row_spec, whole((width, 3 * width))],
        rows_shapes,
        rows_specs,
        [],
        micros=4, mib=20,
    )
    other_1, states_parts = after(other_1, states_parts)
    core_1 = reduce_core(kept_1, other_1)
    planes_1 = exchange_plane(core_1)
    states_sent = exchange(states_parts, 1)
    states_other = reduce_row_core(states_far_part, states_sent)
    (planes_2, half_sum_3, memory_far), states_other = after(
        (planes_2, half_sum_3, memory_far), states_other
    )
    plane_sum_2 = reduce_plane(planes_2)
    half_sum_2 = exchange_half(plane_sum_2)
    states_far = exchange(states_other, 2)
    total_3 = reduce_half(plane_sum_3, half_sum_3)
    total_2 = reduce_half(plane_sum_2, half_sum_2)
    planes_1, (total_2, total_3, states_other) = after(planes_1, (total_2, total_3, states_other))
    plane_sum_1 = reduce_plane(planes_1)
    fars_1 = exchange_far(plane_sum_1)
    memory_grad = reduce_row(memory_own, memory_sent, memory_far)
    states_grad = reduce_row(states_own, states_sent, states_far)
    count = norm_gain.shape[0]
    if staged():
        near = exchange(jnp.concatenate([total_2[1], total_3[1]], axis=1), FAR[0])
        settled = [
            shaped((rows, width), FULL),
            shaped((rows, width), FULL),
            shaped((rows, 2 * width), FULL),
            shaped((rows, width), FULL),
            shaped((rows, ff), FULL),
            shaped((rows * ff // width, width), FULL),
            shaped(norm_gain.shape, FULL),
            shaped(norm_gain.shape, FULL),
        ]
        out, cross, pairs_grad, cross_out, expand_grad, contract_grad, gain, bias = call(
            settle_kernel,
            [total_2[0], total_3[0], near],
            [whole((rows, batches[1])), whole((rows, batches[2])), whole((rows, later))],
            settled,
            [whole(each.shape) for each in settled],
            [pltpu.VMEM((LANES, LANES), FULL)],
            mib=8,
        )
        fars_1, out = after(fars_1, out)
        project = reduce_far(fars_1)
    else:
        grad_3 = reduce_far(total_3, ff // width)
        grad_2 = reduce_far(total_2)
        project = reduce_far(fars_1)
        expand_grad, contract_grad = grad_3[:, :ff], unfold_rows(grad_3[:, ff:], width)
        out, cross = grad_2[:, :width], grad_2[:, width : 2 * width]
        pairs_grad, cross_out = grad_2[:, 2 * width : 4 * width], grad_2[:, 4 * width : 5 * width]
        norm_grads = grad_2[:, 5 * width :].T
        gain, bias = norm_grads[:count], norm_grads[count : 2 * count]
    return (
        output[None],
        states_grad[None],
        memory_grad[None],
        project,
        out,
        cross,
        pairs_grad,
        cross_out,
        expand_grad,
        contract_grad,
        gain,
        bias,
    )


def reduce_row_core(part, sent):
    return add_all(part, [sent[1]]).astype(LOW)


def reduce_row(own, sent, far):
    return add_all(own, [sent[0], far])


def solution(mesh):
    in_specs = (
        P("wide", "narrow", None),
        P("wide", "narrow", None),
        P("wide", None),
        P("wide", None),
        P(("wide", "narrow"), None),
        P(("wide", "narrow"), None),
        P(("wide", "narrow"), None),
        P(("wide", "narrow"), None),
        P(("wide", "narrow"), None),
        P(("wide", "narrow"), None),
        P(("wide", "narrow"), None),
        P(None, ("wide", "narrow")),
        P(None, ("wide", "narrow")),
        P("wide", "narrow", None),
    )
    out_specs = (
        P("wide", "narrow", None),
        P("wide", "narrow", None),
        P("wide", "narrow", None),
        P(("wide", "narrow"), None),
        P(("wide", "narrow"), None),
        P(("wide", "narrow"), None),
        P(("wide", "narrow"), None),
        P(("wide", "narrow"), None),
        P(("wide", "narrow"), None),
        P(("wide", "narrow"), None),
        P(None, ("wide", "narrow")),
        P(None, ("wide", "narrow")),
    )
    return jax.shard_map(
        per_device, mesh=mesh, in_specs=in_specs, out_specs=out_specs, check_vma=False
    )
```
